512 devices in a mesh: group: 2 (over y_hi), dp: 64 (over y_lo, z, core), tensor: 4 (over x).
Axes of the slice: x: 4, y: 8 (y_hi: 2, y_lo: 4; y = y_hi * 4 + y_lo), z: 8, core: 2. Of those that a mesh axis runs over, the one named last changes fastest.
Arguments:
- teacher_clips: bfloat16 [128, 256, 1024], P(('group', 'dp')), may hold values from -6 to 6
- teacher_gain: float32 [1024], replicated, may hold values from 0.5 to 2
- teacher_qkv: bfloat16 [1024, 3072], P('dp', 'tensor'), may hold values from -0.25 to 0.25
- teacher_out_t: bfloat16 [1024, 1024], P('dp', 'tensor'), may hold values from -0.75 to 0.75
- event_tokens: bfloat16 [128, 256, 768], P(('group', 'dp')), may hold values from -6 to 6
- valid_counts: int32 [128], P(('group', 'dp')), may hold values from 32 to 256, as said below
- alignment: int32 [128, 2], P(('group', 'dp')), may hold values from 0 to 1
- student_qkv: bfloat16 [768, 2304], P(None, 'tensor'), may hold values from -0.3125 to 0.3125
- student_out: bfloat16 [768, 768], P('tensor'), may hold values from -0.75 to 0.75
- projector: bfloat16 [768, 1024], P(None, 'tensor'), may hold values from -0.21875 to 0.21875
Outputs:
- clip_loss: float32 [128], P(('group', 'dp'))
- grad_qkv: float32 [768, 2304], P(('group', 'dp'), 'tensor')
- grad_out: float32 [768, 768], P('tensor', ('group', 'dp'))
- grad_projector: float32 [768, 1024], P(('group', 'dp'), 'tensor')
The draws below stay inside these ranges and needn't reach their ends.
Inputs may be any that keep to these rules, and one draw needn't show every extreme that they name: `valid_counts`: some clip has all 256 event tokens valid.
All inputs are finite; a program needn't handle non-finite values.
Results may differ from the reference program's by a relative error of at most 0.018.
Values may be sent and summed in bfloat16 or wider, within the bound.
No kernel may reach another device: no remote copies, remote signals or barrier semaphores. Data moves between devices by JAX's collectives and lax.ppermute only.
A program may use at most 64 MiB of HBM per device.

```python
import math
import jax
import jax.numpy as jnp
from jax import lax

DT = 1024
HT = 16
DS = 768
HS = 12
HEAD = 64
BLOCK = 128
TT = 256
TS = 256
CLIPS = 128
N_TENSOR = 4


def draw_valid_counts(key, part):
    key = jax.random.fold_in(key, 7)
    counts = jax.random.randint(key, (CLIPS,), TS // 8, TS + 1)
    return counts.at[0].set(TS).astype(jnp.int32)


def touch_ends(array, key, low, largest):
    longest = array.shape.index(max(array.shape))
    spots = []
    for shift in (0, 1):
        where = [jax.random.randint(jax.random.fold_in(key, axis), (), 0, length) for axis, length in enumerate(array.shape)]
        where[longest] = (where[longest] + shift) % array.shape[longest]
        spots.append(tuple(where))
    return array.at[spots[0]].set(low).at[spots[1]].set(largest)


def steps_of(stream_key, shape, cuts, smallest, largest):
    level, own = 1.0, jax.random.fold_in(stream_key, 6)
    for dim, parts in cuts:
        heights = jnp.exp(jax.random.uniform(jax.random.fold_in(own, dim), (parts,), jnp.float32, smallest / len(cuts), largest / len(cuts)))
        level = level * jnp.repeat(heights, shape[dim] // parts).reshape([-1 if axis == dim else 1 for axis in range(len(shape))])
    return level


def scatter_about(stream_key, shape, width, reach, shards=(), dtype=jnp.bfloat16):
    result = jax.random.normal(stream_key, shape, jnp.float32) * width
    if len(shards) > 0:
        result = steps_of(stream_key, shape, shards, -0.22, 0.18) * result
    return jnp.clip(result, min=-reach, max=reach).astype(dtype)


def setup_inputs(seed: int = 0) -> dict:
    seeds = jax.random.split(jax.random.key(seed), 11)
    return {
        "teacher_clips": scatter_about(seeds[0], (CLIPS, TT, DT), 1.0, 6.0, ((0, 128),)),
        "teacher_gain": jnp.clip(jnp.exp(jax.random.uniform(seeds[1], (DT,), jnp.float32, math.log(0.5), math.log(2.0))), 0.5, 2.0),
        "teacher_qkv": scatter_about(seeds[2], (DT, HT * 3 * HEAD), (DT // 2) ** -0.5, 0.25, ((0, 64), (1, 4))),
        "teacher_out_t": scatter_about(seeds[3], (DT, HT * HEAD), HEAD ** -0.5, 0.75, ((0, 64), (1, 4))),
        "event_tokens": scatter_about(seeds[4], (CLIPS, TS, DS), 1.0, 6.0, ((0, 128),)),
        "valid_counts": draw_valid_counts(jax.random.fold_in(seeds[10], 71), 0),
        "alignment": touch_ends(jax.random.randint(seeds[6], (CLIPS, TS // BLOCK), 0, TT // BLOCK), jax.random.fold_in(seeds[6], 1), 0, (TT // BLOCK) - 1).astype(jnp.int32),
        "student_qkv": scatter_about(seeds[7], (DS, HS * 3 * HEAD), (DS // 2) ** -0.5, 0.3125, ((1, 4),)),
        "student_out": scatter_about(seeds[8], (HS * HEAD, DS), HEAD ** -0.5, 0.75, ((0, 4),)),
        "projector": scatter_about(seeds[9], (DS, DT), DS ** -0.5, 0.21875, ((1, 4),)),
    }


def norm_rows(rows):
    rows = rows.astype(jnp.float32)
    centre = rows - lax.optimization_barrier(jnp.mean(rows, -1, keepdims=True))
    spread = lax.optimization_barrier(jnp.mean(centre * centre, -1, keepdims=True))
    return centre * lax.rsqrt(spread + 1e-05)

def attend(normed, weight, count):
    length = normed.shape[0]
    head_size = HEAD
    heads = weight.shape[1] // (3 * head_size)
    packed = jnp.dot(normed, weight, preferred_element_type=jnp.float32).astype(jnp.bfloat16)
    packed = packed.reshape(length, heads, 3, head_size)
    query = packed[:, :, 0].astype(jnp.float32)
    keys = packed[:, :, 1].astype(jnp.float32)
    values = packed[:, :, 2].astype(jnp.float32)
    scores = jnp.einsum('qhd,khd->hqk', query, keys) * head_size ** (-0.5)
    usable = jnp.arange(length) < count
    scores = jnp.where(usable[None, None, :], scores, -1e+30)
    top = lax.optimization_barrier(jnp.max(scores, -1, keepdims=True))
    weights = jnp.exp(scores - top)
    weights = (weights / lax.optimization_barrier(jnp.sum(weights, -1, keepdims=True))).astype(jnp.bfloat16)
    mixed = jnp.einsum('hqk,khd->qhd', weights.astype(jnp.float32), values).astype(jnp.bfloat16)
    return mixed.reshape(length, heads * head_size)

def student_heads(normed, weight_qkv, weight_out, count):
    mixed = attend(normed, weight_qkv.astype(jnp.bfloat16), count)
    return jnp.dot(mixed, weight_out.astype(jnp.bfloat16), preferred_element_type=jnp.float32)

def teacher_part(normed, weight_qkv, weight_out_t):
    mixed = attend(normed, weight_qkv, normed.shape[0])
    return lax.dot_general(mixed, weight_out_t, (((1,), (1,)), ((), ())), preferred_element_type=jnp.float32)

def rounded(value):
    return lax.optimization_barrier(value.astype(jnp.bfloat16)).astype(jnp.float32)

def reference(teacher_clips, teacher_gain, teacher_qkv, teacher_out_t, event_tokens, valid_counts, alignment, student_qkv, student_out, projector):
    teacher_cols = HT * 3 * HEAD // N_TENSOR
    teacher_outc = HT * HEAD // N_TENSOR
    student_cols = HS * 3 * HEAD // N_TENSOR
    student_rows = HS * HEAD // N_TENSOR

    def one_clip(totals, inputs):
        clip, events, count, align = inputs
        teacher_normed = (norm_rows(clip) * teacher_gain).astype(jnp.bfloat16)
        branch = jnp.zeros((TT, DT), jnp.float32)
        for shard in range(N_TENSOR):
            part = teacher_part(teacher_normed, teacher_qkv[:, shard * teacher_cols:(shard + 1) * teacher_cols], teacher_out_t[:, shard * teacher_outc:(shard + 1) * teacher_outc])
            branch = branch + rounded(part)
        teacher_feat = (clip.astype(jnp.float32) + branch).astype(jnp.bfloat16)
        target = jnp.take(teacher_feat.reshape(TT // BLOCK, BLOCK, DT), align, axis=0).reshape(TS, DT)
        student_normed = norm_rows(events).astype(jnp.bfloat16)
        pieces = []
        sbranch = jnp.zeros((TS, DS), jnp.float32)
        for shard in range(N_TENSOR):
            wq = student_qkv[:, shard * student_cols:(shard + 1) * student_cols].astype(jnp.float32)
            wo = student_out[shard * student_rows:(shard + 1) * student_rows].astype(jnp.float32)
            pieces.append((wq, wo))
            sbranch = sbranch + rounded(student_heads(student_normed, wq, wo, count))
        student_feat = (events.astype(jnp.float32) + sbranch).astype(jnp.bfloat16)
        pred = jnp.dot(student_feat, projector, preferred_element_type=jnp.float32)
        live = (jnp.arange(TS) < count)[:, None]
        diff = jnp.where(live, pred - target.astype(jnp.float32), 0.0)
        scale = count.astype(jnp.float32) * DT
        loss = jnp.sum(diff * diff) / scale
        dpred = (diff * (2.0 / (scale * CLIPS))).astype(jnp.bfloat16)
        grad_proj = lax.dot_general(student_feat, dpred, (((0,), (0,)), ((), ())), preferred_element_type=jnp.float32)
        dfeat = lax.dot_general(dpred, projector, (((1,), (1,)), ((), ())), preferred_element_type=jnp.float32)
        grads_q = []
        grads_o = []
        for wq, wo in pieces:
            _, back = jax.vjp(lambda first, second: student_heads(student_normed, first, second, count), wq, wo)
            gq, go = back(dfeat)
            grads_q.append(gq.astype(jnp.float32))
            grads_o.append(go.astype(jnp.float32))
        totals = (totals[0] + jnp.concatenate(grads_q, 1), totals[1] + jnp.concatenate(grads_o, 0), totals[2] + grad_proj)
        return (totals, loss)
    start = (jnp.zeros((DS, HS * 3 * HEAD), jnp.float32), jnp.zeros((HS * HEAD, DS), jnp.float32), jnp.zeros((DS, DT), jnp.float32))
    totals, losses = lax.scan(one_clip, start, (teacher_clips, event_tokens, valid_counts, alignment))
    return (losses, totals[0], totals[1], totals[2])
```

```python
import jax
import jax.numpy as jnp
from jax import lax
from jax.experimental import pallas as pl
from jax.experimental.pallas import tpu as pltpu
from jax.sharding import Mesh, PartitionSpec as P

HEAD = 64
BLOCK = 128
F32 = jnp.float32
BF16 = jnp.bfloat16
CLIP = ("g", "yl", "z", "c")
VMEM = pl.BlockSpec(memory_space=pltpu.VMEM)
SMEM = pl.BlockSpec(memory_space=pltpu.SMEM)
PARAMS = pltpu.CompilerParams(vmem_limit_bytes=40 * 1024 * 1024)


def shape(dims, dtype):
    return jax.ShapeDtypeStruct(dims, dtype)


def nn(a, b):
    return lax.dot_general(a, b, (((1,), (0,)), ((), ())), preferred_element_type=F32)


def nt(a, b):
    return lax.dot_general(a, b, (((1,), (1,)), ((), ())), preferred_element_type=F32)


def tn(a, b):
    return lax.dot_general(a, b, (((0,), (0,)), ((), ())), preferred_element_type=F32)


def norm_rows(rows):
    rows = rows.astype(F32)
    centre = rows - jnp.mean(rows, -1, keepdims=True)
    spread = jnp.mean(centre * centre, -1, keepdims=True)
    return centre * lax.rsqrt(spread + 1e-05)


def split_head(packed, head):
    first = head * 3 * HEAD
    return [packed[:, first + i * HEAD : first + (i + 1) * HEAD].astype(BF16) for i in range(3)]


def softmax(scores):
    top = jnp.max(scores, -1, keepdims=True)
    weights = jnp.exp(scores - top)
    return weights / jnp.sum(weights, -1, keepdims=True)


def student_kernel(
    count_ref, events_ref, qkv_ref, out_ref, clip_ref, gain_ref,
    part_ref, normed_ref, packed_ref, mixed_ref, weights_ref, teacher_ref,
):
    length = events_ref.shape[0]
    heads = out_ref.shape[0] // HEAD
    normed = norm_rows(events_ref[...]).astype(BF16)
    normed_ref[...] = normed
    packed = nn(normed, qkv_ref[...])
    packed_ref[...] = packed.astype(BF16)
    usable = lax.broadcasted_iota(jnp.int32, (length, length), 1) < count_ref[0]
    mixed = []
    for head in range(heads):
        query, keys, values = split_head(packed, head)
        scores = jnp.where(usable, nt(query, keys) * HEAD ** (-0.5), -1e30)
        weights = softmax(scores)
        weights_ref[head] = weights
        mixed.append(nn(weights.astype(BF16), values))
    mixed = jnp.concatenate(mixed, axis=1).astype(BF16)
    mixed_ref[...] = mixed
    part_ref[...] = nn(mixed, out_ref[...]).astype(BF16)
    teacher_ref[...] = (norm_rows(clip_ref[...]) * gain_ref[...]).astype(BF16)


def teacher_kernel(
    place_ref, align_ref, normed_ref, own_ref, near_ref, swap_ref, far_ref, fars_ref,
    part_ref, full_ref, mixed_ref,
):
    rows = own_ref.shape[0]
    for i, piece in enumerate((own_ref, near_ref, swap_ref, far_ref, fars_ref)):
        size = piece.shape[0]
        full_ref[pl.ds(pl.multiple_of(place_ref[i], BLOCK), size), :] = piece[...]
    width = full_ref.shape[1]
    heads = width // (4 * HEAD)
    packed = nn(normed_ref[...], full_ref[:, : heads * 3 * HEAD])
    mixed = []
    for head in range(heads):
        query, keys, values = split_head(packed, head)
        weights = softmax(nt(query, keys) * HEAD ** (-0.5))
        mixed.append(nn(weights.astype(BF16), values))
    mixed_ref[...] = jnp.concatenate(mixed, axis=1)
    for i in range(align_ref.shape[0]):
        first = pl.multiple_of(align_ref[i] * BLOCK, BLOCK)
        chosen = mixed_ref[pl.ds(first, BLOCK), :].astype(BF16)
        part_ref[i * BLOCK : (i + 1) * BLOCK, :] = nt(
            chosen, full_ref[:, heads * 3 * HEAD :]
        ).astype(BF16)


def diff_kernel(clips, count_ref, start_ref, parts_ref, tokens_ref, feat_ref, proj_ref, out_ref):
    rows, width = tokens_ref.shape
    ways = proj_ref.shape[0]
    columns = proj_ref.shape[2]
    branch = parts_ref[0].astype(F32)
    for i in range(1, ways):
        branch = branch + parts_ref[i].astype(F32)
    target = (tokens_ref[...].astype(F32) + branch).astype(BF16).astype(F32)
    count = count_ref[0]
    live = lax.broadcasted_iota(jnp.int32, (rows, 1), 0) + start_ref[0] < count
    scale = jnp.full((1, 1), count, jnp.int32).astype(F32) * width
    factor = 2.0 / (scale * clips)
    feat = feat_ref[...]
    features = proj_ref.shape[1]
    dfeat = jnp.zeros((rows, features), F32)
    squares = jnp.zeros((rows, 1), F32)
    for i in range(ways):
        pred = nn(feat, proj_ref[i])
        diff = jnp.where(live, pred - target[:, i * columns : (i + 1) * columns], 0.0)
        squares = squares + jnp.sum(diff * diff, -1, keepdims=True)
        dpred = (diff * factor).astype(BF16)
        out_ref[i, :, features : features + columns] = dpred
        dfeat = dfeat + nt(dpred, proj_ref[i])
    dfeat = dfeat.astype(BF16)
    squares = squares / scale
    high = squares.astype(BF16)
    rest = squares - high.astype(F32)
    middle = rest.astype(BF16)
    low = (rest - middle.astype(F32)).astype(BF16)
    lane = lax.broadcasted_iota(jnp.int32, (rows, BLOCK), 1)
    tail = jnp.where(lane == 0, high.astype(F32), jnp.where(lane == 1, middle.astype(F32), 0.0))
    tail = jnp.where(lane == 2, low.astype(F32), tail).astype(BF16)
    for i in range(ways):
        out_ref[i, :, :features] = dfeat
        out_ref[i, :, features + columns :] = tail


def backward_kernel(
    back_ref, packed_ref, weights_ref, mixed_ref, out_ref, pick_ref, normed_ref, feat_ref,
    keep_ref, send_ref, loss_ref,
):
    features = out_ref.shape[1]
    heads = out_ref.shape[0] // HEAD
    dfeat = back_ref[:, :features]
    columns = back_ref.shape[1] - features - BLOCK
    dpred = back_ref[:, features : features + columns]
    tail = back_ref[:, features + columns :].astype(F32)
    loss_ref[...] = jnp.sum(jnp.sum(tail, 0, keepdims=True), 1, keepdims=True)
    dmixed = nt(dfeat, out_ref[...])
    packed = packed_ref[...].astype(F32)
    pieces = []
    for head in range(heads):
        query, keys, values = split_head(packed, head)
        weights = weights_ref[head]
        cot = dmixed[:, head * HEAD : (head + 1) * HEAD].astype(BF16)
        dvalues = tn(weights.astype(BF16), cot)
        dweights = nt(cot, values)
        inner = jnp.sum(dweights * weights, -1, keepdims=True)
        dscores = (weights * (dweights - inner) * HEAD ** (-0.5)).astype(BF16)
        pieces += [nn(dscores, keys), tn(dscores, query), dvalues]
    dpacked = jnp.concatenate(pieces, axis=1)
    used = dpacked.shape[1]
    length = dpacked.shape[0]
    right = jnp.concatenate([dpacked, jnp.zeros((length, features - used), F32)], 1).astype(BF16)
    tailed = features - columns
    mixed = jnp.concatenate(
        [jnp.zeros((length, used - tailed), F32), mixed_ref[...].astype(F32)], 1
    ).astype(BF16)
    for half, into in enumerate((keep_ref, send_ref)):
        dfeat_rows = nt(pick_ref[half], dfeat).astype(BF16)
        normed_rows = normed_ref[half]
        for b in range(features // columns):
            block = slice(b * columns, (b + 1) * columns)
            total = nn(normed_rows, right[:, block]) + nn(feat_ref[half, b], dpred)
            if b == features // columns - 1:
                total = total + nn(dfeat_rows, mixed)
            into[:, block] = total.astype(BF16)


def gather_rows(shard, own_c, own_yl):
    spread = lax.axis_size("z") * lax.axis_size("c")
    rows, width = shard.shape
    run = lax.all_to_all(
        jnp.broadcast_to(shard[None], (spread, rows, width)), ("z", "c"), 0, 0
    ).reshape(spread * rows, width)
    ring = lax.axis_size("g") * lax.axis_size("yl")
    near, far = [], []
    for y in range(ring):
        for c, sign in ((0, -1), (1, 1)):
            near.append((y * 2 + c, (y + sign) % ring * 2 + c))
            far.append((y * 2 + c, (y + 2 * sign) % ring * 2 + c))
    half = spread * rows // 2
    first = lax.ppermute(run, ("g", "yl", "c"), near)
    second = lax.ppermute(lax.dynamic_slice_in_dim(run, own_c * half, half, 0), ("g", "yl", "c"), far)
    swap = [(0, 1), (1, 0)]
    first_other = lax.ppermute(first, "c", swap)
    second_other = lax.ppermute(second, "c", swap)
    ways = lax.axis_size("yl")
    step = 1 - 2 * own_c
    size = spread * rows
    opposite = (own_yl + 2) % ways * size
    place = jnp.stack([
        own_yl * size,
        (own_yl + step + ways) % ways * size,
        (own_yl - step + ways) % ways * size,
        opposite + own_c * half,
        opposite + (1 - own_c) * half,
    ]).astype(jnp.int32)
    return place, (run, first, first_other, second, second_other)


def pick_rows(rows, own_c, shares, columns):
    each = rows // shares
    extra = each * columns // rows
    block = each + extra
    place = jnp.arange(shares // 2 * block)
    chip, row = place // block, place % block
    source = jnp.arange(rows)
    picks, extras = [], []
    for core in (own_c, 1 - own_c):
        base = (chip * 2 + core) * each
        picks.append((source[None] == (base + row)[:, None]) & (row < each)[:, None])
        extras.append(jnp.stack([
            (source[None] == (base + (row - each) * (rows // columns) + b)[:, None]) & (row >= each)[:, None]
            for b in range(rows // columns)
        ]))
    return jnp.stack(picks).astype(BF16), jnp.stack(extras).astype(BF16)


def on_device(
    teacher_clips, teacher_gain, teacher_qkv, teacher_out_t, event_tokens, valid_counts, alignment,
    student_qkv, student_out, projector,
):
    clip, events, align = teacher_clips[0], event_tokens[0], alignment[0]
    length, width = clip.shape
    features = events.shape[1]
    columns = projector.shape[1]
    ways = lax.axis_size("x")
    rows = length // ways
    own_c, own_yl, own_x = lax.axis_index("c"), lax.axis_index("yl"), lax.axis_index("x")
    shares = 1
    for axis in CLIP:
        shares = shares * lax.axis_size(axis)

    place, pieces = gather_rows(jnp.concatenate([teacher_qkv, teacher_out_t], 1), own_c, own_yl)

    heads = student_out.shape[0] // HEAD
    part, normed, packed, mixed, weights, teacher_normed = pl.pallas_call(
        student_kernel,
        out_shape=(
            shape((length, features), BF16),
            shape((length, features), BF16),
            shape((length, 3 * HEAD * heads), BF16),
            shape((length, HEAD * heads), BF16),
            shape((heads, length, length), F32),
            shape((length, width), BF16),
        ),
        in_specs=[SMEM] + [VMEM] * 5,
        out_specs=(VMEM,) * 6,
        compiler_params=PARAMS,
        name="student_forward",
    )(valid_counts, events, student_qkv, student_out, clip, teacher_gain.reshape(1, width))

    whole_proj = lax.all_gather(projector, "x", axis=0, tiled=False)
    parts = lax.all_to_all(part.reshape(ways, rows, features), "x", 0, 0)
    own_events = lax.dynamic_slice_in_dim(events, own_x * rows, rows, 0)
    feat_rows = (own_events.astype(F32) + jnp.sum(parts.astype(F32), 0)).astype(BF16)
    feat = lax.all_gather(feat_rows, "x", axis=0, tiled=True)

    pick, extra = pick_rows(features, own_c, shares, columns)
    normed_rows = jnp.einsum("hpf,tf->hpt", pick, normed, preferred_element_type=F32).astype(BF16)
    feat_extra = jnp.einsum("hbpf,tf->hbpt", extra, feat, preferred_element_type=F32).astype(BF16)

    teacher_part = pl.pallas_call(
        teacher_kernel,
        out_shape=shape((length, width), BF16),
        in_specs=[SMEM] * 2 + [VMEM] * 6,
        out_specs=VMEM,
        scratch_shapes=[
            pltpu.VMEM((width, teacher_qkv.shape[1] + teacher_out_t.shape[1]), BF16),
            pltpu.VMEM((length, teacher_out_t.shape[1]), F32),
        ],
        compiler_params=PARAMS,
        name="teacher",
    )(place, align, teacher_normed, *pieces)

    teacher_parts = lax.all_to_all(teacher_part.reshape(ways, rows, width), "x", 0, 0)
    per_block = BLOCK // rows
    source = align[own_x // per_block] * BLOCK + own_x % per_block * rows
    own_tokens = lax.dynamic_slice_in_dim(clip, source, rows, 0)
    message = pl.pallas_call(
        lambda *refs: diff_kernel(shares, *refs),
        out_shape=shape((ways, rows, features + columns + BLOCK), BF16),
        in_specs=[SMEM] * 2 + [VMEM] * 4,
        out_specs=VMEM,
        compiler_params=PARAMS,
        name="difference",
    )(
        valid_counts, (own_x * rows).astype(jnp.int32).reshape(1), teacher_parts, own_tokens,
        feat_rows, whole_proj,
    )
    back = lax.all_to_all(message, "x", 0, 0).reshape(length, features + columns + BLOCK)

    half = pick.shape[1]
    keep, send, loss = pl.pallas_call(
        backward_kernel,
        out_shape=(shape((half, features), BF16), shape((half, features), BF16), shape((1, 1), F32)),
        in_specs=[VMEM] * 8,
        out_specs=(VMEM,) * 3,
        compiler_params=PARAMS,
        name="student_backward",
    )(back, packed, weights, mixed, student_out, pick, normed_rows, feat_extra)

    chips = shares // 2
    both = (keep.astype(F32) + lax.ppermute(send, "c", [(0, 1), (1, 0)]).astype(F32)).astype(BF16)
    spread = lax.all_to_all(both.reshape(chips, half // chips, features), ("g", "yl", "z"), 0, 0)
    total = jnp.sum(spread.astype(F32), 0)
    each = features // shares
    used = 3 * HEAD * heads
    grad_q = total[:each, :used]
    grad_o = total[:each, used:].T
    grad_p = total[each:].reshape(each, columns)
    return loss.reshape(1), grad_q, grad_o, grad_p


def solution(mesh):
    sizes = mesh.devices.shape
    fine = Mesh(mesh.devices.reshape(sizes[0], 4, sizes[1] // 8, 2, sizes[2]), (*CLIP, "x"))
    dp = CLIP[1:]
    in_specs = (
        P(CLIP, None, None), P(), P(dp, "x"), P(dp, "x"), P(CLIP, None, None), P(CLIP), P(CLIP, None),
        P(None, "x"), P("x", None), P(None, "x"),
    )
    out_specs = (P(CLIP), P(CLIP, "x"), P("x", CLIP), P(CLIP, "x"))
    return jax.shard_map(
        on_device, mesh=fine, in_specs=in_specs, out_specs=out_specs, check_vma=False
    )
```

```python
import jax
import jax.numpy as jnp
from jax import lax
from jax.experimental import pallas as pl
from jax.experimental.pallas import tpu as pltpu
from jax.sharding import Mesh, PartitionSpec as P

HEAD = 64
BLOCK = 128
F32 = jnp.float32
BF16 = jnp.bfloat16
CLIP = ("g", "yl", "z", "c")
VMEM = pl.BlockSpec(memory_space=pltpu.VMEM)
SMEM = pl.BlockSpec(memory_space=pltpu.SMEM)
PARAMS = pltpu.CompilerParams(vmem_limit_bytes=20 * 1024 * 1024)


def cost(microseconds):
    return pl.CostEstimate(flops=microseconds * 10**9, bytes_accessed=10**6, transcendentals=0)


def shape(dims, dtype):
    return jax.ShapeDtypeStruct(dims, dtype)


def nn(a, b):
    return lax.dot_general(a, b, (((1,), (0,)), ((), ())), preferred_element_type=F32)


def nt(a, b):
    return lax.dot_general(a, b, (((1,), (1,)), ((), ())), preferred_element_type=F32)


def tn(a, b):
    return lax.dot_general(a, b, (((0,), (0,)), ((), ())), preferred_element_type=F32)


def norm_rows(rows):
    rows = rows.astype(F32)
    centre = rows - jnp.mean(rows, -1, keepdims=True)
    spread = jnp.mean(centre * centre, -1, keepdims=True)
    return centre * lax.rsqrt(spread + 1e-05)


def split_head(packed, head):
    first = head * 3 * HEAD
    return [packed[:, first + i * HEAD : first + (i + 1) * HEAD].astype(BF16) for i in range(3)]


def softmax(scores):
    top = jnp.max(scores, -1, keepdims=True)
    weights = jnp.exp(scores - top)
    return weights / jnp.sum(weights, -1, keepdims=True)


def pick_rows(rows, shares, columns, core, extra):
    each = rows // shares
    block = each + each * columns // rows
    place = lax.broadcasted_iota(jnp.int32, (shares // 2 * block, 1), 0)
    chip, row = place // block, place % block
    base = (chip * 2 + core) * each
    if extra is None:
        wanted = jnp.where(row < each, base + row, -1)
    else:
        wanted = jnp.where(row >= each, base + (row - each) * (rows // columns) + extra, -1)
    source = lax.broadcasted_iota(jnp.int32, (shares // 2 * block, rows), 1)
    return jnp.where(source == wanted, 1.0, 0.0).astype(BF16)


def student_kernel(
    shares, count_ref, core_ref, events_ref, qkv_ref, out_ref, clip_ref, gain_ref,
    part_ref, normed_ref, packed_ref, mixed_ref, weights_ref, teacher_ref, pick_ref,
):
    length, features = events_ref.shape
    heads = out_ref.shape[0] // HEAD
    normed = norm_rows(events_ref[...]).astype(BF16)
    for half in range(2):
        core = core_ref[0] if half == 0 else 1 - core_ref[0]
        pick_ref[half] = pick_rows(features, shares, clip_ref.shape[1] // 4, core, None)
        normed_ref[half] = nt(pick_ref[half], normed).astype(BF16)
    packed = nt(normed, qkv_ref[...])
    packed_ref[...] = packed.astype(BF16)
    usable = lax.broadcasted_iota(jnp.int32, (length, length), 1) < count_ref[0]
    mixed = []
    for head in range(heads):
        query, keys, values = split_head(packed, head)
        scores = jnp.where(usable, nt(query, keys) * HEAD ** (-0.5), -1e30)
        weights = softmax(scores)
        weights_ref[head] = weights
        mixed.append(nn(weights.astype(BF16), values))
    mixed = jnp.concatenate(mixed, axis=1).astype(BF16)
    mixed_ref[...] = mixed
    part_ref[...] = nn(mixed, out_ref[...]).astype(BF16)
    teacher_ref[...] = (norm_rows(clip_ref[...]) * gain_ref[...]).astype(BF16)


def teacher_kernel(
    place_ref, align_ref, normed_ref, own_ref, near_ref, swap_ref, far_ref, fars_ref,
    part_ref, full_ref, mixed_ref,
):
    rows = own_ref.shape[0]
    for i, piece in enumerate((own_ref, near_ref, swap_ref, far_ref, fars_ref)):
        size = piece.shape[0]
        full_ref[pl.ds(pl.multiple_of(place_ref[i], BLOCK), size), :] = piece[...]
    width = full_ref.shape[1]
    heads = width // (4 * HEAD)
    packed = nn(normed_ref[...], full_ref[:, : heads * 3 * HEAD])
    mixed = []
    for head in range(heads):
        query, keys, values = split_head(packed, head)
        weights = softmax(nt(query, keys) * HEAD ** (-0.5))
        mixed.append(nn(weights.astype(BF16), values))
    mixed_ref[...] = jnp.concatenate(mixed, axis=1)
    for i in range(align_ref.shape[0]):
        first = pl.multiple_of(align_ref[i] * BLOCK, BLOCK)
        chosen = mixed_ref[pl.ds(first, BLOCK), :].astype(BF16)
        part_ref[i * BLOCK : (i + 1) * BLOCK, :] = nt(
            chosen, full_ref[:, heads * 3 * HEAD :]
        ).astype(BF16)


def feature_kernel(shares, ways, place_ref, *refs):
    feat_refs = refs[:ways]
    proj_ref, after_ref, extra_ref, pred_ref, feat_ref = refs[ways:]
    features, columns = proj_ref.shape[1:]
    rows = feat_refs[0].shape[0]
    for k in range(ways):
        source = place_ref[1 + k]
        feat_ref[pl.ds(pl.multiple_of(source * rows, rows), rows), :] = feat_refs[k][...]
        pred_ref[:, k * columns : (k + 1) * columns] = nn(feat_refs[0][...], proj_ref[k])
    feat = feat_ref[...]
    for half in range(2):
        core = place_ref[0] if half == 0 else 1 - place_ref[0]
        for b in range(features // columns):
            pick = pick_rows(features, shares, columns, core, b)
            extra_ref[half, b] = nt(pick, feat).astype(BF16)


def diff_kernel(
    clips, count_ref, place_ref, parts_ref, tokens_ref, pred_ref, proj_ref, out_ref
):
    rows, width = tokens_ref.shape
    ways, features, columns = proj_ref.shape
    branch = parts_ref[0].astype(F32)
    for i in range(1, ways):
        branch = branch + parts_ref[i].astype(F32)
    target = (tokens_ref[...].astype(F32) + branch).astype(BF16).astype(F32)
    count = count_ref[0]
    live = lax.broadcasted_iota(jnp.int32, (rows, 1), 0) + place_ref[1] * rows < count
    scale = jnp.full((1, 1), count, jnp.int32).astype(F32) * width
    factor = 2.0 / (scale * clips)
    diff = jnp.where(live, pred_ref[...] - target, 0.0)
    squares = jnp.sum(diff * diff, -1, keepdims=True) / scale
    dpred = (diff * factor).astype(BF16)
    dfeat = jnp.zeros((rows, features), F32)
    for k in range(ways):
        dfeat = dfeat + nt(dpred[:, k * columns : (k + 1) * columns], proj_ref[k])
    dfeat = dfeat.astype(BF16)
    high = squares.astype(BF16)
    rest = squares - high.astype(F32)
    middle = rest.astype(BF16)
    low = (rest - middle.astype(F32)).astype(BF16)
    lane = lax.broadcasted_iota(jnp.int32, (rows, BLOCK), 1)
    tail = jnp.where(lane == 0, high.astype(F32), jnp.where(lane == 1, middle.astype(F32), 0.0))
    tail = jnp.where(lane == 2, low.astype(F32), tail).astype(BF16)
    for i in range(ways):
        out_ref[i, :, :features] = dfeat
        out_ref[i, :, features : features + columns] = dpred[:, i * columns : (i + 1) * columns]
        out_ref[i, :, features + columns :] = tail


def backward_kernel(
    back_ref, packed_ref, weights_ref, mixed_ref, out_ref, pick_ref, normed_ref, feat_ref,
    keep_ref, send_ref, loss_ref,
):
    features = out_ref.shape[1]
    heads = out_ref.shape[0] // HEAD
    dfeat = back_ref[:, :features]
    columns = back_ref.shape[1] - features - BLOCK
    dpred = back_ref[:, features : features + columns]
    tail = back_ref[:, features + columns :].astype(F32)
    loss_ref[...] = jnp.sum(jnp.sum(tail, 0, keepdims=True), 1, keepdims=True)
    dmixed = nt(dfeat, out_ref[...])
    packed = packed_ref[...].astype(F32)
    pieces = []
    for head in range(heads):
        query, keys, values = split_head(packed, head)
        weights = weights_ref[head]
        cot = dmixed[:, head * HEAD : (head + 1) * HEAD].astype(BF16)
        dvalues = tn(weights.astype(BF16), cot)
        dweights = nt(cot, values)
        inner = jnp.sum(dweights * weights, -1, keepdims=True)
        dscores = (weights * (dweights - inner) * HEAD ** (-0.5)).astype(BF16)
        pieces += [nn(dscores, keys), tn(dscores, query), dvalues]
    dpacked = jnp.concatenate(pieces, axis=1)
    used = dpacked.shape[1]
    length = dpacked.shape[0]
    right = jnp.concatenate([dpacked, jnp.zeros((length, features - used), F32)], 1).astype(BF16)
    tailed = features - columns
    mixed = jnp.concatenate(
        [jnp.zeros((length, used - tailed), F32), mixed_ref[...].astype(F32)], 1
    ).astype(BF16)
    for half, into in enumerate((keep_ref, send_ref)):
        dfeat_rows = nt(pick_ref[half], dfeat).astype(BF16)
        normed_rows = normed_ref[half]
        for b in range(features // columns):
            block = slice(b * columns, (b + 1) * columns)
            total = nn(normed_rows, right[:, block]) + nn(feat_ref[half, b], dpred)
            if b == features // columns - 1:
                total = total + nn(dfeat_rows, mixed)
            into[:, block] = total.astype(BF16)


def gather_run(shard):
    spread = lax.axis_size("z") * lax.axis_size("c")
    return lax.all_to_all(
        jnp.broadcast_to(shard[None], (spread, *shard.shape)), ("z", "c"), 0, 0
    ).reshape(spread * shard.shape[0], shard.shape[1])


def gather_runs(run, own_c, own_yl):
    size = run.shape[0]
    half = size // 2
    ring = lax.axis_size("g") * lax.axis_size("yl")
    near, far = [], []
    for y in range(ring):
        for c, sign in ((0, -1), (1, 1)):
            near.append((y * 2 + c, (y + sign) % ring * 2 + c))
            far.append((y * 2 + c, (y + 2 * sign) % ring * 2 + c))
    first = lax.ppermute(run, ("g", "yl", "c"), near)
    second = lax.ppermute(lax.dynamic_slice_in_dim(run, own_c * half, half, 0), ("g", "yl", "c"), far)
    swap = [(0, 1), (1, 0)]
    first_other = lax.ppermute(first, "c", swap)
    second_other = lax.ppermute(second, "c", swap)
    ways = lax.axis_size("yl")
    step = 1 - 2 * own_c
    opposite = (own_yl + 2) % ways * size
    place = jnp.stack([
        own_yl * size,
        (own_yl + step + ways) % ways * size,
        (own_yl - step + ways) % ways * size,
        opposite + own_c * half,
        opposite + (1 - own_c) * half,
    ]).astype(jnp.int32)
    return place, (run, first, first_other, second, second_other)


def from_peers(rows, axis):
    ways = lax.axis_size(axis)
    return [
        lax.ppermute(rows(k), axis, [(i, (i + k) % ways) for i in range(ways)])
        for k in range(1, ways)
    ]


def result_kernel(parts_ref, q_ref, o_ref, p_ref):
    each, used = q_ref.shape
    columns = p_ref.shape[1]
    total = jnp.sum(parts_ref[...].astype(F32), 0)
    q_ref[...] = total[:each, :used]
    o_ref[...] = total[:each, used:]
    for i in range(total.shape[0] - each):
        for b in range(total.shape[1] // columns):
            row = i * (total.shape[1] // columns) + b
            p_ref[row : row + 1] = total[each + i : each + i + 1, b * columns : (b + 1) * columns]


def on_device(
    teacher_clips, teacher_gain, teacher_qkv, teacher_out_t, event_tokens, valid_counts, alignment,
    student_qkv, student_out, projector,
):
    clip, events, align = teacher_clips[0], event_tokens[0], alignment[0]
    length, width = clip.shape
    features = events.shape[1]
    columns = projector.shape[1]
    ways = lax.axis_size("x")
    rows = length // ways
    own_c, own_yl, own_x = lax.axis_index("c"), lax.axis_index("yl"), lax.axis_index("x")
    shares = 1
    for axis in CLIP:
        shares = shares * lax.axis_size(axis)

    run = gather_run(jnp.concatenate([teacher_qkv, teacher_out_t], 1))

    heads = student_out.shape[0] // HEAD
    each = features // shares
    half = shares // 2 * (each + each * columns // features)
    core = own_c.astype(jnp.int32).reshape(1)
    part, normed_rows, packed, mixed, weights, teacher_normed, pick = pl.pallas_call(
        lambda *refs: student_kernel(shares, *refs),
        out_shape=(
            shape((length, features), BF16),
            shape((2, half, length), BF16),
            shape((length, 3 * HEAD * heads), BF16),
            shape((length, HEAD * heads), BF16),
            shape((heads, length, length), F32),
            shape((length, width), BF16),
            shape((2, half, features), BF16),
        ),
        in_specs=[SMEM] * 2 + [VMEM] * 5,
        out_specs=(VMEM,) * 7,
        compiler_params=PARAMS,
        cost_estimate=cost(4),
        name="student_forward",
    )(valid_counts, core, events, student_qkv.T, student_out, clip, teacher_gain.reshape(1, width))

    whole_proj = lax.all_gather(projector, "x", axis=0, tiled=False)
    own_rows = lambda array, place: lax.dynamic_slice_in_dim(array, place * rows, rows, 0)
    branch = own_rows(part, own_x).astype(F32)
    for received in from_peers(lambda k: own_rows(part, (own_x + k) % ways), "x"):
        branch = branch + received.astype(F32)
    feat_rows = (own_rows(events, own_x).astype(F32) + branch).astype(BF16)
    run, feat_rows = lax.optimization_barrier((run, feat_rows))
    place, pieces = gather_runs(run, own_c, own_yl)
    feats = [feat_rows] + from_peers(lambda k: feat_rows, "x")

    teacher_part = pl.pallas_call(
        teacher_kernel,
        out_shape=shape((length, width), BF16),
        in_specs=[SMEM] * 2 + [VMEM] * 6,
        out_specs=VMEM,
        scratch_shapes=[
            pltpu.VMEM((width, teacher_qkv.shape[1] + teacher_out_t.shape[1]), BF16),
            pltpu.VMEM((length, teacher_out_t.shape[1]), F32),
        ],
        compiler_params=PARAMS,
        cost_estimate=cost(5),
        name="teacher",
    )(place, align, teacher_normed, *pieces)

    teacher_parts = lax.all_to_all(teacher_part.reshape(ways, rows, width), "x", 0, 0)
    per_block = BLOCK // rows
    source = align[own_x // per_block] * BLOCK + own_x % per_block * rows
    own_tokens = lax.dynamic_slice_in_dim(clip, source, rows, 0)
    places = jnp.stack([own_c] + [(own_x - k + ways) % ways for k in range(ways)]).astype(jnp.int32)
    feat_extra, pred = pl.pallas_call(
        lambda *refs: feature_kernel(shares, ways, *refs),
        out_shape=(
            shape((2, features // columns, half, length), BF16), shape((rows, width), F32),
        ),
        in_specs=[SMEM] + [VMEM] * (ways + 1) + [pl.BlockSpec(memory_space=pl.ANY)],
        out_specs=(VMEM,) * 2,
        scratch_shapes=[pltpu.VMEM((length, features), BF16)],
        compiler_params=PARAMS,
        cost_estimate=cost(4),
        name="student_features",
    )(places, *feats, whole_proj, teacher_part)
    message = pl.pallas_call(
        lambda *refs: diff_kernel(shares, *refs),
        out_shape=shape((ways, rows, features + columns + BLOCK), BF16),
        in_specs=[SMEM] * 2 + [VMEM] * 4,
        out_specs=VMEM,
        compiler_params=PARAMS,
        cost_estimate=cost(2),
        name="difference",
    )(valid_counts, places, teacher_parts, own_tokens, pred, whole_proj)
    back = lax.all_to_all(message, "x", 0, 0).reshape(length, features + columns + BLOCK)

    keep, send, loss = pl.pallas_call(
        backward_kernel,
        out_shape=(shape((half, features), BF16), shape((half, features), BF16), shape((1, 1), F32)),
        in_specs=[VMEM] * 8,
        out_specs=(VMEM,) * 3,
        compiler_params=PARAMS,
        cost_estimate=cost(4),
        name="student_backward",
    )(back, packed, weights, mixed, student_out, pick, normed_rows, feat_extra)

    chips = shares // 2
    both = (keep.astype(F32) + lax.ppermute(send, "c", [(0, 1), (1, 0)]).astype(F32)).astype(BF16)
    spread = lax.all_to_all(both.reshape(chips, half // chips, features), ("g", "yl", "z"), 0, 0)
    used = 3 * HEAD * heads
    grad_q, grad_o, grad_p = pl.pallas_call(
        result_kernel,
        out_shape=(
            shape((each, used), F32), shape((each, HEAD * heads), F32), shape((each, columns), F32),
        ),
        in_specs=[VMEM],
        out_specs=(VMEM,) * 3,
        compiler_params=PARAMS,
        cost_estimate=cost(1),
        name="gradient_rows",
    )(spread)
    return loss.reshape(1), grad_q, grad_o.T, grad_p


def solution(mesh):
    sizes = mesh.devices.shape
    fine = Mesh(mesh.devices.reshape(sizes[0], 4, sizes[1] // 8, 2, sizes[2]), (*CLIP, "x"))
    dp = CLIP[1:]
    in_specs = (
        P(CLIP, None, None), P(), P(dp, "x"), P(dp, "x"), P(CLIP, None, None), P(CLIP), P(CLIP, None),
        P(None, "x"), P("x", None), P(None, "x"),
    )
    out_specs = (P(CLIP), P(CLIP, "x"), P("x", CLIP), P(CLIP, "x"))
    return jax.shard_map(
        on_device, mesh=fine, in_specs=in_specs, out_specs=out_specs, check_vma=False
    )
```

```python
import jax
import jax.numpy as jnp
from jax import lax
from jax.experimental import pallas as pl
from jax.experimental.pallas import tpu as pltpu
from jax.sharding import Mesh, PartitionSpec as P

HEAD = 64
BLOCK = 128
F32 = jnp.float32
BF16 = jnp.bfloat16
CLIP = ("g", "yh", "y0", "zh", "z0", "c")
Y, Z = CLIP[:3], CLIP[3:5]
FAR = ("g", "yh", "zh")
ANY = pl.BlockSpec(memory_space=pl.ANY)
VMEM = pl.BlockSpec(memory_space=pltpu.VMEM)
SMEM = pl.BlockSpec(memory_space=pltpu.SMEM)
PARAMS = pltpu.CompilerParams(vmem_limit_bytes=20 * 1024 * 1024)


def cost(microseconds):
    return pl.CostEstimate(flops=microseconds * 10**9, bytes_accessed=10**6, transcendentals=0)


def shape(dims, dtype):
    return jax.ShapeDtypeStruct(dims, dtype)


def nn(a, b):
    return lax.dot_general(a, b, (((1,), (0,)), ((), ())), preferred_element_type=F32)


def nt(a, b):
    return lax.dot_general(a, b, (((1,), (1,)), ((), ())), preferred_element_type=F32)


def tn(a, b):
    return lax.dot_general(a, b, (((0,), (0,)), ((), ())), preferred_element_type=F32)


def norm_rows(rows):
    rows = rows.astype(F32)
    centre = rows - jnp.mean(rows, -1, keepdims=True)
    spread = jnp.mean(centre * centre, -1, keepdims=True)
    return centre * lax.rsqrt(spread + 1e-05)


def split_head(packed, head):
    first = head * 3 * HEAD
    return [packed[:, first + i * HEAD : first + (i + 1) * HEAD].astype(BF16) for i in range(3)]


def softmax(scores):
    top = jnp.max(scores, -1, keepdims=True)
    weights = jnp.exp(scores - top)
    return weights / jnp.sum(weights, -1, keepdims=True)


def pick_rows(rows, shares, run, columns, core, extra):
    each = rows // shares
    block = each + each * columns // rows
    place = lax.broadcasted_iota(jnp.int32, (shares // 2 * block, 1), 0)
    order, row = place // block, place % block
    others = shares // 8
    first, second, rest = order // (2 * others), order // others % 2, order % others
    low_y, low_z = first + core * (second - first), second + core * (first - second)
    chip = (rest // (run // 2) * 2 + low_y) * run + rest % (run // 2) * 2 + low_z
    base = (chip * 2 + core) * each
    if extra is None:
        wanted = jnp.where(row < each, base + row, -1)
    else:
        wanted = jnp.where(row >= each, base + (row - each) * (rows // columns) + extra, -1)
    source = lax.broadcasted_iota(jnp.int32, (shares // 2 * block, rows), 1)
    return jnp.where(source == wanted, 1.0, 0.0).astype(BF16)


def student_kernel(
    shares, run, columns, count_ref, core_ref, events_ref, qkv_ref, out_ref,
    part_ref, normed_ref, packed_ref, mixed_ref, weights_ref, pick_ref,
):
    length, features = events_ref.shape
    heads = out_ref.shape[0] // HEAD
    normed = norm_rows(events_ref[...]).astype(BF16)
    for half in range(2):
        core = core_ref[0] if half == 0 else 1 - core_ref[0]
        pick_ref[half] = pick_rows(features, shares, run, columns, core, None)
        normed_ref[half] = nt(pick_ref[half], normed).astype(BF16)
    packed = nt(normed, qkv_ref[...])
    packed_ref[...] = packed.astype(BF16)
    usable = lax.broadcasted_iota(jnp.int32, (length, length), 1) < count_ref[0]
    mixed = []
    for head in range(heads):
        query, keys, values = split_head(packed, head)
        scores = jnp.where(usable, nt(query, keys) * HEAD ** (-0.5), -1e30)
        weights = softmax(scores)
        weights_ref[head] = weights
        mixed.append(nn(weights.astype(BF16), values))
    mixed = jnp.concatenate(mixed, axis=1).astype(BF16)
    mixed_ref[...] = mixed
    part_ref[...] = nn(mixed, out_ref[...]).astype(BF16)


def teacher_norm_kernel(clip_ref, gain_ref, after_ref, normed_ref):
    normed_ref[...] = (norm_rows(clip_ref[...]) * gain_ref[...]).astype(BF16)


def teacher_kernel(
    place_ref, align_ref, normed_ref, own_ref, near_ref, swap_ref, far_ref, fars_ref,
    part_ref, full_ref, mixed_ref,
):
    rows = own_ref.shape[0]
    for i, piece in enumerate((own_ref, near_ref, swap_ref, far_ref, fars_ref)):
        size = piece.shape[0]
        full_ref[pl.ds(pl.multiple_of(place_ref[i], BLOCK), size), :] = piece[...]
    width = full_ref.shape[1]
    heads = width // (4 * HEAD)
    packed = nn(normed_ref[...], full_ref[:, : heads * 3 * HEAD])
    mixed = []
    for head in range(heads):
        query, keys, values = split_head(packed, head)
        weights = softmax(nt(query, keys) * HEAD ** (-0.5))
        mixed.append(nn(weights.astype(BF16), values))
    mixed_ref[...] = jnp.concatenate(mixed, axis=1)
    for i in range(align_ref.shape[0]):
        first = pl.multiple_of(align_ref[i] * BLOCK, BLOCK)
        chosen = mixed_ref[pl.ds(first, BLOCK), :].astype(BF16)
        part_ref[i * BLOCK : (i + 1) * BLOCK, :] = nt(
            chosen, full_ref[:, heads * 3 * HEAD :]
        ).astype(BF16)


def feature_kernel(
    shares, run, place_ref, feat_ref, rows_ref, proj_ref, after_ref, extra_ref, pred_ref
):
    ways, features, columns = proj_ref.shape
    for k in range(ways):
        pred_ref[:, k * columns : (k + 1) * columns] = nn(rows_ref[...], proj_ref[k])
    feat = feat_ref[...]
    for half in range(2):
        core = place_ref[0] if half == 0 else 1 - place_ref[0]
        for b in range(features // columns):
            pick = pick_rows(features, shares, run, columns, core, b)
            extra_ref[half, b] = nt(pick, feat).astype(BF16)


def diff_kernel(
    clips, count_ref, place_ref, parts_ref, tokens_ref, pred_ref, proj_ref, out_ref
):
    rows, width = tokens_ref.shape
    ways, features, columns = proj_ref.shape
    branch = parts_ref[0].astype(F32)
    for i in range(1, ways):
        branch = branch + parts_ref[i].astype(F32)
    target = (tokens_ref[...].astype(F32) + branch).astype(BF16).astype(F32)
    count = count_ref[0]
    live = lax.broadcasted_iota(jnp.int32, (rows, 1), 0) + place_ref[1] * rows < count
    scale = jnp.full((1, 1), count, jnp.int32).astype(F32) * width
    factor = 2.0 / (scale * clips)
    diff = jnp.where(live, pred_ref[...] - target, 0.0)
    squares = jnp.sum(diff * diff, -1, keepdims=True) / scale
    dpred = (diff * factor).astype(BF16)
    dfeat = jnp.zeros((rows, features), F32)
    for k in range(ways):
        dfeat = dfeat + nt(dpred[:, k * columns : (k + 1) * columns], proj_ref[k])
    dfeat = dfeat.astype(BF16)
    high = squares.astype(BF16)
    rest = squares - high.astype(F32)
    middle = rest.astype(BF16)
    low = (rest - middle.astype(F32)).astype(BF16)
    lane = lax.broadcasted_iota(jnp.int32, (rows, BLOCK), 1)
    tail = jnp.where(lane == 0, high.astype(F32), jnp.where(lane == 1, middle.astype(F32), 0.0))
    tail = jnp.where(lane == 2, low.astype(F32), tail).astype(BF16)
    for i in range(ways):
        out_ref[i, :, :features] = dfeat
        out_ref[i, :, features : features + columns] = dpred[:, i * columns : (i + 1) * columns]
        out_ref[i, :, features + columns :] = tail


def backward_kernel(
    back_ref, packed_ref, weights_ref, mixed_ref, out_ref, pick_ref, normed_ref, feat_ref,
    keep_ref, send_ref, loss_ref,
):
    features = out_ref.shape[1]
    heads = out_ref.shape[0] // HEAD
    dfeat = back_ref[:, :features]
    columns = back_ref.shape[1] - features - BLOCK
    dpred = back_ref[:, features : features + columns]
    tail = back_ref[:, features + columns :].astype(F32)
    loss_ref[...] = jnp.sum(jnp.sum(tail, 0, keepdims=True), 1, keepdims=True)
    dmixed = nt(dfeat, out_ref[...])
    packed = packed_ref[...].astype(F32)
    pieces = []
    for head in range(heads):
        query, keys, values = split_head(packed, head)
        weights = weights_ref[head]
        cot = dmixed[:, head * HEAD : (head + 1) * HEAD].astype(BF16)
        dvalues = tn(weights.astype(BF16), cot)
        dweights = nt(cot, values)
        inner = jnp.sum(dweights * weights, -1, keepdims=True)
        dscores = (weights * (dweights - inner) * HEAD ** (-0.5)).astype(BF16)
        pieces += [nn(dscores, keys), tn(dscores, query), dvalues]
    dpacked = jnp.concatenate(pieces, axis=1)
    used = dpacked.shape[1]
    length = dpacked.shape[0]
    right = jnp.concatenate([dpacked, jnp.zeros((length, features - used), F32)], 1).astype(BF16)
    tailed = features - columns
    mixed = jnp.concatenate(
        [jnp.zeros((length, used - tailed), F32), mixed_ref[...].astype(F32)], 1
    ).astype(BF16)
    for half, into in enumerate((keep_ref, send_ref)):
        dfeat_rows = nt(pick_ref[half], dfeat).astype(BF16)
        normed_rows = normed_ref[half]
        for b in range(features // columns):
            block = slice(b * columns, (b + 1) * columns)
            total = nn(normed_rows, right[:, block]) + nn(feat_ref[half, b], dpred)
            if b == features // columns - 1:
                total = total + nn(dfeat_rows, mixed)
            into[:, block] = total.astype(BF16)


def axes_size(axes):
    size = 1
    for axis in axes:
        size = size * lax.axis_size(axis)
    return size


def share(rows, axes):
    return lax.all_to_all(
        jnp.broadcast_to(rows[None], (axes_size(axes), *rows.shape)), axes, 0, 0
    )


def gather_run(shard):
    runs = share(shard, (*Z, "c"))
    return runs.reshape(runs.shape[0] * runs.shape[1], runs.shape[2])


def gather_runs(run, own_c, own_yl):
    size = run.shape[0]
    half = size // 2
    ring = axes_size(Y)
    near, far = [], []
    for y in range(ring):
        for c, sign in ((0, -1), (1, 1)):
            near.append((y * 2 + c, (y + sign) % ring * 2 + c))
            far.append((y * 2 + c, (y + 2 * sign) % ring * 2 + c))
    first = lax.ppermute(run, (*Y, "c"), near)
    second = lax.ppermute(lax.dynamic_slice_in_dim(run, own_c * half, half, 0), (*Y, "c"), far)
    swap = [(0, 1), (1, 0)]
    first_other = lax.ppermute(first, "c", swap)
    second_other = lax.ppermute(second, "c", swap)
    ways = axes_size(Y[1:])
    step = 1 - 2 * own_c
    opposite = (own_yl + 2) % ways * size
    place = jnp.stack([
        own_yl * size,
        (own_yl + step + ways) % ways * size,
        (own_yl - step + ways) % ways * size,
        opposite + own_c * half,
        opposite + (1 - own_c) * half,
    ]).astype(jnp.int32)
    return place, (run, first, first_other, second, second_other)


def from_peers(rows, axis):
    ways = lax.axis_size(axis)
    return [
        lax.ppermute(rows(k), axis, [(i, (i + k) % ways) for i in range(ways)])
        for k in range(1, ways)
    ]


def add(a, b):
    return a.astype(F32) + b.astype(F32)


def result_kernel(parts_ref, q_ref, o_ref, p_ref):
    each, used = q_ref.shape
    columns = p_ref.shape[1]
    total = jnp.sum(parts_ref[...].astype(F32), 0)
    q_ref[...] = total[:each, :used]
    o_ref[...] = total[:each, used:]
    for i in range(total.shape[0] - each):
        for b in range(total.shape[1] // columns):
            row = i * (total.shape[1] // columns) + b
            p_ref[row : row + 1] = total[each + i : each + i + 1, b * columns : (b + 1) * columns]


def on_device(
    teacher_clips, teacher_gain, teacher_qkv, teacher_out_t, event_tokens, valid_counts, alignment,
    student_qkv, student_out, projector,
):
    clip, events, align = teacher_clips[0], event_tokens[0], alignment[0]
    length, width = clip.shape
    features = events.shape[1]
    columns = projector.shape[1]
    ways = lax.axis_size("x")
    rows = length // ways
    own_c, own_x = lax.axis_index("c"), lax.axis_index("x")
    own_y, own_z = lax.axis_index("y0"), lax.axis_index("z0")
    own_yl = lax.axis_index("yh") * 2 + own_y
    shares, along_z = axes_size(CLIP), axes_size(Z)

    run = gather_run(jnp.concatenate([teacher_qkv, teacher_out_t], 1))

    heads = student_out.shape[0] // HEAD
    each = features // shares
    half = shares // 2 * (each + each * columns // features)
    core = own_c.astype(jnp.int32).reshape(1)
    part, normed_rows, packed, mixed, weights, pick = pl.pallas_call(
        lambda *refs: student_kernel(shares, along_z, columns, *refs),
        out_shape=(
            shape((length, features), BF16),
            pltpu.HBM((2, half, length), BF16),
            pltpu.HBM((length, 3 * HEAD * heads), BF16),
            pltpu.HBM((length, HEAD * heads), BF16),
            pltpu.HBM((heads, length, length), F32),
            pltpu.HBM((2, half, features), BF16),
        ),
        in_specs=[SMEM] * 2 + [VMEM] * 3,
        out_specs=(VMEM,) + (pl.BlockSpec(),) * 5,
        compiler_params=PARAMS,
        cost_estimate=cost(4),
        name="student_forward",
    )(valid_counts, core, events, student_qkv.T, student_out)

    whole_proj = lax.all_gather(projector, "x", axis=0, tiled=False)
    own_rows = lambda array, place: lax.dynamic_slice_in_dim(array, place * rows, rows, 0)
    branch = own_rows(part, own_x).astype(F32)
    received = from_peers(lambda k: own_rows(part, (own_x + k) % ways), "x")
    run, received = lax.optimization_barrier((run, received))
    for other in received:
        branch = branch + other.astype(F32)
    feat_rows = (own_rows(events, own_x).astype(F32) + branch).astype(BF16)
    place, pieces = gather_runs(run, own_c, own_yl)
    feat = share(feat_rows, "x").reshape(length, features)
    teacher_normed = pl.pallas_call(
        teacher_norm_kernel,
        out_shape=shape((length, width), BF16),
        in_specs=[VMEM] * 2 + [ANY],
        out_specs=VMEM,
        compiler_params=PARAMS,
        cost_estimate=cost(1),
        name="teacher_norm",
    )(clip, teacher_gain.reshape(1, width), pieces[1])

    teacher_part = pl.pallas_call(
        teacher_kernel,
        out_shape=shape((length, width), BF16),
        in_specs=[SMEM] * 2 + [VMEM] * 6,
        out_specs=VMEM,
        scratch_shapes=[
            pltpu.VMEM((width, teacher_qkv.shape[1] + teacher_out_t.shape[1]), BF16),
            pltpu.VMEM((length, teacher_out_t.shape[1]), F32),
        ],
        compiler_params=PARAMS,
        cost_estimate=cost(5),
        name="teacher",
    )(place, align, teacher_normed, *pieces)

    teacher_parts = lax.all_to_all(teacher_part.reshape(ways, rows, width), "x", 0, 0)
    per_block = BLOCK // rows
    source = align[own_x // per_block] * BLOCK + own_x % per_block * rows
    own_tokens = lax.dynamic_slice_in_dim(clip, source, rows, 0)
    places = jnp.stack([own_c, own_x]).astype(jnp.int32)
    feat_extra, pred = pl.pallas_call(
        lambda *refs: feature_kernel(shares, along_z, *refs),
        out_shape=(
            pltpu.HBM((2, features // columns, half, length), BF16), shape((rows, width), F32),
        ),
        in_specs=[SMEM] + [VMEM] * 3 + [ANY],
        out_specs=(pl.BlockSpec(), VMEM),
        compiler_params=PARAMS,
        cost_estimate=cost(4),
        name="student_features",
    )(places, feat, feat_rows, whole_proj, teacher_part)
    message = pl.pallas_call(
        lambda *refs: diff_kernel(shares, *refs),
        out_shape=shape((ways, rows, features + columns + BLOCK), BF16),
        in_specs=[SMEM] * 2 + [VMEM] * 4,
        out_specs=VMEM,
        compiler_params=PARAMS,
        cost_estimate=cost(2),
        name="difference",
    )(valid_counts, places, teacher_parts, own_tokens, pred, whole_proj)
    back = lax.all_to_all(message, "x", 0, 0).reshape(length, features + columns + BLOCK)

    keep, send, loss = pl.pallas_call(
        backward_kernel,
        out_shape=(shape((half, features), BF16), shape((half, features), BF16), shape((1, 1), F32)),
        in_specs=[VMEM] * 8,
        out_specs=(VMEM,) * 3,
        compiler_params=PARAMS,
        cost_estimate=cost(4),
        name="student_backward",
    )(back, packed, weights, mixed, student_out, pick, normed_rows, feat_extra)

    total = add(keep, lax.ppermute(send, "c", [(0, 1), (1, 0)]))
    for step in range(2):
        bit = jnp.where(own_c == step, own_y, own_z)
        parts = total.reshape(2, total.shape[0] // 2, features)
        partners = []
        for y in range(2):
            for z in range(2):
                for c in range(2):
                    other = (1 - y, z) if c == step else (y, 1 - z)
                    partners.append(((y * 2 + z) * 2 + c, (other[0] * 2 + other[1]) * 2 + c))
        away = lax.dynamic_index_in_dim(parts, 1 - bit, 0, False).astype(BF16)
        stay = lax.dynamic_index_in_dim(parts, bit, 0, False)
        total = add(stay, lax.ppermute(away, ("y0", "z0", "c"), partners))
    far = axes_size(FAR)
    total = total.astype(BF16).reshape(far, total.shape[0] // far, features)
    spread = lax.all_to_all(total, FAR, 0, 0)
    used = 3 * HEAD * heads
    grad_q, grad_o, grad_p = pl.pallas_call(
        result_kernel,
        out_shape=(
            shape((each, used), F32), shape((each, HEAD * heads), F32), shape((each, columns), F32),
        ),
        in_specs=[VMEM],
        out_specs=(VMEM,) * 3,
        compiler_params=PARAMS,
        cost_estimate=cost(1),
        name="gradient_rows",
    )(spread)
    return loss.reshape(1), grad_q, grad_o.T, grad_p


def solution(mesh):
    group, dp, tensor = mesh.devices.shape
    devices = mesh.devices.reshape(group, 2, 2, dp // 16, 2, 2, tensor)
    fine = Mesh(devices, (*CLIP, "x"))
    dp = CLIP[1:]
    in_specs = (
        P(CLIP, None, None), P(), P(dp, "x"), P(dp, "x"), P(CLIP, None, None), P(CLIP), P(CLIP, None),
        P(None, "x"), P("x", None), P(None, "x"),
    )
    out_specs = (P(CLIP), P(CLIP, "x"), P("x", CLIP), P(CLIP, "x"))
    return jax.shard_map(
        on_device, mesh=fine, in_specs=in_specs, out_specs=out_specs, check_vma=False
    )
```

```python
import jax
import jax.numpy as jnp
from jax import lax
from jax.experimental import pallas as pl
from jax.experimental.pallas import tpu as pltpu
from jax.sharding import Mesh, PartitionSpec as P

HEAD = 64
BLOCK = 128
F32 = jnp.float32
BF16 = jnp.bfloat16
CLIP = ("g", "y", "z", "c")
ANY = pl.BlockSpec(memory_space=pl.ANY)
VMEM = pl.BlockSpec(memory_space=pltpu.VMEM)
SMEM = pl.BlockSpec(memory_space=pltpu.SMEM)
PARAMS = pltpu.CompilerParams(vmem_limit_bytes=20 * 1024 * 1024)


def cost(microseconds):
    return pl.CostEstimate(flops=microseconds * 10**9, bytes_accessed=10**6, transcendentals=0)


def shape(dims, dtype):
    return jax.ShapeDtypeStruct(dims, dtype)


def nn(a, b):
    return lax.dot_general(a, b, (((1,), (0,)), ((), ())), preferred_element_type=F32)


def nt(a, b):
    return lax.dot_general(a, b, (((1,), (1,)), ((), ())), preferred_element_type=F32)


def tn(a, b):
    return lax.dot_general(a, b, (((0,), (0,)), ((), ())), preferred_element_type=F32)


def norm_rows(rows):
    rows = rows.astype(F32)
    centre = rows - jnp.mean(rows, -1, keepdims=True)
    spread = jnp.mean(centre * centre, -1, keepdims=True)
    return centre * lax.rsqrt(spread + 1e-05)


def split_head(packed, head):
    first = head * 3 * HEAD
    return [packed[:, first + i * HEAD : first + (i + 1) * HEAD].astype(BF16) for i in range(3)]


def softmax(scores):
    top = jnp.max(scores, -1, keepdims=True)
    weights = jnp.exp(scores - top)
    return weights / jnp.sum(weights, -1, keepdims=True)


def pick_rows(rows, shares, columns, core, extra):
    each = rows // shares
    block = each + each * columns // rows
    place = lax.broadcasted_iota(jnp.int32, (shares // 2 * block, 1), 0)
    chip, row = place // block, place % block
    base = (chip * 2 + core) * each
    if extra is None:
        wanted = jnp.where(row < each, base + row, -1)
    else:
        wanted = jnp.where(row >= each, base + (row - each) * (rows // columns) + extra, -1)
    source = lax.broadcasted_iota(jnp.int32, (shares // 2 * block, rows), 1)
    return jnp.where(source == wanted, 1.0, 0.0).astype(BF16)


def spread_kernel(qkv_ref, out_ref, spread_ref):
    joined = jnp.concatenate([qkv_ref[...], out_ref[...]], 1)
    spread_ref[...] = jnp.broadcast_to(joined[None], spread_ref.shape)


def student_kernel(
    shares, columns, count_ref, core_ref, events_ref, qkv_ref, out_ref,
    part_ref, normed_ref, packed_ref, mixed_ref, weights_ref, pick_ref,
):
    length, features = events_ref.shape
    heads = out_ref.shape[0] // HEAD
    normed = norm_rows(events_ref[...]).astype(BF16)
    for half in range(2):
        core = core_ref[0] if half == 0 else 1 - core_ref[0]
        pick_ref[half] = pick_rows(features, shares, columns, core, None)
        normed_ref[half] = nt(pick_ref[half], normed).astype(BF16)
    packed = nt(normed, qkv_ref[...])
    packed_ref[...] = packed.astype(BF16)
    usable = lax.broadcasted_iota(jnp.int32, (length, length), 1) < count_ref[0]
    mixed = []
    for head in range(heads):
        query, keys, values = split_head(packed, head)
        scores = jnp.where(usable, nt(query, keys) * HEAD ** (-0.5), -1e30)
        weights = softmax(scores)
        weights_ref[head] = weights
        mixed.append(nn(weights.astype(BF16), values))
    mixed = jnp.concatenate(mixed, axis=1).astype(BF16)
    mixed_ref[...] = mixed
    part_ref[...] = nn(mixed, out_ref[...]).astype(BF16)


def teacher_norm_kernel(clip_ref, gain_ref, after_ref, normed_ref):
    normed_ref[...] = (norm_rows(clip_ref[...]) * gain_ref[...]).astype(BF16)


def teacher_kernel(
    place_ref, align_ref, normed_ref, own_ref, other_ref, part_ref, parts_ref, mixed_ref
):
    blocks, cores, rows, width = parts_ref.shape
    for i, piece in enumerate((own_ref, other_ref)):
        core = place_ref[0] if i == 0 else 1 - place_ref[0]
        parts_ref[:, pl.ds(core, 1)] = piece[...].reshape(blocks, 1, rows, width)
    full_ref = parts_ref[...].reshape(blocks * cores * rows, width)
    heads = width // (4 * HEAD)
    packed = nn(normed_ref[...], full_ref[:, : heads * 3 * HEAD])
    mixed = []
    for head in range(heads):
        query, keys, values = split_head(packed, head)
        weights = softmax(nt(query, keys) * HEAD ** (-0.5))
        mixed.append(nn(weights.astype(BF16), values))
    mixed_ref[...] = jnp.concatenate(mixed, axis=1)
    for i in range(align_ref.shape[0]):
        first = pl.multiple_of(align_ref[i] * BLOCK, BLOCK)
        chosen = mixed_ref[pl.ds(first, BLOCK), :].astype(BF16)
        part_ref[i * BLOCK : (i + 1) * BLOCK, :] = nt(
            chosen, full_ref[:, heads * 3 * HEAD :]
        ).astype(BF16)


def feature_kernel(shares, ways, place_ref, *refs):
    feat_refs = refs[:ways]
    own_ref, mine_ref, other_ref, after_ref, extra_ref, pred_ref, proj_ref, feat_ref = refs[ways:]
    features, columns = own_ref.shape
    rows = feat_refs[0].shape[0]
    half = features // 2
    proj_ref[place_ref[1]] = own_ref[...]
    for k in range(ways):
        source = place_ref[1 + k]
        feat_ref[pl.ds(pl.multiple_of(source * rows, rows), rows), :] = feat_refs[k][...]
        if k > 0:
            first = pl.multiple_of(place_ref[0] * half, half)
            second = pl.multiple_of((1 - place_ref[0]) * half, half)
            proj_ref[source, pl.ds(first, half), :] = mine_ref[k - 1]
            proj_ref[source, pl.ds(second, half), :] = other_ref[k - 1]
    for k in range(ways):
        pred_ref[:, k * columns : (k + 1) * columns] = nn(feat_refs[0][...], proj_ref[k])
    feat = feat_ref[...]
    for half in range(2):
        core = place_ref[0] if half == 0 else 1 - place_ref[0]
        for b in range(features // columns):
            pick = pick_rows(features, shares, columns, core, b)
            extra_ref[half, b] = nt(pick, feat).astype(BF16)


def diff_kernel(
    clips, count_ref, place_ref, parts_ref, tokens_ref, pred_ref, source_ref, out_ref, proj_ref, sem
):
    copy = pltpu.make_async_copy(source_ref, proj_ref, sem)
    copy.start()
    rows, width = tokens_ref.shape
    ways, features, columns = proj_ref.shape
    branch = parts_ref[0].astype(F32)
    for i in range(1, ways):
        branch = branch + parts_ref[i].astype(F32)
    target = (tokens_ref[...].astype(F32) + branch).astype(BF16).astype(F32)
    count = count_ref[0]
    live = lax.broadcasted_iota(jnp.int32, (rows, 1), 0) + place_ref[1] * rows < count
    scale = jnp.full((1, 1), count, jnp.int32).astype(F32) * width
    factor = 2.0 / (scale * clips)
    diff = jnp.where(live, pred_ref[...] - target, 0.0)
    squares = jnp.sum(diff * diff, -1, keepdims=True) / scale
    dpred = (diff * factor).astype(BF16)
    copy.wait()
    dfeat = jnp.zeros((rows, features), F32)
    for k in range(ways):
        dfeat = dfeat + nt(dpred[:, k * columns : (k + 1) * columns], proj_ref[k])
    dfeat = dfeat.astype(BF16)
    high = squares.astype(BF16)
    rest = squares - high.astype(F32)
    middle = rest.astype(BF16)
    low = (rest - middle.astype(F32)).astype(BF16)
    lane = lax.broadcasted_iota(jnp.int32, (rows, BLOCK), 1)
    tail = jnp.where(lane == 0, high.astype(F32), jnp.where(lane == 1, middle.astype(F32), 0.0))
    tail = jnp.where(lane == 2, low.astype(F32), tail).astype(BF16)
    for i in range(ways):
        out_ref[i, :, :features] = dfeat
        out_ref[i, :, features : features + columns] = dpred[:, i * columns : (i + 1) * columns]
        out_ref[i, :, features + columns :] = tail


def backward_kernel(
    back_ref, packed_ref, weights_ref, mixed_ref, out_ref, pick_ref, normed_ref, feat_ref,
    keep_ref, send_ref, loss_ref,
):
    features = out_ref.shape[1]
    heads = out_ref.shape[0] // HEAD
    dfeat = back_ref[:, :features]
    columns = back_ref.shape[1] - features - BLOCK
    dpred = back_ref[:, features : features + columns]
    tail = back_ref[:, features + columns :].astype(F32)
    loss_ref[...] = jnp.sum(jnp.sum(tail, 0, keepdims=True), 1, keepdims=True)
    dmixed = nt(dfeat, out_ref[...])
    packed = packed_ref[...].astype(F32)
    pieces = []
    for head in range(heads):
        query, keys, values = split_head(packed, head)
        weights = weights_ref[head]
        cot = dmixed[:, head * HEAD : (head + 1) * HEAD].astype(BF16)
        dvalues = tn(weights.astype(BF16), cot)
        dweights = nt(cot, values)
        inner = jnp.sum(dweights * weights, -1, keepdims=True)
        dscores = (weights * (dweights - inner) * HEAD ** (-0.5)).astype(BF16)
        pieces += [nn(dscores, keys), tn(dscores, query), dvalues]
    dpacked = jnp.concatenate(pieces, axis=1)
    used = dpacked.shape[1]
    length = dpacked.shape[0]
    right = jnp.concatenate([dpacked, jnp.zeros((length, features - used), F32)], 1).astype(BF16)
    tailed = features - columns
    mixed = jnp.concatenate(
        [jnp.zeros((length, used - tailed), F32), mixed_ref[...].astype(F32)], 1
    ).astype(BF16)
    for half, into in enumerate((keep_ref, send_ref)):
        dfeat_rows = nt(pick_ref[half], dfeat).astype(BF16)
        normed_rows = normed_ref[half]
        for b in range(features // columns):
            block = slice(b * columns, (b + 1) * columns)
            total = nn(normed_rows, right[:, block]) + nn(feat_ref[half, b], dpred)
            if b == features // columns - 1:
                total = total + nn(dfeat_rows, mixed)
            into[:, block] = total.astype(BF16)


SWAP = [(0, 1), (1, 0)]


def from_peers(rows, axis):
    ways = lax.axis_size(axis)
    return [
        lax.ppermute(rows(k), axis, [(i, (i + k) % ways) for i in range(ways)])
        for k in range(1, ways)
    ]


def add(a, b):
    return a.astype(F32) + b.astype(F32)


def result_kernel(parts_ref, q_ref, o_ref, p_ref):
    each, used = q_ref.shape
    columns = p_ref.shape[1]
    total = jnp.sum(parts_ref[...].astype(F32), 0)
    q_ref[...] = total[:each, :used]
    o_ref[...] = total[:each, used:]
    for i in range(total.shape[0] - each):
        for b in range(total.shape[1] // columns):
            row = i * (total.shape[1] // columns) + b
            p_ref[row : row + 1] = total[each + i : each + i + 1, b * columns : (b + 1) * columns]


def on_device(
    teacher_clips, teacher_gain, teacher_qkv, teacher_out_t, event_tokens, valid_counts, alignment,
    student_qkv, student_out, projector,
):
    clip, events, align = teacher_clips[0], event_tokens[0], alignment[0]
    length, width = clip.shape
    features = events.shape[1]
    columns = projector.shape[1]
    ways = lax.axis_size("x")
    rows = length // ways
    own_c, own_x = lax.axis_index("c"), lax.axis_index("x")
    shares = 1
    for axis in CLIP:
        shares = shares * lax.axis_size(axis)

    senders = lax.axis_size("y") * lax.axis_size("z")
    shard = pl.pallas_call(
        spread_kernel,
        out_shape=shape(
            (senders, teacher_qkv.shape[0], teacher_qkv.shape[1] + teacher_out_t.shape[1]), BF16
        ),
        compiler_params=PARAMS,
        name="spread_rows",
    )(teacher_qkv, teacher_out_t)
    own_core = lax.all_to_all(shard, ("y", "z"), 0, 0)
    half = features // 2
    proj_half = lax.dynamic_slice_in_dim(projector, own_c * half, half, 0)
    proj_halves = jnp.stack(from_peers(lambda k: proj_half, "x"))

    heads = student_out.shape[0] // HEAD
    each = features // shares
    picked = shares // 2 * (each + each * columns // features)
    core = own_c.astype(jnp.int32).reshape(1)
    part, normed_rows, packed, mixed, weights, pick = pl.pallas_call(
        lambda *refs: student_kernel(shares, columns, *refs),
        out_shape=(
            shape((length, features), BF16),
            pltpu.HBM((2, picked, length), BF16),
            pltpu.HBM((length, 3 * HEAD * heads), BF16),
            pltpu.HBM((length, HEAD * heads), BF16),
            pltpu.HBM((heads, length, length), F32),
            pltpu.HBM((2, picked, features), BF16),
        ),
        in_specs=[SMEM] * 2 + [VMEM] * 3,
        out_specs=(VMEM,) + (pl.BlockSpec(),) * 5,
        compiler_params=PARAMS,
        cost_estimate=cost(4),
        name="student_forward",
    )(valid_counts, core, events, student_qkv.T, student_out)

    own_rows = lambda array, place: lax.dynamic_slice_in_dim(array, place * rows, rows, 0)
    branch = own_rows(part, own_x).astype(F32)
    received = from_peers(lambda k: own_rows(part, (own_x + k) % ways), "x")
    for other in received:
        branch = branch + other.astype(F32)
    feat_rows = (own_rows(events, own_x).astype(F32) + branch).astype(BF16)
    feats = [feat_rows] + from_peers(lambda k: feat_rows, "x")
    own_core, feats, proj_halves = lax.optimization_barrier((own_core, feats, proj_halves))
    other_core = lax.ppermute(own_core, "c", SWAP)
    proj_others = lax.ppermute(proj_halves, "c", SWAP)
    places = jnp.stack([own_c] + [(own_x - k + ways) % ways for k in range(ways)]).astype(jnp.int32)
    teacher_normed = pl.pallas_call(
        teacher_norm_kernel,
        out_shape=shape((length, width), BF16),
        in_specs=[VMEM] * 2 + [ANY],
        out_specs=VMEM,
        compiler_params=PARAMS,
        cost_estimate=cost(1),
        name="teacher_norm",
    )(clip, teacher_gain.reshape(1, width), feat_rows)

    teacher_part = pl.pallas_call(
        teacher_kernel,
        out_shape=shape((length, width), BF16),
        in_specs=[SMEM] * 2 + [VMEM] * 3,
        out_specs=VMEM,
        scratch_shapes=[
            pltpu.VMEM((senders, 2, *shard.shape[1:]), BF16),
            pltpu.VMEM((length, teacher_out_t.shape[1]), F32),
        ],
        compiler_params=PARAMS,
        cost_estimate=cost(5),
        name="teacher",
    )(places, align, teacher_normed, own_core, other_core)

    teacher_parts = lax.all_to_all(teacher_part.reshape(ways, rows, width), "x", 0, 0)
    per_block = BLOCK // rows
    source = align[own_x // per_block] * BLOCK + own_x % per_block * rows
    own_tokens = lax.dynamic_slice_in_dim(clip, source, rows, 0)
    feat_extra, pred, whole_proj = pl.pallas_call(
        lambda *refs: feature_kernel(shares, ways, *refs),
        out_shape=(
            pltpu.HBM((2, features // columns, picked, length), BF16), shape((rows, width), F32),
            pltpu.HBM((ways, features, columns), BF16),
        ),
        in_specs=[SMEM] + [pl.BlockSpec()] * (ways + 3) + [ANY],
        out_specs=(pl.BlockSpec(), VMEM, pl.BlockSpec()),
        scratch_shapes=[pltpu.VMEM((length, features), BF16)],
        compiler_params=PARAMS,
        cost_estimate=cost(4),
        name="student_features",
    )(places, *feats, projector, proj_halves, proj_others, teacher_part)
    message = pl.pallas_call(
        lambda *refs: diff_kernel(shares, *refs),
        out_shape=shape((ways, rows, features + columns + BLOCK), BF16),
        in_specs=[SMEM] * 2 + [VMEM] * 3 + [ANY],
        out_specs=VMEM,
        scratch_shapes=[
            pltpu.VMEM((ways, features, columns), BF16), pltpu.SemaphoreType.DMA,
        ],
        compiler_params=PARAMS,
        cost_estimate=cost(2),
        name="difference",
    )(valid_counts, places, teacher_parts, own_tokens, pred, whole_proj)
    back = lax.all_to_all(message, "x", 0, 0).reshape(length, features + columns + BLOCK)

    keep, send, loss = pl.pallas_call(
        backward_kernel,
        out_shape=(shape((picked, features), BF16), shape((picked, features), BF16), shape((1, 1), F32)),
        in_specs=[VMEM] * 8,
        out_specs=(VMEM,) * 3,
        compiler_params=PARAMS,
        cost_estimate=cost(4),
        name="student_backward",
    )(back, packed, weights, mixed, student_out, pick, normed_rows, feat_extra)

    total = add(keep, lax.ppermute(send, "c", SWAP)).astype(BF16)
    chips = shares // 2
    spread = lax.all_to_all(
        total.reshape(chips, total.shape[0] // chips, features), CLIP[:3], 0, 0
    )
    used = 3 * HEAD * heads
    grad_q, grad_o, grad_p = pl.pallas_call(
        result_kernel,
        out_shape=(
            shape((each, used), F32), shape((each, HEAD * heads), F32), shape((each, columns), F32),
        ),
        in_specs=[VMEM],
        out_specs=(VMEM,) * 3,
        compiler_params=PARAMS,
        cost_estimate=cost(1),
        name="gradient_rows",
    )(spread)
    return loss.reshape(1), grad_q, grad_o.T, grad_p


def solution(mesh):
    group, dp, tensor = mesh.devices.shape
    fine = Mesh(mesh.devices.reshape(group, 4, dp // 8, 2, tensor), (*CLIP, "x"))
    dp = CLIP[1:]
    in_specs = (
        P(CLIP, None, None), P(), P(dp, "x"), P(dp, "x"), P(CLIP, None, None), P(CLIP), P(CLIP, None),
        P(None, "x"), P("x", None), P(None, "x"),
    )
    out_specs = (P(CLIP), P(CLIP, "x"), P("x", CLIP), P(CLIP, "x"))
    return jax.shard_map(
        on_device, mesh=fine, in_specs=in_specs, out_specs=out_specs, check_vma=False
    )
```

```python
import jax
import jax.numpy as jnp
from jax import lax
from jax.experimental import pallas as pl
from jax.experimental.pallas import tpu as pltpu
from jax.sharding import Mesh, PartitionSpec as P

HEAD = 64
BLOCK = 128
F32 = jnp.float32
BF16 = jnp.bfloat16
CLIP = ("g", "y", "z", "c")
ANY = pl.BlockSpec(memory_space=pl.ANY)
HBM = pl.BlockSpec(memory_space=pltpu.HBM)
VMEM = pl.BlockSpec(memory_space=pltpu.VMEM)
SMEM = pl.BlockSpec(memory_space=pltpu.SMEM)
PARAMS = pltpu.CompilerParams(vmem_limit_bytes=20 * 1024 * 1024)
FETCHING = pltpu.CompilerParams(vmem_limit_bytes=52 * 1024 * 1024)


def cost(microseconds):
    return pl.CostEstimate(flops=microseconds * 10**9, bytes_accessed=10**6, transcendentals=0)


def shape(dims, dtype):
    return jax.ShapeDtypeStruct(dims, dtype)


def nn(a, b):
    return lax.dot_general(a, b, (((1,), (0,)), ((), ())), preferred_element_type=F32)


def nt(a, b):
    return lax.dot_general(a, b, (((1,), (1,)), ((), ())), preferred_element_type=F32)


def tn(a, b):
    return lax.dot_general(a, b, (((0,), (0,)), ((), ())), preferred_element_type=F32)


def norm_rows(rows):
    rows = rows.astype(F32)
    centre = rows - jnp.mean(rows, -1, keepdims=True)
    spread = jnp.mean(centre * centre, -1, keepdims=True)
    return centre * lax.rsqrt(spread + 1e-05)


def split_head(packed, head):
    first = head * 3 * HEAD
    return [packed[:, first + i * HEAD : first + (i + 1) * HEAD].astype(BF16) for i in range(3)]


def softmax(scores):
    top = jnp.max(scores, -1, keepdims=True)
    weights = jnp.exp(scores - top)
    return weights / jnp.sum(weights, -1, keepdims=True)


def pick_rows(rows, shares, columns, core, extra):
    each = rows // shares
    block = each + each * columns // rows
    place = lax.broadcasted_iota(jnp.int32, (shares // 2 * block, 1), 0)
    chip, row = place // block, place % block
    base = (chip * 2 + core) * each
    if extra is None:
        wanted = jnp.where(row < each, base + row, -1)
    else:
        wanted = jnp.where(row >= each, base + (row - each) * (rows // columns) + extra, -1)
    source = lax.broadcasted_iota(jnp.int32, (shares // 2 * block, rows), 1)
    return jnp.where(source == wanted, 1.0, 0.0).astype(BF16)


def spread_kernel(qkv_ref, out_ref, spread_ref):
    joined = jnp.concatenate([qkv_ref[...], out_ref[...]], 1)
    spread_ref[...] = jnp.broadcast_to(joined[None], spread_ref.shape)


def student_kernel(
    shares, count_ref, place_ref, events_ref, qkv_ref, out_ref, proj_ref, *refs
):
    ways = len(refs) - 6
    own_ref, peer_refs = refs[0], refs[1:ways]
    normed_ref, packed_ref, mixed_ref, weights_ref, pick_ref, part_ref = refs[ways:]
    columns = proj_ref.shape[1]
    length, features = events_ref.shape
    heads = out_ref.shape[0] // HEAD
    normed = norm_rows(events_ref[...]).astype(BF16)
    for half in range(2):
        core = place_ref[0] if half == 0 else 1 - place_ref[0]
        pick_ref[half] = pick_rows(features, shares, columns, core, None)
        normed_ref[half] = nt(pick_ref[half], normed).astype(BF16)
    packed = nt(normed, qkv_ref[...])
    packed_ref[...] = packed.astype(BF16)
    usable = lax.broadcasted_iota(jnp.int32, (length, length), 1) < count_ref[0]
    mixed = []
    for head in range(heads):
        query, keys, values = split_head(packed, head)
        scores = jnp.where(usable, nt(query, keys) * HEAD ** (-0.5), -1e30)
        weights = softmax(scores)
        weights_ref[head] = weights
        mixed.append(nn(weights.astype(BF16), values))
    mixed = jnp.concatenate(mixed, axis=1).astype(BF16)
    mixed_ref[...] = mixed
    part_ref[...] = nn(mixed, out_ref[...])
    rows = own_ref.shape[0]
    half = features // 2
    blocks = features // columns
    proj_half = proj_ref[pl.ds(pl.multiple_of(place_ref[0] * half, half), half), :]
    for k in range(ways):
        first = pl.multiple_of(place_ref[1 + k] * rows, rows)
        chosen = part_ref[pl.ds(first, rows), :].astype(BF16)
        if k == 0:
            own_ref[...] = chosen
            continue
        for b in range(blocks):
            peer_refs[k - 1][b * rows : (b + 1) * rows] = chosen[:, b * columns : (b + 1) * columns]
        peer_refs[k - 1][blocks * rows :] = proj_half


def rows_kernel(ways, events_ref, own_ref, *refs):
    peer_refs, (feat_ref, proj_ref) = refs[: ways - 1], refs[ways - 1 :]
    rows, features = own_ref.shape
    columns = proj_ref.shape[2]
    for b in range(features // columns):
        block = slice(b * columns, (b + 1) * columns)
        branch = own_ref[:, block].astype(F32)
        for peer in peer_refs:
            branch = branch + peer[b * rows : (b + 1) * rows].astype(F32)
        feat_ref[:, block] = (events_ref[:, block].astype(F32) + branch).astype(BF16)
    for k, peer in enumerate(peer_refs):
        proj_ref[k] = peer[features // columns * rows :]


def teacher_norm_kernel(clip_ref, gain_ref, after_ref, normed_ref):
    normed_ref[...] = (norm_rows(clip_ref[...]) * gain_ref[...]).astype(BF16)


def teacher_kernel(
    place_ref, align_ref, normed_ref, own_ref, other_ref, feat_ref, part_ref, parts_ref, mixed_ref
):
    blocks, cores, rows, width = parts_ref.shape
    for i, piece in enumerate((own_ref, other_ref)):
        core = place_ref[0] if i == 0 else 1 - place_ref[0]
        parts_ref[:, pl.ds(core, 1)] = piece[...].reshape(blocks, 1, rows, width)
    full_ref = parts_ref[...].reshape(blocks * cores * rows, width)
    heads = width // (4 * HEAD)
    packed = nn(normed_ref[...], full_ref[:, : heads * 3 * HEAD])
    mixed = []
    for head in range(heads):
        query, keys, values = split_head(packed, head)
        weights = softmax(nt(query, keys) * HEAD ** (-0.5))
        mixed.append(nn(weights.astype(BF16), values))
    mixed_ref[...] = jnp.concatenate(mixed, axis=1)
    ways, shared = part_ref.shape[:2]
    per_block = BLOCK // shared
    outputs = blocks * cores * rows
    for i in range(align_ref.shape[0]):
        first = pl.multiple_of(align_ref[i] * BLOCK, BLOCK)
        chosen = mixed_ref[pl.ds(first, BLOCK), :].astype(BF16)
        part = nt(chosen, full_ref[:, heads * 3 * HEAD :]).astype(BF16)
        for k in range(per_block):
            part_ref[i * per_block + k, :, :outputs] = part[k * shared : (k + 1) * shared]
    for i in range(ways):
        part_ref[i, :, outputs:] = feat_ref[...]


def predict_kernel(
    ways, place_ref, feat_ref, own_ref, mine_ref, other_ref, after_ref, pred_ref, proj_ref
):
    features, columns = own_ref.shape
    half = features // 2
    first = pl.multiple_of(place_ref[0] * half, half)
    second = pl.multiple_of((1 - place_ref[0]) * half, half)
    proj_ref[place_ref[1]] = own_ref[...]
    for k in range(1, ways):
        source = place_ref[1 + k]
        proj_ref[source, pl.ds(first, half), :] = mine_ref[k - 1]
        proj_ref[source, pl.ds(second, half), :] = other_ref[k - 1]
    for k in range(ways):
        pred_ref[:, k * columns : (k + 1) * columns] = nn(feat_ref[...], proj_ref[k])


def extra_kernel(shares, columns, place_ref, parts_ref, after_ref, extra_ref):
    features = extra_ref.shape[1] * columns
    rows = parts_ref.shape[0] * parts_ref.shape[1]
    feat = parts_ref[...].reshape(rows, parts_ref.shape[2])[:, -features:]
    for half in range(2):
        core = place_ref[0] if half == 0 else 1 - place_ref[0]
        for b in range(features // columns):
            pick = pick_rows(features, shares, columns, core, b)
            extra_ref[half, b] = nt(pick, feat).astype(BF16)


def diff_kernel(
    clips, count_ref, place_ref, parts_ref, tokens_ref, pred_ref, source_ref, out_ref, proj_ref, sem
):
    copy = pltpu.make_async_copy(source_ref, proj_ref, sem)
    copy.start()
    rows, width = tokens_ref.shape
    ways, features, columns = proj_ref.shape
    branch = parts_ref[0, :, :width].astype(F32)
    for i in range(1, ways):
        branch = branch + parts_ref[i, :, :width].astype(F32)
    target = (tokens_ref[...].astype(F32) + branch).astype(BF16).astype(F32)
    count = count_ref[0]
    live = lax.broadcasted_iota(jnp.int32, (rows, 1), 0) + place_ref[1] * rows < count
    scale = jnp.full((1, 1), count, jnp.int32).astype(F32) * width
    factor = 2.0 / (scale * clips)
    diff = jnp.where(live, pred_ref[...] - target, 0.0)
    squares = jnp.sum(diff * diff, -1, keepdims=True) / scale
    dpred = (diff * factor).astype(BF16)
    copy.wait()
    dfeat = jnp.zeros((rows, features), F32)
    for k in range(ways):
        dfeat = dfeat + nt(dpred[:, k * columns : (k + 1) * columns], proj_ref[k])
    dfeat = dfeat.astype(BF16)
    high = squares.astype(BF16)
    rest = squares - high.astype(F32)
    middle = rest.astype(BF16)
    low = (rest - middle.astype(F32)).astype(BF16)
    lane = lax.broadcasted_iota(jnp.int32, (rows, BLOCK), 1)
    tail = jnp.where(lane == 0, high.astype(F32), jnp.where(lane == 1, middle.astype(F32), 0.0))
    tail = jnp.where(lane == 2, low.astype(F32), tail).astype(BF16)
    for i in range(ways):
        out_ref[i, :, :features] = dfeat
        out_ref[i, :, features : features + columns] = dpred[:, i * columns : (i + 1) * columns]
        out_ref[i, :, features + columns :] = tail


def backward_kernel(back_ref, *refs):
    held = (len(refs) - 4) // 2
    sources, (keep_ref, send_ref, loss_ref) = refs[:held], refs[held : held + 3]
    buffers, sems = refs[held + 3 : -1], refs[-1]
    copies = [
        pltpu.make_async_copy(source, buffer, sems.at[i])
        for i, (source, buffer) in enumerate(zip(sources, buffers))
    ]
    for copy in copies:
        copy.start()
    out_ref, packed_ref, weights_ref, mixed_ref, pick_ref, normed_ref, feat_ref = buffers
    for copy in copies[:4]:
        copy.wait()
    features = out_ref.shape[1]
    heads = out_ref.shape[0] // HEAD
    dfeat = back_ref[:, :features]
    columns = back_ref.shape[1] - features - BLOCK
    dpred = back_ref[:, features : features + columns]
    tail = back_ref[:, features + columns :].astype(F32)
    loss_ref[...] = jnp.sum(jnp.sum(tail, 0, keepdims=True), 1, keepdims=True)
    dmixed = nt(dfeat, out_ref[...])
    packed = packed_ref[...].astype(F32)
    pieces = []
    for head in range(heads):
        query, keys, values = split_head(packed, head)
        weights = weights_ref[head]
        cot = dmixed[:, head * HEAD : (head + 1) * HEAD].astype(BF16)
        dvalues = tn(weights.astype(BF16), cot)
        dweights = nt(cot, values)
        inner = jnp.sum(dweights * weights, -1, keepdims=True)
        dscores = (weights * (dweights - inner) * HEAD ** (-0.5)).astype(BF16)
        pieces += [nn(dscores, keys), tn(dscores, query), dvalues]
    dpacked = jnp.concatenate(pieces, axis=1)
    used = dpacked.shape[1]
    length = dpacked.shape[0]
    right = jnp.concatenate([dpacked, jnp.zeros((length, features - used), F32)], 1).astype(BF16)
    tailed = features - columns
    mixed = jnp.concatenate(
        [jnp.zeros((length, used - tailed), F32), mixed_ref[...].astype(F32)], 1
    ).astype(BF16)
    for copy in copies[4:]:
        copy.wait()
    for half, into in enumerate((keep_ref, send_ref)):
        dfeat_rows = nt(pick_ref[half], dfeat).astype(BF16)
        normed_rows = normed_ref[half]
        for b in range(features // columns):
            block = slice(b * columns, (b + 1) * columns)
            total = nn(normed_rows, right[:, block]) + nn(feat_ref[half, b], dpred)
            if b == features // columns - 1:
                total = total + nn(dfeat_rows, mixed)
            into[:, block] = total.astype(BF16)


SWAP = [(0, 1), (1, 0)]


def from_peers(rows, axis):
    ways = lax.axis_size(axis)
    return [
        lax.ppermute(rows(k), axis, [(i, (i + k) % ways) for i in range(ways)])
        for k in range(1, ways)
    ]


def add(a, b):
    return a.astype(F32) + b.astype(F32)


def result_kernel(parts_ref, q_ref, o_ref, p_ref):
    each, used = q_ref.shape
    columns = p_ref.shape[1]
    total = jnp.sum(parts_ref[...].astype(F32), 0)
    q_ref[...] = total[:each, :used]
    o_ref[...] = total[:each, used:]
    for i in range(total.shape[0] - each):
        for b in range(total.shape[1] // columns):
            row = i * (total.shape[1] // columns) + b
            p_ref[row : row + 1] = total[each + i : each + i + 1, b * columns : (b + 1) * columns]


def on_device(
    teacher_clips, teacher_gain, teacher_qkv, teacher_out_t, event_tokens, valid_counts, alignment,
    student_qkv, student_out, projector,
):
    clip, events, align = teacher_clips[0], event_tokens[0], alignment[0]
    length, width = clip.shape
    features = events.shape[1]
    columns = projector.shape[1]
    ways = lax.axis_size("x")
    rows = length // ways
    own_c, own_x = lax.axis_index("c"), lax.axis_index("x")
    shares = 1
    for axis in CLIP:
        shares = shares * lax.axis_size(axis)

    senders = lax.axis_size("y") * lax.axis_size("z")
    shard = pl.pallas_call(
        spread_kernel,
        out_shape=shape(
            (senders, teacher_qkv.shape[0], teacher_qkv.shape[1] + teacher_out_t.shape[1]), BF16
        ),
        compiler_params=PARAMS,
        name="spread_rows",
    )(teacher_qkv, teacher_out_t)
    own_core = lax.all_to_all(shard, ("y", "z"), 0, 0)
    heads = student_out.shape[0] // HEAD
    each = features // shares
    picked = shares // 2 * (each + each * columns // features)
    places = jnp.stack([own_c] + [(own_x + k) % ways for k in range(ways)]).astype(jnp.int32)
    message_rows = rows * features // columns + features // 2
    outs = pl.pallas_call(
        lambda *refs: student_kernel(shares, *refs),
        out_shape=(
            shape((rows, features), BF16),
            *[shape((message_rows, columns), BF16)] * (ways - 1),
            pltpu.HBM((2, picked, length), BF16),
            pltpu.HBM((length, 3 * HEAD * heads), BF16),
            pltpu.HBM((length, HEAD * heads), BF16),
            pltpu.HBM((heads, length, length), F32),
            pltpu.HBM((2, picked, features), BF16),
        ),
        in_specs=[SMEM] * 2 + [VMEM] * 4,
        out_specs=(VMEM,) * ways + (pl.BlockSpec(),) * 5,
        scratch_shapes=[pltpu.VMEM((length, features), F32)],
        compiler_params=PARAMS,
        cost_estimate=cost(4),
        name="student_forward",
    )(valid_counts, places, events, student_qkv.T, student_out, projector)
    own_part, peer_parts = outs[0], outs[1:ways]
    normed_rows, packed, mixed, weights, pick = outs[ways:]

    received = from_peers(lambda k: peer_parts[k - 1], "x")
    own_events = lax.dynamic_slice_in_dim(events, own_x * rows, rows, 0)
    feat_rows, proj_halves = pl.pallas_call(
        lambda *refs: rows_kernel(ways, *refs),
        out_shape=(
            shape((rows, features), BF16), shape((ways - 1, features // 2, columns), BF16),
        ),
        in_specs=[VMEM] * (ways + 1),
        out_specs=(VMEM,) * 2,
        compiler_params=PARAMS,
        cost_estimate=cost(1),
        name="student_rows",
    )(own_events, own_part, *received)
    own_core, feat_rows, proj_halves = lax.optimization_barrier((own_core, feat_rows, proj_halves))
    other_core = lax.ppermute(own_core, "c", SWAP)
    proj_others = lax.ppermute(proj_halves, "c", SWAP)
    teacher_normed = pl.pallas_call(
        teacher_norm_kernel,
        out_shape=shape((length, width), BF16),
        in_specs=[VMEM] * 2 + [ANY],
        out_specs=VMEM,
        compiler_params=PARAMS,
        cost_estimate=cost(1),
        name="teacher_norm",
    )(clip, teacher_gain.reshape(1, width), feat_rows)

    teacher_part = pl.pallas_call(
        teacher_kernel,
        out_shape=shape((ways, rows, width + features), BF16),
        in_specs=[SMEM] * 2 + [VMEM] * 4,
        out_specs=VMEM,
        scratch_shapes=[
            pltpu.VMEM((senders, 2, *shard.shape[1:]), BF16),
            pltpu.VMEM((length, teacher_out_t.shape[1]), F32),
        ],
        compiler_params=PARAMS,
        cost_estimate=cost(5),
        name="teacher",
    )(places, align, teacher_normed, own_core, other_core, feat_rows)

    teacher_parts = lax.all_to_all(teacher_part, "x", 0, 0)
    per_block = BLOCK // rows
    source = align[own_x // per_block] * BLOCK + own_x % per_block * rows
    own_tokens = lax.dynamic_slice_in_dim(clip, source, rows, 0)
    sources = jnp.stack([own_c] + [(own_x - k + ways) % ways for k in range(ways)]).astype(jnp.int32)
    pred, whole_proj = pl.pallas_call(
        lambda *refs: predict_kernel(ways, *refs),
        out_shape=(shape((rows, width), F32), pltpu.HBM((ways, features, columns), BF16)),
        in_specs=[SMEM] + [VMEM] * 4 + [ANY],
        out_specs=(VMEM, pl.BlockSpec()),
        compiler_params=PARAMS,
        cost_estimate=cost(2),
        name="student_predict",
    )(sources, feat_rows, projector, proj_halves, proj_others, teacher_part)
    message = pl.pallas_call(
        lambda *refs: diff_kernel(shares, *refs),
        out_shape=shape((ways, rows, features + columns + BLOCK), BF16),
        in_specs=[SMEM] * 2 + [VMEM] * 3 + [HBM],
        out_specs=VMEM,
        scratch_shapes=[
            pltpu.VMEM((ways, features, columns), BF16), pltpu.SemaphoreType.DMA,
        ],
        compiler_params=FETCHING,
        cost_estimate=cost(2),
        name="difference",
    )(valid_counts, places, teacher_parts, own_tokens, pred, whole_proj)
    feat_extra = pl.pallas_call(
        lambda *refs: extra_kernel(shares, columns, *refs),
        out_shape=pltpu.HBM((2, features // columns, picked, length), BF16),
        in_specs=[SMEM, VMEM, ANY],
        out_specs=pl.BlockSpec(),
        compiler_params=PARAMS,
        cost_estimate=cost(3),
        name="student_extra",
    )(sources, teacher_parts, message)
    back = lax.all_to_all(message, "x", 0, 0).reshape(length, features + columns + BLOCK)

    held = (student_out, packed, weights, mixed, pick, normed_rows, feat_extra)
    keep, send, loss = pl.pallas_call(
        backward_kernel,
        out_shape=(
            shape((picked, features), BF16), shape((picked, features), BF16), shape((1, 1), F32),
        ),
        in_specs=[VMEM] + [HBM] * len(held),
        out_specs=(VMEM,) * 3,
        scratch_shapes=[pltpu.VMEM(array.shape, array.dtype) for array in held]
        + [pltpu.SemaphoreType.DMA((len(held),))],
        compiler_params=FETCHING,
        cost_estimate=cost(4),
        name="student_backward",
    )(back, *held)

    total = add(keep, lax.ppermute(send, "c", SWAP)).astype(BF16)
    chips = shares // 2
    spread = lax.all_to_all(
        total.reshape(chips, total.shape[0] // chips, features), CLIP[:3], 0, 0
    )
    used = 3 * HEAD * heads
    grad_q, grad_o, grad_p = pl.pallas_call(
        result_kernel,
        out_shape=(
            shape((each, used), F32), shape((each, HEAD * heads), F32), shape((each, columns), F32),
        ),
        in_specs=[VMEM],
        out_specs=(VMEM,) * 3,
        compiler_params=PARAMS,
        cost_estimate=cost(1),
        name="gradient_rows",
    )(spread)
    return loss.reshape(1), grad_q, grad_o.T, grad_p


def solution(mesh):
    group, dp, tensor = mesh.devices.shape
    fine = Mesh(mesh.devices.reshape(group, 4, dp // 8, 2, tensor), (*CLIP, "x"))
    dp = CLIP[1:]
    in_specs = (
        P(CLIP, None, None), P(), P(dp, "x"), P(dp, "x"), P(CLIP, None, None), P(CLIP), P(CLIP, None),
        P(None, "x"), P("x", None), P(None, "x"),
    )
    out_specs = (P(CLIP), P(CLIP, "x"), P("x", CLIP), P(CLIP, "x"))
    return jax.shard_map(
        on_device, mesh=fine, in_specs=in_specs, out_specs=out_specs, check_vma=False
    )
```

```python
import jax
import jax.numpy as jnp
from jax import lax
from jax.experimental import pallas as pl
from jax.experimental.pallas import tpu as pltpu
from jax.sharding import Mesh, PartitionSpec as P

HEAD = 64
BLOCK = 128
F32 = jnp.float32
BF16 = jnp.bfloat16
CLIP = ("g", "y", "z", "c")
ANY = pl.BlockSpec(memory_space=pl.ANY)
HBM = pl.BlockSpec(memory_space=pltpu.HBM)
VMEM = pl.BlockSpec(memory_space=pltpu.VMEM)
SMEM = pl.BlockSpec(memory_space=pltpu.SMEM)
PARAMS = pltpu.CompilerParams(vmem_limit_bytes=20 * 1024 * 1024)


def cost(microseconds):
    return pl.CostEstimate(flops=microseconds * 10**9, bytes_accessed=10**6, transcendentals=0)


def fetch(sources, buffers, sems):
    copies = [
        pltpu.make_async_copy(source, buffer, sems.at[i])
        for i, (source, buffer) in enumerate(zip(sources, buffers))
    ]
    for copy in copies:
        copy.start()
    return copies


def buffers(arrays):
    return [pltpu.VMEM(array.shape, array.dtype) for array in arrays] + [
        pltpu.SemaphoreType.DMA((len(arrays),))
    ]


def in_place(arrays):
    return [pltpu.HBM(array.shape, array.dtype) for array in arrays]


def shape(dims, dtype):
    return jax.ShapeDtypeStruct(dims, dtype)


def nn(a, b):
    return lax.dot_general(a, b, (((1,), (0,)), ((), ())), preferred_element_type=F32)


def nt(a, b):
    return lax.dot_general(a, b, (((1,), (1,)), ((), ())), preferred_element_type=F32)


def tn(a, b):
    return lax.dot_general(a, b, (((0,), (0,)), ((), ())), preferred_element_type=F32)


def norm_rows(rows):
    rows = rows.astype(F32)
    centre = rows - jnp.mean(rows, -1, keepdims=True)
    spread = jnp.mean(centre * centre, -1, keepdims=True)
    return centre * lax.rsqrt(spread + 1e-05)


def split_head(packed, head):
    first = head * 3 * HEAD
    return [packed[:, first + i * HEAD : first + (i + 1) * HEAD].astype(BF16) for i in range(3)]


def softmax(scores):
    top = jnp.max(scores, -1, keepdims=True)
    weights = jnp.exp(scores - top)
    return weights / jnp.sum(weights, -1, keepdims=True)


def pick_rows(rows, shares, columns, core, extra):
    each = rows // shares
    block = each + each * columns // rows
    place = lax.broadcasted_iota(jnp.int32, (shares // 2 * block, 1), 0)
    chip, row = place // block, place % block
    base = (chip * 2 + core) * each
    if extra:
        wanted = jnp.where(row >= each, base + (row - each) * (rows // columns), -1)
    else:
        wanted = jnp.where(row < each, base + row, -1)
    source = lax.broadcasted_iota(jnp.int32, (shares // 2 * block, rows), 1)
    return jnp.where(source == wanted, 1.0, 0.0).astype(BF16)


def student_kernel(
    shares, count_ref, place_ref, events_ref, qkv_ref, out_ref, proj_ref, *refs
):
    ways = len(refs) - 7
    own_ref, peer_refs = refs[0], refs[1:ways]
    normed_ref, packed_ref, mixed_ref, weights_ref, pick_ref, kept_ref, part_ref = refs[ways:]
    kept_ref[...] = out_ref[...]
    columns = proj_ref.shape[1]
    length, features = events_ref.shape
    heads = out_ref.shape[0] // HEAD
    normed = norm_rows(events_ref[...]).astype(BF16)
    for half in range(2):
        core = place_ref[0] if half == 0 else 1 - place_ref[0]
        pick_ref[half] = pick_rows(features, shares, columns, core, False)
        normed_ref[half] = nt(pick_ref[half], normed).astype(BF16)
    packed = nt(normed, qkv_ref[...])
    packed_ref[...] = packed.astype(BF16)
    usable = lax.broadcasted_iota(jnp.int32, (length, length), 1) < count_ref[0]
    mixed = []
    for head in range(heads):
        query, keys, values = split_head(packed, head)
        scores = jnp.where(usable, nt(query, keys) * HEAD ** (-0.5), -1e30)
        weights = softmax(scores)
        weights_ref[head] = weights
        mixed.append(nn(weights.astype(BF16), values))
    mixed = jnp.concatenate(mixed, axis=1).astype(BF16)
    mixed_ref[...] = mixed
    part_ref[...] = nn(mixed, out_ref[...])
    rows = own_ref.shape[0]
    half = features // 2
    blocks = features // columns
    proj_half = proj_ref[pl.ds(pl.multiple_of(place_ref[0] * half, half), half), :]
    for k in range(ways):
        first = pl.multiple_of(place_ref[1 + k] * rows, rows)
        chosen = part_ref[pl.ds(first, rows), :].astype(BF16)
        if k == 0:
            own_ref[...] = chosen
            continue
        for b in range(blocks):
            peer_refs[k - 1][b * rows : (b + 1) * rows] = chosen[:, b * columns : (b + 1) * columns]
        peer_refs[k - 1][blocks * rows :] = proj_half


def rows_kernel(ways, *refs):
    sources, (feat_ref, proj_ref), held = refs[: ways + 1], refs[ways + 1 : ways + 3], refs[-ways - 2 : -1]
    for copy in fetch(sources, held, refs[-1]):
        copy.wait()
    events_ref, own_ref, *peer_refs = held
    rows, features = own_ref.shape
    columns = proj_ref.shape[2]
    for b in range(features // columns):
        block = slice(b * columns, (b + 1) * columns)
        branch = own_ref[:, block].astype(F32)
        for peer in peer_refs:
            branch = branch + peer[b * rows : (b + 1) * rows].astype(F32)
        feat_ref[:, block] = (events_ref[:, block].astype(F32) + branch).astype(BF16)
    for k, peer in enumerate(peer_refs):
        proj_ref[k] = peer[features // columns * rows :]


def teacher_norm_kernel(clip_ref, gain_ref, after_ref, normed_ref):
    normed_ref[...] = (norm_rows(clip_ref[...]) * gain_ref[...]).astype(BF16)


def teacher_kernel(
    place_ref, align_ref, normed_ref, own_ref, other_ref, part_ref, parts_ref, mixed_ref
):
    blocks, cores, rows, width = parts_ref.shape
    for i, piece in enumerate((own_ref, other_ref)):
        core = place_ref[0] if i == 0 else 1 - place_ref[0]
        parts_ref[:, pl.ds(core, 1)] = piece[...].reshape(blocks, 1, rows, width)
    full_ref = parts_ref[...].reshape(blocks * cores * rows, width)
    heads = width // (4 * HEAD)
    packed = nn(normed_ref[...], full_ref[:, : heads * 3 * HEAD])
    mixed = []
    for head in range(heads):
        query, keys, values = split_head(packed, head)
        weights = softmax(nt(query, keys) * HEAD ** (-0.5))
        mixed.append(nn(weights.astype(BF16), values))
    mixed_ref[...] = jnp.concatenate(mixed, axis=1)
    shared = part_ref.shape[1]
    per_block = BLOCK // shared
    for i in range(align_ref.shape[0]):
        first = pl.multiple_of(align_ref[i] * BLOCK, BLOCK)
        chosen = mixed_ref[pl.ds(first, BLOCK), :].astype(BF16)
        part = nt(chosen, full_ref[:, heads * 3 * HEAD :]).astype(BF16)
        for k in range(per_block):
            part_ref[i * per_block + k] = part[k * shared : (k + 1) * shared]


def predict_kernel(
    ways, place_ref, feat_ref, own_ref, mine_ref, other_ref, after_ref, pred_ref, proj_ref
):
    features, columns = own_ref.shape
    half = features // 2
    first = pl.multiple_of(place_ref[0] * half, half)
    second = pl.multiple_of((1 - place_ref[0]) * half, half)
    proj_ref[place_ref[1]] = own_ref[...]
    for k in range(1, ways):
        source = place_ref[1 + k]
        proj_ref[source, pl.ds(first, half), :] = mine_ref[k - 1]
        proj_ref[source, pl.ds(second, half), :] = other_ref[k - 1]
    for k in range(ways):
        pred_ref[:, k * columns : (k + 1) * columns] = nn(feat_ref[...], proj_ref[k])


def extra_kernel(shares, columns, ways, place_ref, *refs):
    sources, (after_ref, extra_ref) = refs[:ways], refs[ways : ways + 2]
    pieces, feat_ref, sems = refs[ways + 2 : -2], refs[-2], refs[-1]
    copies = fetch(sources, pieces, sems)
    rows, features = pieces[0].shape
    for k in range(ways):
        copies[k].wait()
        first = pl.multiple_of(place_ref[1 + k] * rows, rows)
        feat_ref[pl.ds(first, rows), :] = pieces[k][...]
    feat = feat_ref[...]
    shifted = [feat]
    for b in range(1, features // columns):
        shifted.append(jnp.concatenate([feat[:, b:], feat[:, :b]], 1))
    for half in range(2):
        core = place_ref[0] if half == 0 else 1 - place_ref[0]
        pick = pick_rows(features, shares, columns, core, True)
        for b in range(features // columns):
            extra_ref[half, b] = nt(pick, shifted[b]).astype(BF16)


def diff_kernel(
    clips, count_ref, place_ref, parts_ref, tokens_ref, pred_ref, source_ref,
    out_ref, kept_ref, proj_ref, sems,
):
    (copy,) = fetch([source_ref], [proj_ref], sems)
    rows, width = tokens_ref.shape
    ways, features, columns = proj_ref.shape
    branch = parts_ref[0].astype(F32)
    for i in range(1, ways):
        branch = branch + parts_ref[i].astype(F32)
    target = (tokens_ref[...].astype(F32) + branch).astype(BF16).astype(F32)
    count = count_ref[0]
    live = lax.broadcasted_iota(jnp.int32, (rows, 1), 0) + place_ref[1] * rows < count
    scale = jnp.full((1, 1), count, jnp.int32).astype(F32) * width
    factor = 2.0 / (scale * clips)
    diff = jnp.where(live, pred_ref[...] - target, 0.0)
    squares = jnp.sum(diff * diff, -1, keepdims=True) / scale
    dpred = (diff * factor).astype(BF16)
    copy.wait()
    dfeat = jnp.zeros((rows, features), F32)
    for k in range(ways):
        dfeat = dfeat + nt(dpred[:, k * columns : (k + 1) * columns], proj_ref[k])
    dfeat = dfeat.astype(BF16)
    high = squares.astype(BF16)
    rest = squares - high.astype(F32)
    middle = rest.astype(BF16)
    low = (rest - middle.astype(F32)).astype(BF16)
    lane = lax.broadcasted_iota(jnp.int32, (rows, BLOCK), 1)
    tail = jnp.where(lane == 0, high.astype(F32), jnp.where(lane == 1, middle.astype(F32), 0.0))
    tail = jnp.where(lane == 2, low.astype(F32), tail).astype(BF16)
    for i in range(ways):
        out_ref[i, :, :features] = dfeat
        out_ref[i, :, features : features + columns] = dpred[:, i * columns : (i + 1) * columns]
        out_ref[i, :, features + columns :] = tail


def backward_kernel(held, back_ref, *refs):
    sources, (keep_ref, send_ref, loss_ref) = refs[:held], refs[held : held + 3]
    copies = fetch(sources, refs[2 * held + 3 : -1], refs[-1])
    out_ref, packed_ref, weights_ref, mixed_ref, normed_ref, pick_ref, feat_ref = refs[2 * held + 3 : -1]
    copies[0].wait()
    features = out_ref.shape[1]
    heads = out_ref.shape[0] // HEAD
    dfeat = back_ref[:, :features]
    columns = back_ref.shape[1] - features - BLOCK
    dpred = back_ref[:, features : features + columns]
    tail = back_ref[:, features + columns :].astype(F32)
    loss_ref[...] = jnp.sum(jnp.sum(tail, 0, keepdims=True), 1, keepdims=True)
    dmixed = nt(dfeat, out_ref[...])
    for copy in copies[1:3]:
        copy.wait()
    packed = packed_ref[...].astype(F32)
    pieces = []
    for head in range(heads):
        query, keys, values = split_head(packed, head)
        weights = weights_ref[head]
        cot = dmixed[:, head * HEAD : (head + 1) * HEAD].astype(BF16)
        dvalues = tn(weights.astype(BF16), cot)
        dweights = nt(cot, values)
        inner = jnp.sum(dweights * weights, -1, keepdims=True)
        dscores = (weights * (dweights - inner) * HEAD ** (-0.5)).astype(BF16)
        pieces += [nn(dscores, keys), tn(dscores, query), dvalues]
    dpacked = jnp.concatenate(pieces, axis=1)
    used = dpacked.shape[1]
    length = dpacked.shape[0]
    right = jnp.concatenate([dpacked, jnp.zeros((length, features - used), F32)], 1).astype(BF16)
    for copy in copies[3:]:
        copy.wait()
    tailed = features - columns
    mixed = jnp.concatenate(
        [jnp.zeros((length, used - tailed), F32), mixed_ref[...].astype(F32)], 1
    ).astype(BF16)
    for half, into in enumerate((keep_ref, send_ref)):
        dfeat_rows = nt(pick_ref[half], dfeat).astype(BF16)
        normed_rows = normed_ref[half]
        for b in range(features // columns):
            block = slice(b * columns, (b + 1) * columns)
            total = nn(normed_rows, right[:, block]) + nn(feat_ref[half, b], dpred)
            if b == features // columns - 1:
                total = total + nn(dfeat_rows, mixed)
            into[:, block] = total.astype(BF16)


SWAP = [(0, 1), (1, 0)]


def from_peers(rows, axis):
    ways = lax.axis_size(axis)
    return [
        lax.ppermute(rows(k), axis, [(i, (i + k) % ways) for i in range(ways)])
        for k in range(1, ways)
    ]


def add(a, b):
    return a.astype(F32) + b.astype(F32)


def result_kernel(parts_ref, q_ref, o_ref, p_ref):
    each, used = q_ref.shape
    columns = p_ref.shape[1]
    total = jnp.sum(parts_ref[...].astype(F32), 0)
    q_ref[...] = total[:each, :used]
    o_ref[...] = total[:each, used:]
    for i in range(total.shape[0] - each):
        for b in range(total.shape[1] // columns):
            row = i * (total.shape[1] // columns) + b
            p_ref[row : row + 1] = total[each + i : each + i + 1, b * columns : (b + 1) * columns]


def on_device(
    teacher_clips, teacher_gain, teacher_qkv, teacher_out_t, event_tokens, valid_counts, alignment,
    student_qkv, student_out, projector,
):
    clip, events, align = teacher_clips[0], event_tokens[0], alignment[0]
    length, width = clip.shape
    features = events.shape[1]
    columns = projector.shape[1]
    ways = lax.axis_size("x")
    rows = length // ways
    own_c, own_x = lax.axis_index("c"), lax.axis_index("x")
    shares = 1
    for axis in CLIP:
        shares = shares * lax.axis_size(axis)

    senders = lax.axis_size("y") * lax.axis_size("z")
    shard = jnp.concatenate([teacher_qkv, teacher_out_t], 1)
    shard = jnp.broadcast_to(shard[None], (senders, *shard.shape))
    own_core = lax.all_to_all(shard, ("y", "z"), 0, 0)
    heads = student_out.shape[0] // HEAD
    each = features // shares
    picked = shares // 2 * (each + each * columns // features)
    places = jnp.stack([own_c] + [(own_x + k) % ways for k in range(ways)]).astype(jnp.int32)
    message_rows = rows * features // columns + features // 2
    outs = pl.pallas_call(
        lambda *refs: student_kernel(shares, *refs),
        out_shape=(
            pltpu.HBM((rows, features), BF16),
            *[shape((message_rows, columns), BF16)] * (ways - 1),
            pltpu.HBM((2, picked, length), BF16),
            pltpu.HBM((length, 3 * HEAD * heads), BF16),
            pltpu.HBM((length, HEAD * heads), BF16),
            pltpu.HBM((heads, length, length), F32),
            pltpu.HBM((2, picked, features), BF16),
            *in_place([student_out]),
        ),
        in_specs=[SMEM] * 2 + [VMEM] * 4,
        out_specs=(pl.BlockSpec(),) + (VMEM,) * (ways - 1) + (pl.BlockSpec(),) * 6,
        scratch_shapes=[pltpu.VMEM((length, features), F32)],
        compiler_params=PARAMS,
        cost_estimate=cost(4),
        name="student_forward",
    )(valid_counts, places, events, student_qkv.T, student_out, projector)
    own_part, peer_parts = outs[0], outs[1:ways]
    normed_rows, packed, mixed, weights, pick, kept_out = outs[ways:]

    received = from_peers(lambda k: peer_parts[k - 1], "x")
    own_events = lax.dynamic_slice_in_dim(events, own_x * rows, rows, 0)
    feat_rows, proj_halves = pl.pallas_call(
        lambda *refs: rows_kernel(ways, *refs),
        out_shape=(
            shape((rows, features), BF16), shape((ways - 1, features // 2, columns), BF16),
            *in_place(received),
        ),
        in_specs=[ANY] * 2 + [HBM] * (ways - 1),
        out_specs=(VMEM,) * 2 + (HBM,) * (ways - 1),
        input_output_aliases={2 + k: 2 + k for k in range(ways - 1)},
        scratch_shapes=buffers((own_events, own_part, *received)),
        compiler_params=PARAMS,
        cost_estimate=cost(1),
        name="student_rows",
    )(own_events, own_part, *received)[:2]
    own_core, feat_rows, proj_halves = lax.optimization_barrier((own_core, feat_rows, proj_halves))
    other_core = lax.ppermute(own_core, "c", SWAP)
    proj_others = lax.ppermute(proj_halves, "c", SWAP)
    teacher_normed = pl.pallas_call(
        teacher_norm_kernel,
        out_shape=shape((length, width), BF16),
        in_specs=[VMEM] * 2 + [ANY],
        out_specs=VMEM,
        compiler_params=PARAMS,
        cost_estimate=cost(1),
        name="teacher_norm",
    )(clip, teacher_gain.reshape(1, width), feat_rows)

    teacher_part = pl.pallas_call(
        teacher_kernel,
        out_shape=shape((ways, rows, width), BF16),
        in_specs=[SMEM] * 2 + [VMEM] * 3,
        out_specs=VMEM,
        scratch_shapes=[
            pltpu.VMEM((senders, 2, *shard.shape[1:]), BF16),
            pltpu.VMEM((length, teacher_out_t.shape[1]), F32),
        ],
        compiler_params=PARAMS,
        cost_estimate=cost(5),
        name="teacher",
    )(places, align, teacher_normed, own_core, other_core)

    teacher_parts = lax.all_to_all(teacher_part, "x", 0, 0)
    after_teacher, _ = lax.optimization_barrier((feat_rows, teacher_part))
    feats = [feat_rows] + from_peers(lambda k: after_teacher, "x")
    per_block = BLOCK // rows
    source = align[own_x // per_block] * BLOCK + own_x % per_block * rows
    own_tokens = lax.dynamic_slice_in_dim(clip, source, rows, 0)
    sources = jnp.stack([own_c] + [(own_x - k + ways) % ways for k in range(ways)]).astype(jnp.int32)
    pred, whole_proj = pl.pallas_call(
        lambda *refs: predict_kernel(ways, *refs),
        out_shape=(shape((rows, width), F32), pltpu.HBM((ways, features, columns), BF16)),
        in_specs=[SMEM] + [VMEM] * 4 + [ANY],
        out_specs=(VMEM, pl.BlockSpec()),
        compiler_params=PARAMS,
        cost_estimate=cost(2),
        name="student_predict",
    )(sources, feat_rows, projector, proj_halves, proj_others, teacher_part)
    pred, feats[1], feats[-1] = lax.optimization_barrier((pred, feats[1], feats[-1]))
    message, _ = pl.pallas_call(
        lambda *refs: diff_kernel(shares, *refs),
        out_shape=(
            shape((ways, rows, features + columns + BLOCK), BF16), *in_place([whole_proj]),
        ),
        in_specs=[SMEM] * 2 + [VMEM] * 3 + [HBM],
        out_specs=(VMEM, HBM),
        scratch_shapes=buffers([whole_proj]),
        input_output_aliases={5: 1},
        compiler_params=PARAMS,
        cost_estimate=cost(2),
        name="difference",
    )(valid_counts, sources, teacher_parts, own_tokens, pred, whole_proj)
    feat_extra = pl.pallas_call(
        lambda *refs: extra_kernel(shares, columns, ways, *refs),
        out_shape=pltpu.HBM((2, features // columns, picked, length), BF16),
        in_specs=[SMEM] + [ANY] * (ways + 1),
        out_specs=pl.BlockSpec(),
        scratch_shapes=buffers(feats)[:-1]
        + [pltpu.VMEM((length, features), BF16), buffers(feats)[-1]],
        compiler_params=PARAMS,
        cost_estimate=cost(3),
        name="student_extra",
    )(sources, *feats, message)
    back = lax.all_to_all(message, "x", 0, 0).reshape(length, features + columns + BLOCK)

    held = (kept_out, packed, weights, mixed, normed_rows, pick, feat_extra)
    keep, send, loss = pl.pallas_call(
        lambda *refs: backward_kernel(len(held), *refs),
        out_shape=(
            shape((picked, features), BF16), shape((picked, features), BF16), shape((1, 1), F32),
            *in_place(held),
        ),
        in_specs=[VMEM] + [HBM] * len(held),
        out_specs=(VMEM,) * 3 + (HBM,) * len(held),
        scratch_shapes=buffers(held),
        input_output_aliases={1 + i: 3 + i for i in range(len(held))},
        compiler_params=PARAMS,
        cost_estimate=cost(4),
        name="student_backward",
    )(back, *held)[:3]

    total = add(keep, lax.ppermute(send, "c", SWAP)).astype(BF16)
    chips = shares // 2
    spread = lax.all_to_all(
        total.reshape(chips, total.shape[0] // chips, features), CLIP[:3], 0, 0
    )
    used = 3 * HEAD * heads
    grad_q, grad_o, grad_p = pl.pallas_call(
        result_kernel,
        out_shape=(
            shape((each, used), F32), shape((each, HEAD * heads), F32), shape((each, columns), F32),
        ),
        in_specs=[VMEM],
        out_specs=(VMEM,) * 3,
        compiler_params=PARAMS,
        cost_estimate=cost(1),
        name="gradient_rows",
    )(spread)
    return loss.reshape(1), grad_q, grad_o.T, grad_p


def solution(mesh):
    group, dp, tensor = mesh.devices.shape
    fine = Mesh(mesh.devices.reshape(group, 4, dp // 8, 2, tensor), (*CLIP, "x"))
    dp = CLIP[1:]
    in_specs = (
        P(CLIP, None, None), P(), P(dp, "x"), P(dp, "x"), P(CLIP, None, None), P(CLIP), P(CLIP, None),
        P(None, "x"), P("x", None), P(None, "x"),
    )
    out_specs = (P(CLIP), P(CLIP, "x"), P("x", CLIP), P(CLIP, "x"))
    return jax.shard_map(
        on_device, mesh=fine, in_specs=in_specs, out_specs=out_specs, check_vma=False
    )
```

```python
import jax
import jax.numpy as jnp
from jax import lax
from jax.experimental import pallas as pl
from jax.experimental.pallas import tpu as pltpu
from jax.sharding import Mesh, PartitionSpec as P

HEAD = 64
BLOCK = 128
F32 = jnp.float32
BF16 = jnp.bfloat16
CLIP = ("g", "y", "z", "c")
ANY = pl.BlockSpec(memory_space=pl.ANY)
HBM = pl.BlockSpec(memory_space=pltpu.HBM)
VMEM = pl.BlockSpec(memory_space=pltpu.VMEM)
SMEM = pl.BlockSpec(memory_space=pltpu.SMEM)
PARAMS = pltpu.CompilerParams(vmem_limit_bytes=20 * 1024 * 1024)


def cost(microseconds):
    return pl.CostEstimate(flops=microseconds * 10**9, bytes_accessed=10**6, transcendentals=0)


def fetch(sources, buffers, sems):
    copies = [
        pltpu.make_async_copy(source, buffer, sems.at[i])
        for i, (source, buffer) in enumerate(zip(sources, buffers))
    ]
    for copy in copies:
        copy.start()
    return copies


def buffers(arrays):
    return [pltpu.VMEM(array.shape, array.dtype) for array in arrays] + [
        pltpu.SemaphoreType.DMA((len(arrays),))
    ]


def in_place(arrays):
    return [pltpu.HBM(array.shape, array.dtype) for array in arrays]


def shape(dims, dtype):
    return jax.ShapeDtypeStruct(dims, dtype)


def nn(a, b):
    return lax.dot_general(a, b, (((1,), (0,)), ((), ())), preferred_element_type=F32)


def nt(a, b):
    return lax.dot_general(a, b, (((1,), (1,)), ((), ())), preferred_element_type=F32)


def tn(a, b):
    return lax.dot_general(a, b, (((0,), (0,)), ((), ())), preferred_element_type=F32)


def norm_rows(rows):
    rows = rows.astype(F32)
    centre = rows - jnp.mean(rows, -1, keepdims=True)
    spread = jnp.mean(centre * centre, -1, keepdims=True)
    return centre * lax.rsqrt(spread + 1e-05)


def split_head(packed, head):
    first = head * 3 * HEAD
    return [packed[:, first + i * HEAD : first + (i + 1) * HEAD].astype(BF16) for i in range(3)]


def softmax(scores):
    top = jnp.max(scores, -1, keepdims=True)
    weights = jnp.exp(scores - top)
    return weights / jnp.sum(weights, -1, keepdims=True)


def pick_matrix(wanted, width):
    source = lax.broadcasted_iota(jnp.int32, (wanted.shape[0], width), 1)
    return jnp.where(source == wanted, 1.0, 0.0).astype(BF16)


def pick_rows(rows, shares, block, core):
    each = rows // shares
    place = lax.broadcasted_iota(jnp.int32, (shares // 2 * block, 1), 0)
    chip, row = place // block, place % block
    return pick_matrix(jnp.where(row < each, (chip * 2 + core) * each + row, -1), rows)


def pick_extra(rows, shares, extra, core):
    each = rows // shares
    place = lax.broadcasted_iota(jnp.int32, (shares // 2 * extra, 1), 0)
    chip, row = place // extra, place % extra
    return pick_matrix((chip * 2 + core) * each + row * (each // extra), rows)


def spread_extra(shares, block, extra):
    place = lax.broadcasted_iota(jnp.int32, (shares // 2 * block, 1), 0)
    chip, row = place // block, place % block
    kept = block - extra
    return pick_matrix(jnp.where(row >= kept, chip * extra + row - kept, -1), shares // 2 * extra)


def picks_kernel(shares, place_ref, normed_ref, after_ref, rows_ref, pick_ref):
    features = pick_ref.shape[2]
    block = pick_ref.shape[1] // (shares // 2)
    for half in range(2):
        core = place_ref[0] if half == 0 else 1 - place_ref[0]
        pick_ref[half] = pick_rows(features, shares, block, core)
        rows_ref[half] = nt(pick_ref[half], normed_ref[...]).astype(BF16)


def student_kernel(count_ref, place_ref, events_ref, qkv_ref, out_ref, *refs):
    ways = len(refs) - 6
    part_refs = refs[:ways]
    normed_ref, packed_ref, mixed_ref, weights_ref, kept_ref, part_ref = refs[ways:]
    length, features = events_ref.shape
    heads = out_ref.shape[0] // HEAD
    kept_ref[...] = out_ref[...]
    normed = norm_rows(events_ref[...]).astype(BF16)
    normed_ref[...] = normed
    packed = nt(normed, qkv_ref[...])
    packed_ref[...] = packed.astype(BF16)
    usable = lax.broadcasted_iota(jnp.int32, (length, length), 1) < count_ref[0]
    mixed = []
    for head in range(heads):
        query, keys, values = split_head(packed, head)
        scores = jnp.where(usable, nt(query, keys) * HEAD ** (-0.5), -1e30)
        weights = softmax(scores).astype(BF16)
        weights_ref[head] = weights
        mixed.append(nn(weights, values))
    mixed = jnp.concatenate(mixed, axis=1).astype(BF16)
    mixed_ref[...] = mixed
    part_ref[...] = nn(mixed, out_ref[...])
    rows = part_refs[0].shape[0]
    for k in range(ways):
        first = pl.multiple_of(place_ref[1 + k] * rows, rows)
        part_refs[k][...] = part_ref[pl.ds(first, rows), :].astype(BF16)


def teacher_norm_kernel(clip_ref, gain_ref, after_ref, normed_ref):
    normed_ref[...] = (norm_rows(clip_ref[...]) * gain_ref[...]).astype(BF16)


def teacher_kernel(
    place_ref, align_ref, normed_ref, own_ref, other_ref, part_ref, parts_ref, mixed_ref
):
    blocks, cores, rows, width = parts_ref.shape
    for i, piece in enumerate((own_ref, other_ref)):
        core = place_ref[0] if i == 0 else 1 - place_ref[0]
        parts_ref[:, pl.ds(core, 1)] = piece[...].reshape(blocks, 1, rows, width)
    full_ref = parts_ref[...].reshape(blocks * cores * rows, width)
    heads = width // (4 * HEAD)
    packed = nn(normed_ref[...], full_ref[:, : heads * 3 * HEAD])
    mixed = []
    for head in range(heads):
        query, keys, values = split_head(packed, head)
        weights = softmax(nt(query, keys) * HEAD ** (-0.5))
        mixed.append(nn(weights.astype(BF16), values))
    mixed_ref[...] = jnp.concatenate(mixed, axis=1)
    shared = part_ref.shape[1]
    per_block = BLOCK // shared
    for i in range(align_ref.shape[0]):
        first = pl.multiple_of(align_ref[i] * BLOCK, BLOCK)
        chosen = mixed_ref[pl.ds(first, BLOCK), :].astype(BF16)
        part = nt(chosen, full_ref[:, heads * 3 * HEAD :]).astype(BF16)
        for k in range(per_block):
            part_ref[i * per_block + k] = part[k * shared : (k + 1) * shared]


def predict_kernel(
    ways, place_ref, feat_ref, own_ref, near_ref, near_other_ref, far_ref, far_other_ref, after_ref,
    pred_ref, proj_ref,
):
    columns = own_ref.shape[1]
    half = far_ref.shape[0]
    core = place_ref[0]
    first = pl.multiple_of(core * half, half)
    second = pl.multiple_of((1 - core) * half, half)
    proj_ref[place_ref[1]] = own_ref[...]
    before, opposite, behind = place_ref[2], place_ref[3], place_ref[4]
    proj_ref[jnp.where(core == 0, behind, before)] = near_ref[...]
    proj_ref[jnp.where(core == 0, before, behind)] = near_other_ref[...]
    proj_ref[opposite, pl.ds(first, half), :] = far_ref[...]
    proj_ref[opposite, pl.ds(second, half), :] = far_other_ref[...]
    for k in range(ways):
        pred_ref[:, k * columns : (k + 1) * columns] = nn(feat_ref[...], proj_ref[k])


def extra_kernel(shares, ways, place_ref, *refs):
    sources, (after_ref, extra_ref) = refs[:ways], refs[ways : ways + 2]
    pieces, feat_ref, sems = refs[ways + 2 : -2], refs[-2], refs[-1]
    copies = fetch(sources, pieces, sems)
    rows, features = pieces[0].shape
    for k in range(ways):
        copies[k].wait()
        first = pl.multiple_of(place_ref[1 + k] * rows, rows)
        feat_ref[pl.ds(first, rows), :] = pieces[k][...]
    feat = feat_ref[...]
    blocks, runs = extra_ref.shape[1:3]
    for b in range(blocks):
        shifted = feat if b == 0 else jnp.concatenate([feat[:, b:], feat[:, :b]], 1)
        for half in range(2):
            core = place_ref[0] if half == 0 else 1 - place_ref[0]
            pick = pick_extra(features, shares, 2 * runs // shares, core)
            extra_ref[half, b] = nt(pick, shifted).astype(BF16)


def diff_kernel(
    clips, count_ref, place_ref, parts_ref, tokens_ref, pred_ref, source_ref,
    out_ref, kept_ref, proj_ref, sems,
):
    blocks = range(proj_ref.shape[0])
    copies = fetch([source_ref.at[k] for k in blocks], [proj_ref.at[k] for k in blocks], sems)
    rows, width = tokens_ref.shape
    ways, features, columns = proj_ref.shape
    branch = parts_ref[0].astype(F32)
    for i in range(1, ways):
        branch = branch + parts_ref[i].astype(F32)
    target = (tokens_ref[...].astype(F32) + branch).astype(BF16).astype(F32)
    count = count_ref[0]
    live = lax.broadcasted_iota(jnp.int32, (rows, 1), 0) + place_ref[1] * rows < count
    scale = jnp.full((1, 1), count, jnp.int32).astype(F32) * width
    factor = 2.0 / (scale * clips)
    diff = jnp.where(live, pred_ref[...] - target, 0.0)
    squares = jnp.sum(diff * diff, -1, keepdims=True) / scale
    dpred = (diff * factor).astype(BF16)
    dfeat = jnp.zeros((rows, features), F32)
    for k in range(ways):
        copies[k].wait()
        dfeat = dfeat + nt(dpred[:, k * columns : (k + 1) * columns], proj_ref[k])
    dfeat = dfeat.astype(BF16)
    high = squares.astype(BF16)
    rest = squares - high.astype(F32)
    middle = rest.astype(BF16)
    low = (rest - middle.astype(F32)).astype(BF16)
    lane = lax.broadcasted_iota(jnp.int32, (rows, BLOCK), 1)
    tail = jnp.where(lane == 0, high.astype(F32), jnp.where(lane == 1, middle.astype(F32), 0.0))
    tail = jnp.where(lane == 2, low.astype(F32), tail).astype(BF16)
    for i in range(ways):
        out_ref[i, :, :features] = dfeat
        out_ref[i, :, features : features + columns] = dpred[:, i * columns : (i + 1) * columns]
        out_ref[i, :, features + columns :] = tail


def backward_kernel(shares, held, back_ref, *refs):
    sources, (keep_ref, send_ref, loss_ref) = refs[:held], refs[held : held + 3]
    copies = fetch(sources, refs[2 * held + 3 : -1], refs[-1])
    out_ref, packed_ref, weights_ref, pick_ref, mixed_ref, normed_ref, feat_ref = refs[2 * held + 3 : -1]
    copies[0].wait()
    features = out_ref.shape[1]
    heads = out_ref.shape[0] // HEAD
    dfeat = back_ref[:, :features]
    columns = back_ref.shape[1] - features - BLOCK
    dpred = back_ref[:, features : features + columns]
    tail = back_ref[:, features + columns :].astype(F32)
    loss_ref[...] = jnp.sum(jnp.sum(tail, 0, keepdims=True), 1, keepdims=True)
    dmixed = nt(dfeat, out_ref[...])
    for copy in copies[1:3]:
        copy.wait()
    packed = packed_ref[...].astype(F32)
    pieces = []
    for head in range(heads):
        query, keys, values = split_head(packed, head)
        rounded = weights_ref[head]
        weights = rounded.astype(F32)
        cot = dmixed[:, head * HEAD : (head + 1) * HEAD].astype(BF16)
        dvalues = tn(rounded, cot)
        dweights = nt(cot, values)
        inner = jnp.sum(dweights * weights, -1, keepdims=True)
        dscores = (weights * (dweights - inner) * HEAD ** (-0.5)).astype(BF16)
        pieces += [nn(dscores, keys), tn(dscores, query), dvalues]
    dpacked = jnp.concatenate(pieces, axis=1)
    used = dpacked.shape[1]
    length = dpacked.shape[0]
    right = jnp.concatenate([dpacked, jnp.zeros((length, features - used), F32)], 1).astype(BF16)
    for copy in copies[3:]:
        copy.wait()
    tailed = features - columns
    mixed = jnp.concatenate(
        [jnp.zeros((length, used - tailed), F32), mixed_ref[...].astype(F32)], 1
    ).astype(BF16)
    block, extra = pick_ref.shape[1] * 2 // shares, feat_ref.shape[2] * 2 // shares
    placed = spread_extra(shares, block, extra)
    for half, into in enumerate((keep_ref, send_ref)):
        dfeat_rows = nt(pick_ref[half], dfeat).astype(BF16)
        normed_rows = normed_ref[half]
        for b in range(features // columns):
            lanes = slice(b * columns, (b + 1) * columns)
            runs = nn(feat_ref[half, b], dpred).astype(BF16)
            total = nn(normed_rows, right[:, lanes]) + nn(placed, runs)
            if b == features // columns - 1:
                total = total + nn(dfeat_rows, mixed)
            into[:, lanes] = total.astype(BF16)


SWAP = [(0, 1), (1, 0)]


def from_peers(rows, axis, places=None):
    ways = lax.axis_size(axis)
    return [
        lax.ppermute(rows(k), axis, [(i, (i + k) % ways) for i in range(ways)])
        for k in (range(1, ways) if places is None else places)
    ]


def add(a, b):
    return a.astype(F32) + b.astype(F32)


def result_kernel(parts_ref, q_ref, o_ref, p_ref):
    each, used = q_ref.shape
    columns = p_ref.shape[1]
    total = jnp.sum(parts_ref[...].astype(F32), 0)
    q_ref[...] = total[:each, :used]
    o_ref[...] = total[:each, used:]
    for i in range(total.shape[0] - each):
        for b in range(total.shape[1] // columns):
            row = i * (total.shape[1] // columns) + b
            p_ref[row : row + 1] = total[each + i : each + i + 1, b * columns : (b + 1) * columns]


def on_device(
    teacher_clips, teacher_gain, teacher_qkv, teacher_out_t, event_tokens, valid_counts, alignment,
    student_qkv, student_out, projector,
):
    clip, events, align = teacher_clips[0], event_tokens[0], alignment[0]
    length, width = clip.shape
    features = events.shape[1]
    columns = projector.shape[1]
    ways = lax.axis_size("x")
    rows = length // ways
    own_c, own_x = lax.axis_index("c"), lax.axis_index("x")
    shares = 1
    for axis in CLIP:
        shares = shares * lax.axis_size(axis)

    senders = lax.axis_size("y") * lax.axis_size("z")
    shard = jnp.concatenate([teacher_qkv, teacher_out_t], 1)
    shard = jnp.broadcast_to(shard[None], (senders, *shard.shape))
    own_core = lax.all_to_all(shard, ("y", "z"), 0, 0)
    heads = student_out.shape[0] // HEAD
    each = features // shares
    picked = shares // 2 * (each + each * columns // features)
    places = jnp.stack([own_c] + [(own_x + k) % ways for k in range(ways)]).astype(jnp.int32)
    outs = pl.pallas_call(
        student_kernel,
        out_shape=(
            pltpu.HBM((rows, features), BF16),
            *[shape((rows, features), BF16)] * (ways - 1),
            shape((length, features), BF16),
            pltpu.HBM((length, 3 * HEAD * heads), BF16),
            pltpu.HBM((length, HEAD * heads), BF16),
            pltpu.HBM((heads, length, length), BF16),
            *in_place([student_out]),
        ),
        in_specs=[SMEM] * 2 + [VMEM] * 3,
        out_specs=(pl.BlockSpec(),) + (VMEM,) * ways + (pl.BlockSpec(),) * 4,
        scratch_shapes=[pltpu.VMEM((length, features), F32)],
        compiler_params=PARAMS,
        cost_estimate=cost(4),
        name="student_forward",
    )(valid_counts, places, events, student_qkv.T, student_out)
    own_part, peer_parts = outs[0], outs[1:ways]
    normed, packed, mixed, weights, kept_out = outs[ways:]

    received = from_peers(lambda k: peer_parts[k - 1], "x")
    own_events = lax.dynamic_slice_in_dim(events, own_x * rows, rows, 0)
    feat_rows = own_events.astype(F32) + own_part.astype(F32)
    for other in received:
        feat_rows = feat_rows + other.astype(F32)
    feat_rows = feat_rows.astype(BF16)
    one_on = [
        (c * ways + x, c * ways + (x + (1 if c else -1)) % ways) for x in range(ways) for c in range(2)
    ]
    near = lax.ppermute(projector, ("c", "x"), one_on)
    picked_rows, pick = pl.pallas_call(
        lambda *refs: picks_kernel(shares, *refs),
        out_shape=(
            pltpu.HBM((2, picked, length), BF16), pltpu.HBM((2, picked, features), BF16),
        ),
        in_specs=[SMEM, VMEM, ANY],
        out_specs=(pl.BlockSpec(),) * 2,
        compiler_params=PARAMS,
        cost_estimate=cost(2),
        name="student_picks",
    )(places, normed, near)
    feats = [feat_rows] + from_peers(lambda k: feat_rows, "x", (1, ways - 1))
    own_core, feat_rows, near, feats, picked_rows = lax.optimization_barrier(
        (own_core, feat_rows, near, feats, picked_rows)
    )
    other_core = lax.ppermute(own_core, "c", SWAP)
    half = features // 2
    far = lax.ppermute(lax.dynamic_slice_in_dim(near, own_c * half, half, 0), ("c", "x"), one_on)
    near_other, far_other = (lax.ppermute(array, "c", SWAP) for array in (near, far))
    teacher_normed = pl.pallas_call(
        teacher_norm_kernel,
        out_shape=shape((length, width), BF16),
        in_specs=[VMEM] * 2 + [ANY],
        out_specs=VMEM,
        compiler_params=PARAMS,
        cost_estimate=cost(1),
        name="teacher_norm",
    )(clip, teacher_gain.reshape(1, width), feat_rows)

    teacher_part = pl.pallas_call(
        teacher_kernel,
        out_shape=shape((ways, rows, width), BF16),
        in_specs=[SMEM] * 2 + [VMEM] * 3,
        out_specs=VMEM,
        scratch_shapes=[
            pltpu.VMEM((senders, 2, *shard.shape[1:]), BF16),
            pltpu.VMEM((length, teacher_out_t.shape[1]), F32),
        ],
        compiler_params=PARAMS,
        cost_estimate=cost(5),
        name="teacher",
    )(places, align, teacher_normed, own_core, other_core)

    teacher_parts = lax.all_to_all(teacher_part, "x", 0, 0)
    after_teacher, _ = lax.optimization_barrier((feat_rows, teacher_part))
    feats[2:-1] = from_peers(lambda k: after_teacher, "x", range(2, ways - 1))
    per_block = BLOCK // rows
    source = align[own_x // per_block] * BLOCK + own_x % per_block * rows
    own_tokens = lax.dynamic_slice_in_dim(clip, source, rows, 0)
    sources = jnp.stack([own_c] + [(own_x - k + ways) % ways for k in range(ways)]).astype(jnp.int32)
    pred, whole_proj = pl.pallas_call(
        lambda *refs: predict_kernel(ways, *refs),
        out_shape=(shape((rows, width), F32), pltpu.HBM((ways, features, columns), BF16)),
        in_specs=[SMEM] + [VMEM] * 6 + [ANY],
        out_specs=(VMEM, pl.BlockSpec()),
        compiler_params=PARAMS,
        cost_estimate=cost(2),
        name="student_predict",
    )(sources, feat_rows, projector, near, near_other, far, far_other, teacher_part)
    pred, feats = lax.optimization_barrier((pred, feats))
    message, _ = pl.pallas_call(
        lambda *refs: diff_kernel(shares, *refs),
        out_shape=(
            shape((ways, rows, features + columns + BLOCK), BF16), *in_place([whole_proj]),
        ),
        in_specs=[SMEM] * 2 + [VMEM] * 3 + [HBM],
        out_specs=(VMEM, HBM),
        scratch_shapes=[
            pltpu.VMEM(whole_proj.shape, BF16), pltpu.SemaphoreType.DMA((ways,)),
        ],
        input_output_aliases={5: 1},
        compiler_params=PARAMS,
        cost_estimate=cost(2),
        name="difference",
    )(valid_counts, sources, teacher_parts, own_tokens, pred, whole_proj)
    feat_extra = pl.pallas_call(
        lambda *refs: extra_kernel(shares, ways, *refs),
        out_shape=pltpu.HBM((2, features // columns, picked - shares // 2 * each, length), BF16),
        in_specs=[SMEM] + [ANY] * (ways + 1),
        out_specs=pl.BlockSpec(),
        scratch_shapes=buffers(feats)[:-1]
        + [pltpu.VMEM((length, features), BF16), buffers(feats)[-1]],
        compiler_params=PARAMS,
        cost_estimate=cost(3),
        name="student_extra",
    )(sources, *feats, message)
    back = lax.all_to_all(message, "x", 0, 0).reshape(length, features + columns + BLOCK)

    held = (kept_out, packed, weights, pick, mixed, picked_rows, feat_extra)
    keep, send, loss = pl.pallas_call(
        lambda *refs: backward_kernel(shares, len(held), *refs),
        out_shape=(
            shape((picked, features), BF16), shape((picked, features), BF16), shape((1, 1), F32),
            *in_place(held),
        ),
        in_specs=[VMEM] + [HBM] * len(held),
        out_specs=(VMEM,) * 3 + (HBM,) * len(held),
        scratch_shapes=buffers(held),
        input_output_aliases={1 + i: 3 + i for i in range(len(held))},
        compiler_params=PARAMS,
        cost_estimate=cost(4),
        name="student_backward",
    )(back, *held)[:3]

    total = add(keep, lax.ppermute(send, "c", SWAP)).astype(BF16)
    chips = shares // 2
    spread = lax.all_to_all(
        total.reshape(chips, total.shape[0] // chips, features), CLIP[:3], 0, 0
    )
    used = 3 * HEAD * heads
    grad_q, grad_o, grad_p = pl.pallas_call(
        result_kernel,
        out_shape=(
            shape((each, used), F32), shape((each, HEAD * heads), F32), shape((each, columns), F32),
        ),
        in_specs=[VMEM],
        out_specs=(VMEM,) * 3,
        compiler_params=PARAMS,
        cost_estimate=cost(1),
        name="gradient_rows",
    )(spread)
    return loss.reshape(1), grad_q, grad_o.T, grad_p


def solution(mesh):
    group, dp, tensor = mesh.devices.shape
    fine = Mesh(mesh.devices.reshape(group, 4, dp // 8, 2, tensor), (*CLIP, "x"))
    dp = CLIP[1:]
    in_specs = (
        P(CLIP, None, None), P(), P(dp, "x"), P(dp, "x"), P(CLIP, None, None), P(CLIP), P(CLIP, None),
        P(None, "x"), P("x", None), P(None, "x"),
    )
    out_specs = (P(CLIP), P(CLIP, "x"), P("x", CLIP), P(CLIP, "x"))
    return jax.shard_map(
        on_device, mesh=fine, in_specs=in_specs, out_specs=out_specs, check_vma=False
    )
```

```python
import jax
import jax.numpy as jnp
from jax import lax
from jax.experimental import pallas as pl
from jax.experimental.pallas import tpu as pltpu
from jax.sharding import Mesh, PartitionSpec as P

HEAD = 64
BLOCK = 128
F32 = jnp.float32
BF16 = jnp.bfloat16
CLIP = ("g", "y", "z", "c")
ANY = pl.BlockSpec(memory_space=pl.ANY)
HBM = pl.BlockSpec(memory_space=pltpu.HBM)
VMEM = pl.BlockSpec(memory_space=pltpu.VMEM)
SMEM = pl.BlockSpec(memory_space=pltpu.SMEM)
PARAMS = pltpu.CompilerParams(vmem_limit_bytes=20 * 1024 * 1024)


def cost(microseconds):
    return pl.CostEstimate(flops=microseconds * 10**9, bytes_accessed=10**6, transcendentals=0)


def fetch(sources, buffers, sems):
    copies = [
        pltpu.make_async_copy(source, buffer, sems.at[i])
        for i, (source, buffer) in enumerate(zip(sources, buffers))
    ]
    for copy in copies:
        copy.start()
    return copies


def buffers(arrays):
    return [pltpu.VMEM(array.shape, array.dtype) for array in arrays] + [
        pltpu.SemaphoreType.DMA((len(arrays),))
    ]


def in_place(arrays):
    return [pltpu.HBM(array.shape, array.dtype) for array in arrays]


def shape(dims, dtype):
    return jax.ShapeDtypeStruct(dims, dtype)


def nn(a, b):
    return lax.dot_general(a, b, (((1,), (0,)), ((), ())), preferred_element_type=F32)


def nt(a, b):
    return lax.dot_general(a, b, (((1,), (1,)), ((), ())), preferred_element_type=F32)


def tn(a, b):
    return lax.dot_general(a, b, (((0,), (0,)), ((), ())), preferred_element_type=F32)


def norm_rows(rows):
    rows = rows.astype(F32)
    centre = rows - jnp.mean(rows, -1, keepdims=True)
    spread = jnp.mean(centre * centre, -1, keepdims=True)
    return centre * lax.rsqrt(spread + 1e-05)


def split_head(packed, head):
    first = head * 3 * HEAD
    return [packed[:, first + i * HEAD : first + (i + 1) * HEAD].astype(BF16) for i in range(3)]


def softmax(scores):
    top = jnp.max(scores, -1, keepdims=True)
    weights = jnp.exp(scores - top)
    return weights / jnp.sum(weights, -1, keepdims=True)


def pick_rows(rows, shares, columns, core, extra):
    each = rows // shares
    block = each + each * columns // rows
    place = lax.broadcasted_iota(jnp.int32, (shares // 2 * block, 1), 0)
    chip, row = place // block, place % block
    base = (chip * 2 + core) * each
    if extra:
        wanted = jnp.where(row >= each, base + (row - each) * (rows // columns), -1)
    else:
        wanted = jnp.where(row < each, base + row, -1)
    source = lax.broadcasted_iota(jnp.int32, (shares // 2 * block, rows), 1)
    return jnp.where(source == wanted, 1.0, 0.0).astype(BF16)


def student_kernel(
    shares, count_ref, place_ref, events_ref, qkv_ref, out_ref, proj_ref, *refs
):
    ways = len(refs) - 7
    own_ref, peer_refs = refs[0], refs[1:ways]
    normed_ref, packed_ref, mixed_ref, weights_ref, pick_ref, kept_ref, part_ref = refs[ways:]
    kept_ref[...] = out_ref[...]
    columns = proj_ref.shape[1]
    length, features = events_ref.shape
    heads = out_ref.shape[0] // HEAD
    normed = norm_rows(events_ref[...]).astype(BF16)
    for half in range(2):
        core = place_ref[0] if half == 0 else 1 - place_ref[0]
        pick_ref[half] = pick_rows(features, shares, columns, core, False)
        normed_ref[half] = nt(pick_ref[half], normed).astype(BF16)
    packed = nt(normed, qkv_ref[...])
    packed_ref[...] = packed.astype(BF16)
    usable = lax.broadcasted_iota(jnp.int32, (length, length), 1) < count_ref[0]
    mixed = []
    for head in range(heads):
        query, keys, values = split_head(packed, head)
        scores = jnp.where(usable, nt(query, keys) * HEAD ** (-0.5), -1e30)
        weights = softmax(scores)
        weights_ref[head] = weights
        mixed.append(nn(weights.astype(BF16), values))
    mixed = jnp.concatenate(mixed, axis=1).astype(BF16)
    mixed_ref[...] = mixed
    part_ref[...] = nn(mixed, out_ref[...])
    rows = own_ref.shape[0]
    half = features // 2
    blocks = features // columns
    proj_half = proj_ref[pl.ds(pl.multiple_of(place_ref[0] * half, half), half), :]
    for k in range(ways):
        first = pl.multiple_of(place_ref[1 + k] * rows, rows)
        chosen = part_ref[pl.ds(first, rows), :].astype(BF16)
        if k == 0:
            own_ref[...] = chosen
            continue
        for b in range(blocks):
            peer_refs[k - 1][b * rows : (b + 1) * rows] = chosen[:, b * columns : (b + 1) * columns]
        peer_refs[k - 1][blocks * rows :] = proj_half


def rows_kernel(ways, *refs):
    sources, (feat_ref, proj_ref), held = refs[: ways + 1], refs[ways + 1 : ways + 3], refs[-ways - 2 : -1]
    for copy in fetch(sources, held, refs[-1]):
        copy.wait()
    events_ref, own_ref, *peer_refs = held
    rows, features = own_ref.shape
    columns = proj_ref.shape[2]
    for b in range(features // columns):
        block = slice(b * columns, (b + 1) * columns)
        branch = own_ref[:, block].astype(F32)
        for peer in peer_refs:
            branch = branch + peer[b * rows : (b + 1) * rows].astype(F32)
        feat_ref[:, block] = (events_ref[:, block].astype(F32) + branch).astype(BF16)
    for k, peer in enumerate(peer_refs):
        proj_ref[k] = peer[features // columns * rows :]


def teacher_norm_kernel(clip_ref, gain_ref, after_ref, normed_ref):
    normed_ref[...] = (norm_rows(clip_ref[...]) * gain_ref[...]).astype(BF16)


def teacher_kernel(
    place_ref, align_ref, normed_ref, own_ref, other_ref, feat_ref, part_ref, parts_ref, mixed_ref
):
    blocks, cores, rows, width = parts_ref.shape
    for i, piece in enumerate((own_ref, other_ref)):
        core = place_ref[0] if i == 0 else 1 - place_ref[0]
        parts_ref[:, pl.ds(core, 1)] = piece[...].reshape(blocks, 1, rows, width)
    full_ref = parts_ref[...].reshape(blocks * cores * rows, width)
    heads = width // (4 * HEAD)
    packed = nn(normed_ref[...], full_ref[:, : heads * 3 * HEAD])
    mixed = []
    for head in range(heads):
        query, keys, values = split_head(packed, head)
        weights = softmax(nt(query, keys) * HEAD ** (-0.5))
        mixed.append(nn(weights.astype(BF16), values))
    mixed_ref[...] = jnp.concatenate(mixed, axis=1)
    ways, shared = part_ref.shape[:2]
    outputs = blocks * cores * rows
    per_block = BLOCK // shared
    for i in range(align_ref.shape[0]):
        first = pl.multiple_of(align_ref[i] * BLOCK, BLOCK)
        chosen = mixed_ref[pl.ds(first, BLOCK), :].astype(BF16)
        part = nt(chosen, full_ref[:, heads * 3 * HEAD :]).astype(BF16)
        for k in range(per_block):
            part_ref[i * per_block + k, :, :outputs] = part[k * shared : (k + 1) * shared]
    for i in range(ways):
        part_ref[i, :, outputs:] = feat_ref[...]


def assemble_kernel(ways, place_ref, own_ref, mine_ref, other_ref, proj_ref):
    features, columns = own_ref.shape
    half = features // 2
    first = pl.multiple_of(place_ref[0] * half, half)
    second = pl.multiple_of((1 - place_ref[0]) * half, half)
    proj_ref[place_ref[1]] = own_ref[...]
    for k in range(1, ways):
        source = place_ref[1 + k]
        proj_ref[source, pl.ds(first, half), :] = mine_ref[k - 1]
        proj_ref[source, pl.ds(second, half), :] = other_ref[k - 1]


def predict_kernel(feat_ref, proj_ref, pred_ref):
    ways, features, columns = proj_ref.shape
    for k in range(ways):
        pred_ref[:, k * columns : (k + 1) * columns] = nn(feat_ref[...], proj_ref[k])


def extra_kernel(shares, columns, place_ref, parts_ref, after_ref, extra_ref):
    features = extra_ref.shape[1] * columns
    rows = parts_ref.shape[0] * parts_ref.shape[1]
    feat = parts_ref[...].reshape(rows, parts_ref.shape[2])[:, -features:]
    shifted = [feat]
    for b in range(1, features // columns):
        shifted.append(jnp.concatenate([feat[:, b:], feat[:, :b]], 1))
    for half in range(2):
        core = place_ref[0] if half == 0 else 1 - place_ref[0]
        pick = pick_rows(features, shares, columns, core, True)
        for b in range(features // columns):
            extra_ref[half, b] = nt(pick, shifted[b]).astype(BF16)


def diff_kernel(
    clips, count_ref, place_ref, parts_ref, tokens_ref, pred_ref, proj_ref, out_ref
):
    rows, width = tokens_ref.shape
    ways, features, columns = proj_ref.shape
    branch = parts_ref[0, :, :width].astype(F32)
    for i in range(1, ways):
        branch = branch + parts_ref[i, :, :width].astype(F32)
    target = (tokens_ref[...].astype(F32) + branch).astype(BF16).astype(F32)
    count = count_ref[0]
    live = lax.broadcasted_iota(jnp.int32, (rows, 1), 0) + place_ref[1] * rows < count
    scale = jnp.full((1, 1), count, jnp.int32).astype(F32) * width
    factor = 2.0 / (scale * clips)
    diff = jnp.where(live, pred_ref[...] - target, 0.0)
    squares = jnp.sum(diff * diff, -1, keepdims=True) / scale
    dpred = (diff * factor).astype(BF16)
    dfeat = jnp.zeros((rows, features), F32)
    for k in range(ways):
        dfeat = dfeat + nt(dpred[:, k * columns : (k + 1) * columns], proj_ref[k])
    dfeat = dfeat.astype(BF16)
    high = squares.astype(BF16)
    rest = squares - high.astype(F32)
    middle = rest.astype(BF16)
    low = (rest - middle.astype(F32)).astype(BF16)
    lane = lax.broadcasted_iota(jnp.int32, (rows, BLOCK), 1)
    tail = jnp.where(lane == 0, high.astype(F32), jnp.where(lane == 1, middle.astype(F32), 0.0))
    tail = jnp.where(lane == 2, low.astype(F32), tail).astype(BF16)
    for i in range(ways):
        out_ref[i, :, :features] = dfeat
        out_ref[i, :, features : features + columns] = dpred[:, i * columns : (i + 1) * columns]
        out_ref[i, :, features + columns :] = tail


def backward_kernel(held, back_ref, *refs):
    sources, (keep_ref, send_ref, loss_ref) = refs[:held], refs[held : held + 3]
    copies = fetch(sources, refs[2 * held + 3 : -1], refs[-1])
    out_ref, packed_ref, weights_ref, mixed_ref, normed_ref, pick_ref, feat_ref = refs[2 * held + 3 : -1]
    copies[0].wait()
    features = out_ref.shape[1]
    heads = out_ref.shape[0] // HEAD
    dfeat = back_ref[:, :features]
    columns = back_ref.shape[1] - features - BLOCK
    dpred = back_ref[:, features : features + columns]
    tail = back_ref[:, features + columns :].astype(F32)
    loss_ref[...] = jnp.sum(jnp.sum(tail, 0, keepdims=True), 1, keepdims=True)
    dmixed = nt(dfeat, out_ref[...])
    for copy in copies[1:3]:
        copy.wait()
    packed = packed_ref[...].astype(F32)
    pieces = []
    for head in range(heads):
        query, keys, values = split_head(packed, head)
        weights = weights_ref[head]
        cot = dmixed[:, head * HEAD : (head + 1) * HEAD].astype(BF16)
        dvalues = tn(weights.astype(BF16), cot)
        dweights = nt(cot, values)
        inner = jnp.sum(dweights * weights, -1, keepdims=True)
        dscores = (weights * (dweights - inner) * HEAD ** (-0.5)).astype(BF16)
        pieces += [nn(dscores, keys), tn(dscores, query), dvalues]
    dpacked = jnp.concatenate(pieces, axis=1)
    used = dpacked.shape[1]
    length = dpacked.shape[0]
    right = jnp.concatenate([dpacked, jnp.zeros((length, features - used), F32)], 1).astype(BF16)
    for copy in copies[3:]:
        copy.wait()
    tailed = features - columns
    mixed = jnp.concatenate(
        [jnp.zeros((length, used - tailed), F32), mixed_ref[...].astype(F32)], 1
    ).astype(BF16)
    for half, into in enumerate((keep_ref, send_ref)):
        dfeat_rows = nt(pick_ref[half], dfeat).astype(BF16)
        normed_rows = normed_ref[half]
        for b in range(features // columns):
            block = slice(b * columns, (b + 1) * columns)
            total = nn(normed_rows, right[:, block]) + nn(feat_ref[half, b], dpred)
            if b == features // columns - 1:
                total = total + nn(dfeat_rows, mixed)
            into[:, block] = total.astype(BF16)


SWAP = [(0, 1), (1, 0)]


def from_peers(rows, axis, places=None):
    ways = lax.axis_size(axis)
    return [
        lax.ppermute(rows(k), axis, [(i, (i + k) % ways) for i in range(ways)])
        for k in (range(1, ways) if places is None else places)
    ]


def add(a, b):
    return a.astype(F32) + b.astype(F32)


def result_kernel(parts_ref, q_ref, o_ref, p_ref):
    each, used = q_ref.shape
    columns = p_ref.shape[1]
    total = jnp.sum(parts_ref[...].astype(F32), 0)
    q_ref[...] = total[:each, :used]
    o_ref[...] = total[:each, used:]
    for i in range(total.shape[0] - each):
        for b in range(total.shape[1] // columns):
            row = i * (total.shape[1] // columns) + b
            p_ref[row : row + 1] = total[each + i : each + i + 1, b * columns : (b + 1) * columns]


def on_device(
    teacher_clips, teacher_gain, teacher_qkv, teacher_out_t, event_tokens, valid_counts, alignment,
    student_qkv, student_out, projector,
):
    clip, events, align = teacher_clips[0], event_tokens[0], alignment[0]
    length, width = clip.shape
    features = events.shape[1]
    columns = projector.shape[1]
    ways = lax.axis_size("x")
    rows = length // ways
    own_c, own_x = lax.axis_index("c"), lax.axis_index("x")
    shares = 1
    for axis in CLIP:
        shares = shares * lax.axis_size(axis)

    senders = lax.axis_size("y") * lax.axis_size("z")
    shard = jnp.concatenate([teacher_qkv, teacher_out_t], 1)
    shard = jnp.broadcast_to(shard[None], (senders, *shard.shape))
    own_core = lax.all_to_all(shard, ("y", "z"), 0, 0)
    heads = student_out.shape[0] // HEAD
    each = features // shares
    picked = shares // 2 * (each + each * columns // features)
    places = jnp.stack([own_c] + [(own_x + k) % ways for k in range(ways)]).astype(jnp.int32)
    message_rows = rows * features // columns + features // 2
    outs = pl.pallas_call(
        lambda *refs: student_kernel(shares, *refs),
        out_shape=(
            pltpu.HBM((rows, features), BF16),
            *[shape((message_rows, columns), BF16)] * (ways - 1),
            pltpu.HBM((2, picked, length), BF16),
            pltpu.HBM((length, 3 * HEAD * heads), BF16),
            pltpu.HBM((length, HEAD * heads), BF16),
            pltpu.HBM((heads, length, length), F32),
            pltpu.HBM((2, picked, features), BF16),
            *in_place([student_out]),
        ),
        in_specs=[SMEM] * 2 + [VMEM] * 4,
        out_specs=(pl.BlockSpec(),) + (VMEM,) * (ways - 1) + (pl.BlockSpec(),) * 6,
        scratch_shapes=[pltpu.VMEM((length, features), F32)],
        compiler_params=PARAMS,
        cost_estimate=cost(4),
        name="student_forward",
    )(valid_counts, places, events, student_qkv.T, student_out, projector)
    own_part, peer_parts = outs[0], outs[1:ways]
    normed_rows, packed, mixed, weights, pick, kept_out = outs[ways:]

    received = from_peers(lambda k: peer_parts[k - 1], "x")
    own_events = lax.dynamic_slice_in_dim(events, own_x * rows, rows, 0)
    feat_rows, proj_halves = pl.pallas_call(
        lambda *refs: rows_kernel(ways, *refs),
        out_shape=(
            shape((rows, features), BF16), shape((ways - 1, features // 2, columns), BF16),
            *in_place(received),
        ),
        in_specs=[ANY] * 2 + [HBM] * (ways - 1),
        out_specs=(VMEM,) * 2 + (HBM,) * (ways - 1),
        input_output_aliases={2 + k: 2 + k for k in range(ways - 1)},
        scratch_shapes=buffers((own_events, own_part, *received)),
        compiler_params=PARAMS,
        cost_estimate=cost(1),
        name="student_rows",
    )(own_events, own_part, *received)[:2]
    own_core, feat_rows, proj_halves = lax.optimization_barrier((own_core, feat_rows, proj_halves))
    other_core = lax.ppermute(own_core, "c", SWAP)
    proj_others = lax.ppermute(proj_halves, "c", SWAP)
    teacher_normed = pl.pallas_call(
        teacher_norm_kernel,
        out_shape=shape((length, width), BF16),
        in_specs=[VMEM] * 2 + [ANY],
        out_specs=VMEM,
        compiler_params=PARAMS,
        cost_estimate=cost(1),
        name="teacher_norm",
    )(clip, teacher_gain.reshape(1, width), feat_rows)

    teacher_part = pl.pallas_call(
        teacher_kernel,
        out_shape=shape((ways, rows, width + features), BF16),
        in_specs=[SMEM] * 2 + [VMEM] * 4,
        out_specs=VMEM,
        scratch_shapes=[
            pltpu.VMEM((senders, 2, *shard.shape[1:]), BF16),
            pltpu.VMEM((length, teacher_out_t.shape[1]), F32),
        ],
        compiler_params=PARAMS,
        cost_estimate=cost(5),
        name="teacher",
    )(places, align, teacher_normed, own_core, other_core, feat_rows)

    teacher_parts = lax.all_to_all(teacher_part, "x", 0, 0)
    per_block = BLOCK // rows
    source = align[own_x // per_block] * BLOCK + own_x % per_block * rows
    own_tokens = lax.dynamic_slice_in_dim(clip, source, rows, 0)
    sources = jnp.stack([own_c] + [(own_x - k + ways) % ways for k in range(ways)]).astype(jnp.int32)
    whole_proj = pl.pallas_call(
        lambda *refs: assemble_kernel(ways, *refs),
        out_shape=pltpu.HBM((ways, features, columns), BF16),
        in_specs=[SMEM] + [VMEM] * 3,
        out_specs=pl.BlockSpec(),
        compiler_params=PARAMS,
        cost_estimate=cost(1),
        name="projector",
    )(sources, projector, proj_halves, proj_others)
    pred = pl.pallas_call(
        predict_kernel,
        out_shape=shape((rows, width), F32),
        in_specs=[VMEM] * 2,
        out_specs=VMEM,
        compiler_params=PARAMS,
        cost_estimate=cost(2),
        name="student_predict",
    )(feat_rows, whole_proj)
    message = pl.pallas_call(
        lambda *refs: diff_kernel(shares, *refs),
        out_shape=shape((ways, rows, features + columns + BLOCK), BF16),
        in_specs=[SMEM] * 2 + [VMEM] * 4,
        out_specs=VMEM,
        compiler_params=PARAMS,
        cost_estimate=cost(2),
        name="difference",
    )(valid_counts, sources, teacher_parts, own_tokens, pred, whole_proj)
    feat_extra = pl.pallas_call(
        lambda *refs: extra_kernel(shares, columns, *refs),
        out_shape=pltpu.HBM((2, features // columns, picked, length), BF16),
        in_specs=[SMEM, VMEM, ANY],
        out_specs=pl.BlockSpec(),
        compiler_params=PARAMS,
        cost_estimate=cost(3),
        name="student_extra",
    )(sources, teacher_parts, message)
    back = lax.all_to_all(message, "x", 0, 0).reshape(length, features + columns + BLOCK)

    held = (kept_out, packed, weights, mixed, normed_rows, pick, feat_extra)
    keep, send, loss = pl.pallas_call(
        lambda *refs: backward_kernel(len(held), *refs),
        out_shape=(
            shape((picked, features), BF16), shape((picked, features), BF16), shape((1, 1), F32),
            *in_place(held),
        ),
        in_specs=[VMEM] + [HBM] * len(held),
        out_specs=(VMEM,) * 3 + (HBM,) * len(held),
        scratch_shapes=buffers(held),
        input_output_aliases={1 + i: 3 + i for i in range(len(held))},
        compiler_params=PARAMS,
        cost_estimate=cost(4),
        name="student_backward",
    )(back, *held)[:3]

    total = add(keep, lax.ppermute(send, "c", SWAP)).astype(BF16)
    chips = shares // 2
    spread = lax.all_to_all(
        total.reshape(chips, total.shape[0] // chips, features), CLIP[:3], 0, 0
    )
    used = 3 * HEAD * heads
    grad_q, grad_o, grad_p = pl.pallas_call(
        result_kernel,
        out_shape=(
            shape((each, used), F32), shape((each, HEAD * heads), F32), shape((each, columns), F32),
        ),
        in_specs=[VMEM],
        out_specs=(VMEM,) * 3,
        compiler_params=PARAMS,
        cost_estimate=cost(1),
        name="gradient_rows",
    )(spread)
    return loss.reshape(1), grad_q, grad_o.T, grad_p


def solution(mesh):
    group, dp, tensor = mesh.devices.shape
    fine = Mesh(mesh.devices.reshape(group, 4, dp // 8, 2, tensor), (*CLIP, "x"))
    dp = CLIP[1:]
    in_specs = (
        P(CLIP, None, None), P(), P(dp, "x"), P(dp, "x"), P(CLIP, None, None), P(CLIP), P(CLIP, None),
        P(None, "x"), P("x", None), P(None, "x"),
    )
    out_specs = (P(CLIP), P(CLIP, "x"), P("x", CLIP), P(CLIP, "x"))
    return jax.shard_map(
        on_device, mesh=fine, in_specs=in_specs, out_specs=out_specs, check_vma=False
    )
```

```python
import jax
import jax.numpy as jnp
from jax import lax
from jax.experimental import pallas as pl
from jax.experimental.pallas import tpu as pltpu
from jax.sharding import Mesh, PartitionSpec as P

HEAD = 64
BLOCK = 128
F32 = jnp.float32
BF16 = jnp.bfloat16
CLIP = ("g", "y", "z", "c")
ANY = pl.BlockSpec(memory_space=pl.ANY)
HBM = pl.BlockSpec(memory_space=pltpu.HBM)
VMEM = pl.BlockSpec(memory_space=pltpu.VMEM)
SMEM = pl.BlockSpec(memory_space=pltpu.SMEM)
PARAMS = pltpu.CompilerParams(vmem_limit_bytes=20 * 1024 * 1024)


def cost(microseconds):
    return pl.CostEstimate(flops=microseconds * 10**9, bytes_accessed=10**6, transcendentals=0)


def fetch(sources, buffers, sems):
    copies = [
        pltpu.make_async_copy(source, buffer, sems.at[i])
        for i, (source, buffer) in enumerate(zip(sources, buffers))
    ]
    for copy in copies:
        copy.start()
    return copies


def buffers(arrays):
    return [pltpu.VMEM(array.shape, array.dtype) for array in arrays] + [
        pltpu.SemaphoreType.DMA((len(arrays),))
    ]


def in_place(arrays):
    return [pltpu.HBM(array.shape, array.dtype) for array in arrays]


def shape(dims, dtype):
    return jax.ShapeDtypeStruct(dims, dtype)


def nn(a, b):
    return lax.dot_general(a, b, (((1,), (0,)), ((), ())), preferred_element_type=F32)


def nt(a, b):
    return lax.dot_general(a, b, (((1,), (1,)), ((), ())), preferred_element_type=F32)


def tn(a, b):
    return lax.dot_general(a, b, (((0,), (0,)), ((), ())), preferred_element_type=F32)


def norm_rows(rows):
    rows = rows.astype(F32)
    centre = rows - jnp.mean(rows, -1, keepdims=True)
    spread = jnp.mean(centre * centre, -1, keepdims=True)
    return centre * lax.rsqrt(spread + 1e-05)


def split_head(packed, head):
    first = head * 3 * HEAD
    return [packed[:, first + i * HEAD : first + (i + 1) * HEAD].astype(BF16) for i in range(3)]


def softmax(scores):
    top = jnp.max(scores, -1, keepdims=True)
    weights = jnp.exp(scores - top)
    return weights / jnp.sum(weights, -1, keepdims=True)


def pick_rows(rows, shares, columns, core, extra):
    each = rows // shares
    block = each + each * columns // rows
    place = lax.broadcasted_iota(jnp.int32, (shares // 2 * block, 1), 0)
    chip, row = place // block, place % block
    base = (chip * 2 + core) * each
    if extra:
        wanted = jnp.where(row >= each, base + (row - each) * (rows // columns), -1)
    else:
        wanted = jnp.where(row < each, base + row, -1)
    source = lax.broadcasted_iota(jnp.int32, (shares // 2 * block, rows), 1)
    return jnp.where(source == wanted, 1.0, 0.0).astype(BF16)


def picks_kernel(shares, columns, place_ref, normed_ref, after_ref, rows_ref, pick_ref):
    features = pick_ref.shape[2]
    for half in range(2):
        core = place_ref[0] if half == 0 else 1 - place_ref[0]
        pick_ref[half] = pick_rows(features, shares, columns, core, False)
        rows_ref[half] = nt(pick_ref[half], normed_ref[...]).astype(BF16)


def student_kernel(count_ref, place_ref, events_ref, qkv_ref, out_ref, proj_ref, *refs):
    ways = len(refs) - 6
    own_ref, peer_refs = refs[0], refs[1:ways]
    normed_ref, packed_ref, mixed_ref, weights_ref, kept_ref, part_ref = refs[ways:]
    kept_ref[...] = out_ref[...]
    columns = proj_ref.shape[1]
    length, features = events_ref.shape
    heads = out_ref.shape[0] // HEAD
    normed = norm_rows(events_ref[...]).astype(BF16)
    normed_ref[...] = normed
    packed = nt(normed, qkv_ref[...])
    packed_ref[...] = packed.astype(BF16)
    usable = lax.broadcasted_iota(jnp.int32, (length, length), 1) < count_ref[0]
    mixed = []
    for head in range(heads):
        query, keys, values = split_head(packed, head)
        scores = jnp.where(usable, nt(query, keys) * HEAD ** (-0.5), -1e30)
        weights = softmax(scores).astype(BF16)
        weights_ref[head] = weights
        mixed.append(nn(weights, values))
    mixed = jnp.concatenate(mixed, axis=1).astype(BF16)
    mixed_ref[...] = mixed
    part_ref[...] = nn(mixed, out_ref[...])
    rows = own_ref.shape[0]
    half = features // 2
    blocks = features // columns
    proj_half = proj_ref[pl.ds(pl.multiple_of(place_ref[0] * half, half), half), :]
    for k in range(ways):
        first = pl.multiple_of(place_ref[1 + k] * rows, rows)
        chosen = part_ref[pl.ds(first, rows), :].astype(BF16)
        if k not in (1, ways - 1):
            (own_ref if k == 0 else peer_refs[k - 1])[...] = chosen
            continue
        for b in range(blocks):
            peer_refs[k - 1][b * rows : (b + 1) * rows] = chosen[:, b * columns : (b + 1) * columns]
        peer_refs[k - 1][blocks * rows :] = proj_half


def rows_kernel(ways, *refs):
    sources, (feat_ref, proj_ref), held = refs[: ways + 2], refs[ways + 2 : ways + 4], refs[-ways - 3 : -1]
    for copy in fetch(sources, held, refs[-1]):
        copy.wait()
    events_ref, own_ref, before_ref, opposite_ref, behind_ref, far_ref = held
    rows, features = own_ref.shape
    columns = proj_ref.shape[2]
    blocks = features // columns
    for b in range(blocks):
        lanes = slice(b * columns, (b + 1) * columns)
        branch = own_ref[:, lanes].astype(F32) + opposite_ref[:, lanes].astype(F32)
        for peer in (before_ref, behind_ref):
            branch = branch + peer[b * rows : (b + 1) * rows].astype(F32)
        feat_ref[:, lanes] = (events_ref[:, lanes].astype(F32) + branch).astype(BF16)
    proj_ref[0] = before_ref[blocks * rows :]
    proj_ref[1] = far_ref[...]
    proj_ref[2] = behind_ref[blocks * rows :]


def teacher_norm_kernel(clip_ref, gain_ref, after_ref, normed_ref):
    normed_ref[...] = (norm_rows(clip_ref[...]) * gain_ref[...]).astype(BF16)


def teacher_kernel(
    place_ref, align_ref, normed_ref, own_ref, other_ref, feat_ref, part_ref, parts_ref, mixed_ref
):
    blocks, cores, rows, width = parts_ref.shape
    for i, piece in enumerate((own_ref, other_ref)):
        core = place_ref[0] if i == 0 else 1 - place_ref[0]
        parts_ref[:, pl.ds(core, 1)] = piece[...].reshape(blocks, 1, rows, width)
    full_ref = parts_ref[...].reshape(blocks * cores * rows, width)
    heads = width // (4 * HEAD)
    packed = nn(normed_ref[...], full_ref[:, : heads * 3 * HEAD])
    mixed = []
    for head in range(heads):
        query, keys, values = split_head(packed, head)
        weights = softmax(nt(query, keys) * HEAD ** (-0.5))
        mixed.append(nn(weights.astype(BF16), values))
    mixed_ref[...] = jnp.concatenate(mixed, axis=1)
    ways, shared = part_ref.shape[:2]
    outputs = blocks * cores * rows
    per_block = BLOCK // shared
    for i in range(align_ref.shape[0]):
        first = pl.multiple_of(align_ref[i] * BLOCK, BLOCK)
        chosen = mixed_ref[pl.ds(first, BLOCK), :].astype(BF16)
        part = nt(chosen, full_ref[:, heads * 3 * HEAD :]).astype(BF16)
        for k in range(per_block):
            part_ref[i * per_block + k, :, :outputs] = part[k * shared : (k + 1) * shared]
    for i in range(ways):
        part_ref[i, :, outputs:] = feat_ref[...]


def assemble_kernel(ways, place_ref, own_ref, mine_ref, other_ref, proj_ref):
    features, columns = own_ref.shape
    half = features // 2
    first = pl.multiple_of(place_ref[0] * half, half)
    second = pl.multiple_of((1 - place_ref[0]) * half, half)
    proj_ref[place_ref[1]] = own_ref[...]
    for k in range(1, ways):
        source = place_ref[1 + k]
        proj_ref[source, pl.ds(first, half), :] = mine_ref[k - 1]
        proj_ref[source, pl.ds(second, half), :] = other_ref[k - 1]


def predict_kernel(feat_ref, proj_ref, pred_ref):
    ways, features, columns = proj_ref.shape
    for k in range(ways):
        pred_ref[:, k * columns : (k + 1) * columns] = nn(feat_ref[...], proj_ref[k])


def extra_kernel(shares, columns, place_ref, parts_ref, after_ref, extra_ref):
    features = extra_ref.shape[1] * columns
    rows = parts_ref.shape[0] * parts_ref.shape[1]
    feat = parts_ref[...].reshape(rows, parts_ref.shape[2])[:, -features:]
    shifted = [feat]
    for b in range(1, features // columns):
        shifted.append(jnp.concatenate([feat[:, b:], feat[:, :b]], 1))
    for half in range(2):
        core = place_ref[0] if half == 0 else 1 - place_ref[0]
        pick = pick_rows(features, shares, columns, core, True)
        for b in range(features // columns):
            extra_ref[half, b] = nt(pick, shifted[b]).astype(BF16)


def diff_kernel(
    clips, count_ref, place_ref, parts_ref, tokens_ref, pred_ref, proj_ref, out_ref
):
    rows, width = tokens_ref.shape
    ways, features, columns = proj_ref.shape
    branch = parts_ref[0, :, :width].astype(F32)
    for i in range(1, ways):
        branch = branch + parts_ref[i, :, :width].astype(F32)
    target = (tokens_ref[...].astype(F32) + branch).astype(BF16).astype(F32)
    count = count_ref[0]
    live = lax.broadcasted_iota(jnp.int32, (rows, 1), 0) + place_ref[1] * rows < count
    scale = jnp.full((1, 1), count, jnp.int32).astype(F32) * width
    factor = 2.0 / (scale * clips)
    diff = jnp.where(live, pred_ref[...] - target, 0.0)
    squares = jnp.sum(diff * diff, -1, keepdims=True) / scale
    dpred = (diff * factor).astype(BF16)
    dfeat = jnp.zeros((rows, features), F32)
    for k in range(ways):
        dfeat = dfeat + nt(dpred[:, k * columns : (k + 1) * columns], proj_ref[k])
    dfeat = dfeat.astype(BF16)
    high = squares.astype(BF16)
    rest = squares - high.astype(F32)
    middle = rest.astype(BF16)
    low = (rest - middle.astype(F32)).astype(BF16)
    lane = lax.broadcasted_iota(jnp.int32, (rows, BLOCK), 1)
    tail = jnp.where(lane == 0, high.astype(F32), jnp.where(lane == 1, middle.astype(F32), 0.0))
    tail = jnp.where(lane == 2, low.astype(F32), tail).astype(BF16)
    for i in range(ways):
        out_ref[i, :, :features] = dfeat
        out_ref[i, :, features : features + columns] = dpred[:, i * columns : (i + 1) * columns]
        out_ref[i, :, features + columns :] = tail


def backward_kernel(held, back_ref, *refs):
    sources, (keep_ref, send_ref, loss_ref) = refs[:held], refs[held : held + 3]
    copies = fetch(sources, refs[2 * held + 3 : -1], refs[-1])
    out_ref, packed_ref, weights_ref, mixed_ref, normed_ref, pick_ref, feat_ref = refs[2 * held + 3 : -1]
    copies[0].wait()
    features = out_ref.shape[1]
    heads = out_ref.shape[0] // HEAD
    dfeat = back_ref[:, :features]
    columns = back_ref.shape[1] - features - BLOCK
    dpred = back_ref[:, features : features + columns]
    tail = back_ref[:, features + columns :].astype(F32)
    loss_ref[...] = jnp.sum(jnp.sum(tail, 0, keepdims=True), 1, keepdims=True)
    dmixed = nt(dfeat, out_ref[...])
    for copy in copies[1:3]:
        copy.wait()
    packed = packed_ref[...].astype(F32)
    pieces = []
    for head in range(heads):
        query, keys, values = split_head(packed, head)
        rounded = weights_ref[head]
        weights = rounded.astype(F32)
        cot = dmixed[:, head * HEAD : (head + 1) * HEAD].astype(BF16)
        dvalues = tn(rounded, cot)
        dweights = nt(cot, values)
        inner = jnp.sum(dweights * weights, -1, keepdims=True)
        dscores = (weights * (dweights - inner) * HEAD ** (-0.5)).astype(BF16)
        pieces += [nn(dscores, keys), tn(dscores, query), dvalues]
    dpacked = jnp.concatenate(pieces, axis=1)
    used = dpacked.shape[1]
    length = dpacked.shape[0]
    right = jnp.concatenate([dpacked, jnp.zeros((length, features - used), F32)], 1).astype(BF16)
    for copy in copies[3:]:
        copy.wait()
    tailed = features - columns
    mixed = jnp.concatenate(
        [jnp.zeros((length, used - tailed), F32), mixed_ref[...].astype(F32)], 1
    ).astype(BF16)
    for half, into in enumerate((keep_ref, send_ref)):
        dfeat_rows = nt(pick_ref[half], dfeat).astype(BF16)
        normed_rows = normed_ref[half]
        for b in range(features // columns):
            block = slice(b * columns, (b + 1) * columns)
            total = nn(normed_rows, right[:, block]) + nn(feat_ref[half, b], dpred)
            if b == features // columns - 1:
                total = total + nn(dfeat_rows, mixed)
            into[:, block] = total.astype(BF16)


SWAP = [(0, 1), (1, 0)]


def from_peers(rows, axis, places=None):
    ways = lax.axis_size(axis)
    return [
        lax.ppermute(rows(k), axis, [(i, (i + k) % ways) for i in range(ways)])
        for k in (range(1, ways) if places is None else places)
    ]


def add(a, b):
    return a.astype(F32) + b.astype(F32)


def result_kernel(parts_ref, q_ref, o_ref, p_ref):
    each, used = q_ref.shape
    columns = p_ref.shape[1]
    total = jnp.sum(parts_ref[...].astype(F32), 0)
    q_ref[...] = total[:each, :used]
    o_ref[...] = total[:each, used:]
    for i in range(total.shape[0] - each):
        for b in range(total.shape[1] // columns):
            row = i * (total.shape[1] // columns) + b
            p_ref[row : row + 1] = total[each + i : each + i + 1, b * columns : (b + 1) * columns]


def on_device(
    teacher_clips, teacher_gain, teacher_qkv, teacher_out_t, event_tokens, valid_counts, alignment,
    student_qkv, student_out, projector,
):
    clip, events, align = teacher_clips[0], event_tokens[0], alignment[0]
    length, width = clip.shape
    features = events.shape[1]
    columns = projector.shape[1]
    ways = lax.axis_size("x")
    rows = length // ways
    own_c, own_x = lax.axis_index("c"), lax.axis_index("x")
    shares = 1
    for axis in CLIP:
        shares = shares * lax.axis_size(axis)

    senders = lax.axis_size("y") * lax.axis_size("z")
    shard = jnp.concatenate([teacher_qkv, teacher_out_t], 1)
    shard = jnp.broadcast_to(shard[None], (senders, *shard.shape))
    own_core = lax.all_to_all(shard, ("y", "z"), 0, 0)
    heads = student_out.shape[0] // HEAD
    each = features // shares
    picked = shares // 2 * (each + each * columns // features)
    places = jnp.stack([own_c] + [(own_x + k) % ways for k in range(ways)]).astype(jnp.int32)
    message_rows = rows * features // columns + features // 2
    half = features // 2
    proj_half = lax.dynamic_slice_in_dim(projector, own_c * half, half, 0)
    far = from_peers(lambda k: proj_half, "x", range(2, ways - 1))
    outs = pl.pallas_call(
        student_kernel,
        out_shape=(
            pltpu.HBM((rows, features), BF16),
            *[
                shape((message_rows, columns) if k in (1, ways - 1) else (rows, features), BF16)
                for k in range(1, ways)
            ],
            pltpu.HBM((length, features), BF16),
            pltpu.HBM((length, 3 * HEAD * heads), BF16),
            pltpu.HBM((length, HEAD * heads), BF16),
            pltpu.HBM((heads, length, length), BF16),
            *in_place([student_out]),
        ),
        in_specs=[SMEM] * 2 + [VMEM] * 4,
        out_specs=(pl.BlockSpec(),) + (VMEM,) * (ways - 1) + (pl.BlockSpec(),) * 5,
        scratch_shapes=[pltpu.VMEM((length, features), F32)],
        compiler_params=PARAMS,
        cost_estimate=cost(4),
        name="student_forward",
    )(valid_counts, places, events, student_qkv.T, student_out, projector)
    own_part, peer_parts = outs[0], outs[1:ways]
    normed, packed, mixed, weights, kept_out = outs[ways:]
    normed_rows, pick = pl.pallas_call(
        lambda *refs: picks_kernel(shares, columns, *refs),
        out_shape=(
            pltpu.HBM((2, picked, length), BF16), pltpu.HBM((2, picked, features), BF16),
        ),
        in_specs=[SMEM, VMEM, ANY],
        out_specs=(pl.BlockSpec(),) * 2,
        compiler_params=PARAMS,
        cost_estimate=cost(2),
        name="student_picks",
    )(places, normed, far[0])

    received = from_peers(lambda k: peer_parts[k - 1], "x") + far
    own_events = lax.dynamic_slice_in_dim(events, own_x * rows, rows, 0)
    feat_rows, proj_halves = pl.pallas_call(
        lambda *refs: rows_kernel(ways, *refs),
        out_shape=(
            shape((rows, features), BF16), shape((ways - 1, features // 2, columns), BF16),
            *in_place(received),
        ),
        in_specs=[ANY] * 2 + [HBM] * ways,
        out_specs=(VMEM,) * 2 + (HBM,) * ways,
        input_output_aliases={2 + k: 2 + k for k in range(ways)},
        scratch_shapes=buffers((own_events, own_part, *received)),
        compiler_params=PARAMS,
        cost_estimate=cost(1),
        name="student_rows",
    )(own_events, own_part, *received)[:2]
    own_core, feat_rows, proj_halves, normed_rows = lax.optimization_barrier(
        (own_core, feat_rows, proj_halves, normed_rows)
    )
    other_core = lax.ppermute(own_core, "c", SWAP)
    proj_others = lax.ppermute(proj_halves, "c", SWAP)
    teacher_normed = pl.pallas_call(
        teacher_norm_kernel,
        out_shape=shape((length, width), BF16),
        in_specs=[VMEM] * 2 + [ANY],
        out_specs=VMEM,
        compiler_params=PARAMS,
        cost_estimate=cost(1),
        name="teacher_norm",
    )(clip, teacher_gain.reshape(1, width), feat_rows)

    teacher_part = pl.pallas_call(
        teacher_kernel,
        out_shape=shape((ways, rows, width + features), BF16),
        in_specs=[SMEM] * 2 + [VMEM] * 4,
        out_specs=VMEM,
        scratch_shapes=[
            pltpu.VMEM((senders, 2, *shard.shape[1:]), BF16),
            pltpu.VMEM((length, teacher_out_t.shape[1]), F32),
        ],
        compiler_params=PARAMS,
        cost_estimate=cost(5),
        name="teacher",
    )(places, align, teacher_normed, own_core, other_core, feat_rows)

    teacher_parts = lax.all_to_all(teacher_part, "x", 0, 0)
    per_block = BLOCK // rows
    source = align[own_x // per_block] * BLOCK + own_x % per_block * rows
    own_tokens = lax.dynamic_slice_in_dim(clip, source, rows, 0)
    sources = jnp.stack([own_c] + [(own_x - k + ways) % ways for k in range(ways)]).astype(jnp.int32)
    whole_proj = pl.pallas_call(
        lambda *refs: assemble_kernel(ways, *refs),
        out_shape=pltpu.HBM((ways, features, columns), BF16),
        in_specs=[SMEM] + [VMEM] * 3,
        out_specs=pl.BlockSpec(),
        compiler_params=PARAMS,
        cost_estimate=cost(1),
        name="projector",
    )(sources, projector, proj_halves, proj_others)
    pred = pl.pallas_call(
        predict_kernel,
        out_shape=shape((rows, width), F32),
        in_specs=[VMEM] * 2,
        out_specs=VMEM,
        compiler_params=PARAMS,
        cost_estimate=cost(2),
        name="student_predict",
    )(feat_rows, whole_proj)
    message = pl.pallas_call(
        lambda *refs: diff_kernel(shares, *refs),
        out_shape=shape((ways, rows, features + columns + BLOCK), BF16),
        in_specs=[SMEM] * 2 + [VMEM] * 4,
        out_specs=VMEM,
        compiler_params=PARAMS,
        cost_estimate=cost(2),
        name="difference",
    )(valid_counts, sources, teacher_parts, own_tokens, pred, whole_proj)
    feat_extra = pl.pallas_call(
        lambda *refs: extra_kernel(shares, columns, *refs),
        out_shape=pltpu.HBM((2, features // columns, picked, length), BF16),
        in_specs=[SMEM, VMEM, ANY],
        out_specs=pl.BlockSpec(),
        compiler_params=PARAMS,
        cost_estimate=cost(3),
        name="student_extra",
    )(sources, teacher_parts, message)
    back = lax.all_to_all(message, "x", 0, 0).reshape(length, features + columns + BLOCK)

    held = (kept_out, packed, weights, mixed, normed_rows, pick, feat_extra)
    keep, send, loss = pl.pallas_call(
        lambda *refs: backward_kernel(len(held), *refs),
        out_shape=(
            shape((picked, features), BF16), shape((picked, features), BF16), shape((1, 1), F32),
            *in_place(held),
        ),
        in_specs=[VMEM] + [HBM] * len(held),
        out_specs=(VMEM,) * 3 + (HBM,) * len(held),
        scratch_shapes=buffers(held),
        input_output_aliases={1 + i: 3 + i for i in range(len(held))},
        compiler_params=PARAMS,
        cost_estimate=cost(4),
        name="student_backward",
    )(back, *held)[:3]

    total = add(keep, lax.ppermute(send, "c", SWAP)).astype(BF16)
    chips = shares // 2
    spread = lax.all_to_all(
        total.reshape(chips, total.shape[0] // chips, features), CLIP[:3], 0, 0
    )
    used = 3 * HEAD * heads
    grad_q, grad_o, grad_p = pl.pallas_call(
        result_kernel,
        out_shape=(
            shape((each, used), F32), shape((each, HEAD * heads), F32), shape((each, columns), F32),
        ),
        in_specs=[VMEM],
        out_specs=(VMEM,) * 3,
        compiler_params=PARAMS,
        cost_estimate=cost(1),
        name="gradient_rows",
    )(spread)
    return loss.reshape(1), grad_q, grad_o.T, grad_p


def solution(mesh):
    group, dp, tensor = mesh.devices.shape
    fine = Mesh(mesh.devices.reshape(group, 4, dp // 8, 2, tensor), (*CLIP, "x"))
    dp = CLIP[1:]
    in_specs = (
        P(CLIP, None, None), P(), P(dp, "x"), P(dp, "x"), P(CLIP, None, None), P(CLIP), P(CLIP, None),
        P(None, "x"), P("x", None), P(None, "x"),
    )
    out_specs = (P(CLIP), P(CLIP, "x"), P("x", CLIP), P(CLIP, "x"))
    return jax.shard_map(
        on_device, mesh=fine, in_specs=in_specs, out_specs=out_specs, check_vma=False
    )
```

```python
import jax
import jax.numpy as jnp
from jax import lax
from jax.experimental import pallas as pl
from jax.experimental.pallas import tpu as pltpu
from jax.sharding import Mesh, PartitionSpec as P

HEAD = 64
BLOCK = 128
F32 = jnp.float32
BF16 = jnp.bfloat16
CLIP = ("g", "y", "z", "c")
ANY = pl.BlockSpec(memory_space=pl.ANY)
HBM = pl.BlockSpec(memory_space=pltpu.HBM)
VMEM = pl.BlockSpec(memory_space=pltpu.VMEM)
SMEM = pl.BlockSpec(memory_space=pltpu.SMEM)
PARAMS = pltpu.CompilerParams(vmem_limit_bytes=20 * 1024 * 1024)


def cost(microseconds):
    return pl.CostEstimate(flops=microseconds * 10**9, bytes_accessed=10**6, transcendentals=0)


def fetch(sources, buffers, sems):
    copies = [
        pltpu.make_async_copy(source, buffer, sems.at[i])
        for i, (source, buffer) in enumerate(zip(sources, buffers))
    ]
    for copy in copies:
        copy.start()
    return copies


def buffers(arrays):
    return [pltpu.VMEM(array.shape, array.dtype) for array in arrays] + [
        pltpu.SemaphoreType.DMA((len(arrays),))
    ]


def in_place(arrays):
    return [pltpu.HBM(array.shape, array.dtype) for array in arrays]


def shape(dims, dtype):
    return jax.ShapeDtypeStruct(dims, dtype)


def nn(a, b):
    return lax.dot_general(a, b, (((1,), (0,)), ((), ())), preferred_element_type=F32)


def nt(a, b):
    return lax.dot_general(a, b, (((1,), (1,)), ((), ())), preferred_element_type=F32)


def tn(a, b):
    return lax.dot_general(a, b, (((0,), (0,)), ((), ())), preferred_element_type=F32)


def norm_rows(rows):
    rows = rows.astype(F32)
    centre = rows - jnp.mean(rows, -1, keepdims=True)
    spread = jnp.mean(centre * centre, -1, keepdims=True)
    return centre * lax.rsqrt(spread + 1e-05)


def split_head(packed, head):
    first = head * 3 * HEAD
    return [packed[:, first + i * HEAD : first + (i + 1) * HEAD].astype(BF16) for i in range(3)]


def softmax(scores):
    top = jnp.max(scores, -1, keepdims=True)
    weights = jnp.exp(scores - top)
    return weights / jnp.sum(weights, -1, keepdims=True)


def pick_rows(rows, shares, columns, core, extra):
    each = rows // shares
    block = each + each * columns // rows
    place = lax.broadcasted_iota(jnp.int32, (shares // 2 * block, 1), 0)
    chip, row = place // block, place % block
    base = (chip * 2 + core) * each
    if extra:
        wanted = jnp.where(row >= each, base + (row - each) * (rows // columns), -1)
    else:
        wanted = jnp.where(row < each, base + row, -1)
    source = lax.broadcasted_iota(jnp.int32, (shares // 2 * block, rows), 1)
    return jnp.where(source == wanted, 1.0, 0.0).astype(BF16)


def picks_kernel(shares, columns, place_ref, normed_ref, after_ref, rows_ref, pick_ref):
    features = pick_ref.shape[2]
    for half in range(2):
        core = place_ref[0] if half == 0 else 1 - place_ref[0]
        pick_ref[half] = pick_rows(features, shares, columns, core, False)
        rows_ref[half] = nt(pick_ref[half], normed_ref[...]).astype(BF16)


def student_kernel(count_ref, place_ref, events_ref, qkv_ref, out_ref, proj_ref, *refs):
    ways = len(refs) - 6
    own_ref, peer_refs = refs[0], refs[1:ways]
    normed_ref, packed_ref, mixed_ref, weights_ref, kept_ref, part_ref = refs[ways:]
    kept_ref[...] = out_ref[...]
    columns = proj_ref.shape[1]
    length, features = events_ref.shape
    heads = out_ref.shape[0] // HEAD
    normed = norm_rows(events_ref[...]).astype(BF16)
    normed_ref[...] = normed
    packed = nt(normed, qkv_ref[...])
    packed_ref[...] = packed.astype(BF16)
    usable = lax.broadcasted_iota(jnp.int32, (length, length), 1) < count_ref[0]
    mixed = []
    for head in range(heads):
        query, keys, values = split_head(packed, head)
        scores = jnp.where(usable, nt(query, keys) * HEAD ** (-0.5), -1e30)
        weights = softmax(scores).astype(BF16)
        weights_ref[head] = weights
        mixed.append(nn(weights, values))
    mixed = jnp.concatenate(mixed, axis=1).astype(BF16)
    mixed_ref[...] = mixed
    part_ref[...] = nn(mixed, out_ref[...])
    rows = own_ref.shape[0]
    half = features // 2
    blocks = features // columns
    proj_half = proj_ref[pl.ds(pl.multiple_of(place_ref[0] * half, half), half), :]
    for k in range(ways):
        first = pl.multiple_of(place_ref[1 + k] * rows, rows)
        chosen = part_ref[pl.ds(first, rows), :].astype(BF16)
        if k not in (1, ways - 1):
            (own_ref if k == 0 else peer_refs[k - 1])[...] = chosen
            continue
        for b in range(blocks):
            peer_refs[k - 1][b * rows : (b + 1) * rows] = chosen[:, b * columns : (b + 1) * columns]
        peer_refs[k - 1][blocks * rows :] = proj_half


def rows_kernel(ways, *refs):
    sources, (feat_ref, proj_ref), held = refs[: ways + 2], refs[ways + 2 : ways + 4], refs[-ways - 3 : -1]
    for copy in fetch(sources, held, refs[-1]):
        copy.wait()
    events_ref, own_ref, before_ref, opposite_ref, behind_ref, far_ref = held
    rows, features = own_ref.shape
    columns = proj_ref.shape[2]
    blocks = features // columns
    for b in range(blocks):
        lanes = slice(b * columns, (b + 1) * columns)
        branch = own_ref[:, lanes].astype(F32) + opposite_ref[:, lanes].astype(F32)
        for peer in (before_ref, behind_ref):
            branch = branch + peer[b * rows : (b + 1) * rows].astype(F32)
        feat_ref[:, lanes] = (events_ref[:, lanes].astype(F32) + branch).astype(BF16)
    proj_ref[0] = before_ref[blocks * rows :]
    proj_ref[1] = far_ref[...]
    proj_ref[2] = behind_ref[blocks * rows :]


def teacher_norm_kernel(clip_ref, gain_ref, after_ref, normed_ref):
    normed_ref[...] = (norm_rows(clip_ref[...]) * gain_ref[...]).astype(BF16)


def teacher_kernel(
    place_ref, align_ref, normed_ref, own_ref, other_ref, feat_ref, part_ref, full_ref, mixed_ref
):
    blocks, rows, width = own_ref.shape
    for i, piece in enumerate((own_ref, other_ref)):
        core = place_ref[0] if i == 0 else 1 - place_ref[0]
        for b in range(blocks):
            full_ref[pl.ds(pl.multiple_of((2 * b + core) * rows, rows), rows), :] = piece[b]
    heads = width // (4 * HEAD)
    packed = nn(normed_ref[...], full_ref[:, : heads * 3 * HEAD])
    mixed = []
    for head in range(heads):
        query, keys, values = split_head(packed, head)
        weights = softmax(nt(query, keys) * HEAD ** (-0.5))
        mixed.append(nn(weights.astype(BF16), values))
    mixed_ref[...] = jnp.concatenate(mixed, axis=1)
    ways, shared = part_ref.shape[:2]
    outputs = full_ref.shape[0]
    per_block = BLOCK // shared
    for i in range(align_ref.shape[0]):
        first = pl.multiple_of(align_ref[i] * BLOCK, BLOCK)
        chosen = mixed_ref[pl.ds(first, BLOCK), :].astype(BF16)
        part = nt(chosen, full_ref[:, heads * 3 * HEAD :]).astype(BF16)
        for k in range(per_block):
            part_ref[i * per_block + k, :, :outputs] = part[k * shared : (k + 1) * shared]
    for i in range(ways):
        part_ref[i, :, outputs:] = feat_ref[...]


def assemble_kernel(ways, place_ref, own_ref, mine_ref, other_ref, proj_ref, whole_ref):
    features, columns = own_ref.shape
    half = features // 2
    first = pl.multiple_of(place_ref[0] * half, half)
    second = pl.multiple_of((1 - place_ref[0]) * half, half)
    proj_ref[place_ref[1]] = own_ref[...].T
    for k in range(1, ways):
        whole_ref[pl.ds(first, half), :] = mine_ref[k - 1]
        whole_ref[pl.ds(second, half), :] = other_ref[k - 1]
        proj_ref[place_ref[1 + k]] = whole_ref[...].T


def predict_kernel(feat_ref, proj_ref, pred_ref):
    ways, columns, features = proj_ref.shape
    for k in range(ways):
        pred_ref[:, k * columns : (k + 1) * columns] = nt(feat_ref[...], proj_ref[k])


def extra_kernel(shares, columns, place_ref, parts_ref, after_ref, extra_ref):
    features = extra_ref.shape[1] * columns
    rows = parts_ref.shape[0] * parts_ref.shape[1]
    feat = parts_ref[...].reshape(rows, parts_ref.shape[2])[:, -features:]
    shifted = [feat]
    for b in range(1, features // columns):
        shifted.append(jnp.concatenate([feat[:, b:], feat[:, :b]], 1))
    for half in range(2):
        core = place_ref[0] if half == 0 else 1 - place_ref[0]
        pick = pick_rows(features, shares, columns, core, True)
        for b in range(features // columns):
            extra_ref[half, b] = nt(pick, shifted[b]).astype(BF16)


def diff_kernel(
    clips, count_ref, place_ref, parts_ref, tokens_ref, pred_ref, proj_ref, out_ref
):
    rows, width = tokens_ref.shape
    ways, columns, features = proj_ref.shape
    branch = parts_ref[0, :, :width].astype(F32)
    for i in range(1, ways):
        branch = branch + parts_ref[i, :, :width].astype(F32)
    target = (tokens_ref[...].astype(F32) + branch).astype(BF16).astype(F32)
    count = count_ref[0]
    live = lax.broadcasted_iota(jnp.int32, (rows, 1), 0) + place_ref[1] * rows < count
    scale = jnp.full((1, 1), count, jnp.int32).astype(F32) * width
    factor = 2.0 / (scale * clips)
    diff = jnp.where(live, pred_ref[...] - target, 0.0)
    squares = jnp.sum(diff * diff, -1, keepdims=True) / scale
    dpred = (diff * factor).astype(BF16)
    dfeat = jnp.zeros((rows, features), F32)
    for k in range(ways):
        dfeat = dfeat + nn(dpred[:, k * columns : (k + 1) * columns], proj_ref[k])
    dfeat = dfeat.astype(BF16)
    high = squares.astype(BF16)
    rest = squares - high.astype(F32)
    middle = rest.astype(BF16)
    low = (rest - middle.astype(F32)).astype(BF16)
    lane = lax.broadcasted_iota(jnp.int32, (rows, BLOCK), 1)
    tail = jnp.where(lane == 0, high.astype(F32), jnp.where(lane == 1, middle.astype(F32), 0.0))
    tail = jnp.where(lane == 2, low.astype(F32), tail).astype(BF16)
    for i in range(ways):
        out_ref[i, :, :features] = dfeat
        out_ref[i, :, features : features + columns] = dpred[:, i * columns : (i + 1) * columns]
        out_ref[i, :, features + columns :] = tail


def backward_kernel(held, back_ref, feat_ref, *refs):
    sources, (keep_ref, send_ref, loss_ref) = refs[:held], refs[held : held + 3]
    copies = fetch(sources, refs[2 * held + 3 : -1], refs[-1])
    out_ref, packed_ref, weights_ref, mixed_ref, normed_ref, pick_ref = refs[2 * held + 3 : -1]
    copies[0].wait()
    features = out_ref.shape[1]
    heads = out_ref.shape[0] // HEAD
    dfeat = back_ref[:, :features]
    columns = back_ref.shape[1] - features - BLOCK
    dpred = back_ref[:, features : features + columns]
    tail = back_ref[:, features + columns :].astype(F32)
    loss_ref[...] = jnp.sum(jnp.sum(tail, 0, keepdims=True), 1, keepdims=True)
    dmixed = nt(dfeat, out_ref[...])
    for copy in copies[1:3]:
        copy.wait()
    packed = packed_ref[...].astype(F32)
    pieces = []
    for head in range(heads):
        query, keys, values = split_head(packed, head)
        rounded = weights_ref[head]
        weights = rounded.astype(F32)
        cot = dmixed[:, head * HEAD : (head + 1) * HEAD].astype(BF16)
        dvalues = tn(rounded, cot)
        dweights = nt(cot, values)
        inner = jnp.sum(dweights * weights, -1, keepdims=True)
        dscores = (weights * (dweights - inner) * HEAD ** (-0.5)).astype(BF16)
        pieces += [nn(dscores, keys), tn(dscores, query), dvalues]
    dpacked = jnp.concatenate(pieces, axis=1)
    used = dpacked.shape[1]
    length = dpacked.shape[0]
    right = jnp.concatenate([dpacked, jnp.zeros((length, features - used), F32)], 1).astype(BF16)
    for copy in copies[3:]:
        copy.wait()
    tailed = features - columns
    mixed = jnp.concatenate(
        [jnp.zeros((length, used - tailed), F32), mixed_ref[...].astype(F32)], 1
    ).astype(BF16)
    for half, into in enumerate((keep_ref, send_ref)):
        dfeat_rows = nt(pick_ref[half], dfeat).astype(BF16)
        normed_rows = normed_ref[half]
        for b in range(features // columns):
            block = slice(b * columns, (b + 1) * columns)
            total = nn(normed_rows, right[:, block]) + nn(feat_ref[half, b], dpred)
            if b == features // columns - 1:
                total = total + nn(dfeat_rows, mixed)
            into[:, block] = total.astype(BF16)


SWAP = [(0, 1), (1, 0)]


def from_peers(rows, axis, places=None):
    ways = lax.axis_size(axis)
    return [
        lax.ppermute(rows(k), axis, [(i, (i + k) % ways) for i in range(ways)])
        for k in (range(1, ways) if places is None else places)
    ]


def add(a, b):
    return a.astype(F32) + b.astype(F32)


def result_kernel(parts_ref, q_ref, o_ref, p_ref):
    each, used = q_ref.shape
    columns = p_ref.shape[1]
    total = jnp.sum(parts_ref[...].astype(F32), 0)
    q_ref[...] = total[:each, :used]
    o_ref[...] = total[:each, used:]
    for i in range(total.shape[0] - each):
        for b in range(total.shape[1] // columns):
            row = i * (total.shape[1] // columns) + b
            p_ref[row : row + 1] = total[each + i : each + i + 1, b * columns : (b + 1) * columns]


def on_device(
    teacher_clips, teacher_gain, teacher_qkv, teacher_out_t, event_tokens, valid_counts, alignment,
    student_qkv, student_out, projector,
):
    clip, events, align = teacher_clips[0], event_tokens[0], alignment[0]
    length, width = clip.shape
    features = events.shape[1]
    columns = projector.shape[1]
    ways = lax.axis_size("x")
    rows = length // ways
    own_c, own_x = lax.axis_index("c"), lax.axis_index("x")
    shares = 1
    for axis in CLIP:
        shares = shares * lax.axis_size(axis)

    senders = lax.axis_size("y") * lax.axis_size("z")
    shard = jnp.concatenate([teacher_qkv, teacher_out_t], 1)
    shard = jnp.broadcast_to(shard[None], (senders, *shard.shape))
    own_core = lax.all_to_all(shard, ("y", "z"), 0, 0)
    heads = student_out.shape[0] // HEAD
    each = features // shares
    picked = shares // 2 * (each + each * columns // features)
    places = jnp.stack([own_c] + [(own_x + k) % ways for k in range(ways)]).astype(jnp.int32)
    message_rows = rows * features // columns + features // 2
    half = features // 2
    proj_half = lax.dynamic_slice_in_dim(projector, own_c * half, half, 0)
    far = from_peers(lambda k: proj_half, "x", range(2, ways - 1))
    outs = pl.pallas_call(
        student_kernel,
        out_shape=(
            pltpu.HBM((rows, features), BF16),
            *[
                shape((message_rows, columns) if k in (1, ways - 1) else (rows, features), BF16)
                for k in range(1, ways)
            ],
            pltpu.HBM((length, features), BF16),
            pltpu.HBM((length, 3 * HEAD * heads), BF16),
            pltpu.HBM((length, HEAD * heads), BF16),
            pltpu.HBM((heads, length, length), BF16),
            *in_place([student_out]),
        ),
        in_specs=[SMEM] * 2 + [VMEM] * 4,
        out_specs=(pl.BlockSpec(),) + (VMEM,) * (ways - 1) + (pl.BlockSpec(),) * 5,
        scratch_shapes=[pltpu.VMEM((length, features), F32)],
        compiler_params=PARAMS,
        cost_estimate=cost(4),
        name="student_forward",
    )(valid_counts, places, events, student_qkv.T, student_out, projector)
    own_part, peer_parts = outs[0], outs[1:ways]
    normed, packed, mixed, weights, kept_out = outs[ways:]
    normed_rows, pick = pl.pallas_call(
        lambda *refs: picks_kernel(shares, columns, *refs),
        out_shape=(
            pltpu.HBM((2, picked, length), BF16), pltpu.HBM((2, picked, features), BF16),
        ),
        in_specs=[SMEM, VMEM, ANY],
        out_specs=(pl.BlockSpec(),) * 2,
        compiler_params=PARAMS,
        cost_estimate=cost(2),
        name="student_picks",
    )(places, normed, far[0])

    received = from_peers(lambda k: peer_parts[k - 1], "x") + far
    own_events = lax.dynamic_slice_in_dim(events, own_x * rows, rows, 0)
    feat_rows, proj_halves = pl.pallas_call(
        lambda *refs: rows_kernel(ways, *refs),
        out_shape=(
            shape((rows, features), BF16), shape((ways - 1, features // 2, columns), BF16),
            *in_place(received),
        ),
        in_specs=[ANY] * 2 + [HBM] * ways,
        out_specs=(VMEM,) * 2 + (HBM,) * ways,
        input_output_aliases={2 + k: 2 + k for k in range(ways)},
        scratch_shapes=buffers((own_events, own_part, *received)),
        compiler_params=PARAMS,
        cost_estimate=cost(1),
        name="student_rows",
    )(own_events, own_part, *received)[:2]
    own_core, feat_rows, proj_halves, normed_rows = lax.optimization_barrier(
        (own_core, feat_rows, proj_halves, normed_rows)
    )
    other_core = lax.ppermute(own_core, "c", SWAP)
    proj_others = lax.ppermute(proj_halves, "c", SWAP)
    teacher_normed = pl.pallas_call(
        teacher_norm_kernel,
        out_shape=shape((length, width), BF16),
        in_specs=[VMEM] * 2 + [ANY],
        out_specs=VMEM,
        compiler_params=PARAMS,
        cost_estimate=cost(1),
        name="teacher_norm",
    )(clip, teacher_gain.reshape(1, width), feat_rows)

    teacher_part = pl.pallas_call(
        teacher_kernel,
        out_shape=shape((ways, rows, width + features), BF16),
        in_specs=[SMEM] * 2 + [VMEM] * 4,
        out_specs=VMEM,
        scratch_shapes=[
            pltpu.VMEM((senders * 2 * shard.shape[1], shard.shape[2]), BF16),
            pltpu.VMEM((length, teacher_out_t.shape[1]), F32),
        ],
        compiler_params=PARAMS,
        cost_estimate=cost(5),
        name="teacher",
    )(places, align, teacher_normed, own_core, other_core, feat_rows)

    teacher_parts = lax.all_to_all(teacher_part, "x", 0, 0)
    per_block = BLOCK // rows
    source = align[own_x // per_block] * BLOCK + own_x % per_block * rows
    own_tokens = lax.dynamic_slice_in_dim(clip, source, rows, 0)
    sources = jnp.stack([own_c] + [(own_x - k + ways) % ways for k in range(ways)]).astype(jnp.int32)
    whole_proj = pl.pallas_call(
        lambda *refs: assemble_kernel(ways, *refs),
        out_shape=pltpu.HBM((ways, columns, features), BF16),
        in_specs=[SMEM] + [VMEM] * 3,
        out_specs=pl.BlockSpec(),
        scratch_shapes=[pltpu.VMEM((features, columns), BF16)],
        compiler_params=PARAMS,
        cost_estimate=cost(1),
        name="projector",
    )(sources, projector, proj_halves, proj_others)
    pred = pl.pallas_call(
        predict_kernel,
        out_shape=shape((rows, width), F32),
        in_specs=[VMEM] * 2,
        out_specs=VMEM,
        compiler_params=PARAMS,
        cost_estimate=cost(2),
        name="student_predict",
    )(feat_rows, whole_proj)
    message = pl.pallas_call(
        lambda *refs: diff_kernel(shares, *refs),
        out_shape=shape((ways, rows, features + columns + BLOCK), BF16),
        in_specs=[SMEM] * 2 + [VMEM] * 4,
        out_specs=VMEM,
        compiler_params=PARAMS,
        cost_estimate=cost(2),
        name="difference",
    )(valid_counts, sources, teacher_parts, own_tokens, pred, whole_proj)
    feat_extra = pl.pallas_call(
        lambda *refs: extra_kernel(shares, columns, *refs),
        out_shape=shape((2, features // columns, picked, length), BF16),
        in_specs=[SMEM, VMEM, ANY],
        out_specs=VMEM,
        compiler_params=PARAMS,
        cost_estimate=cost(3),
        name="student_extra",
    )(sources, teacher_parts, message)
    back = lax.all_to_all(message, "x", 0, 0).reshape(length, features + columns + BLOCK)

    held = (kept_out, packed, weights, mixed, normed_rows, pick)
    keep, send, loss = pl.pallas_call(
        lambda *refs: backward_kernel(len(held), *refs),
        out_shape=(
            shape((picked, features), BF16), shape((picked, features), BF16), shape((1, 1), F32),
            *in_place(held),
        ),
        in_specs=[VMEM] * 2 + [HBM] * len(held),
        out_specs=(VMEM,) * 3 + (HBM,) * len(held),
        scratch_shapes=buffers(held),
        input_output_aliases={2 + i: 3 + i for i in range(len(held))},
        compiler_params=PARAMS,
        cost_estimate=cost(4),
        name="student_backward",
    )(back, feat_extra, *held)[:3]

    total = add(keep, lax.ppermute(send, "c", SWAP)).astype(BF16)
    chips = shares // 2
    spread = lax.all_to_all(
        total.reshape(chips, total.shape[0] // chips, features), CLIP[:3], 0, 0
    )
    used = 3 * HEAD * heads
    grad_q, grad_o, grad_p = pl.pallas_call(
        result_kernel,
        out_shape=(
            shape((each, used), F32), shape((each, HEAD * heads), F32), shape((each, columns), F32),
        ),
        in_specs=[VMEM],
        out_specs=(VMEM,) * 3,
        compiler_params=PARAMS,
        cost_estimate=cost(1),
        name="gradient_rows",
    )(spread)
    return loss.reshape(1), grad_q, grad_o.T, grad_p


def solution(mesh):
    group, dp, tensor = mesh.devices.shape
    fine = Mesh(mesh.devices.reshape(group, 4, dp // 8, 2, tensor), (*CLIP, "x"))
    dp = CLIP[1:]
    in_specs = (
        P(CLIP, None, None), P(), P(dp, "x"), P(dp, "x"), P(CLIP, None, None), P(CLIP), P(CLIP, None),
        P(None, "x"), P("x", None), P(None, "x"),
    )
    out_specs = (P(CLIP), P(CLIP, "x"), P("x", CLIP), P(CLIP, "x"))
    return jax.shard_map(
        on_device, mesh=fine, in_specs=in_specs, out_specs=out_specs, check_vma=False
    )
```

```python
import jax
import jax.numpy as jnp
from jax import lax
from jax.experimental import pallas as pl
from jax.experimental.pallas import tpu as pltpu
from jax.sharding import Mesh, PartitionSpec as P

HEAD = 64
BLOCK = 128
F32 = jnp.float32
BF16 = jnp.bfloat16
CLIP = ("g", "y", "z", "c")
ANY = pl.BlockSpec(memory_space=pl.ANY)
HBM = pl.BlockSpec(memory_space=pltpu.HBM)
VMEM = pl.BlockSpec(memory_space=pltpu.VMEM)
SMEM = pl.BlockSpec(memory_space=pltpu.SMEM)
PARAMS = pltpu.CompilerParams(vmem_limit_bytes=20 * 1024 * 1024)


def cost(microseconds):
    return pl.CostEstimate(flops=microseconds * 10**9, bytes_accessed=10**6, transcendentals=0)


def fetch(sources, buffers, sems):
    copies = [
        pltpu.make_async_copy(source, buffer, sems.at[i])
        for i, (source, buffer) in enumerate(zip(sources, buffers))
    ]
    for copy in copies:
        copy.start()
    return copies


def buffers(arrays):
    return [pltpu.VMEM(array.shape, array.dtype) for array in arrays] + [
        pltpu.SemaphoreType.DMA((len(arrays),))
    ]


def in_place(arrays):
    return [pltpu.HBM(array.shape, array.dtype) for array in arrays]


def shape(dims, dtype):
    return jax.ShapeDtypeStruct(dims, dtype)


def nn(a, b):
    return lax.dot_general(a, b, (((1,), (0,)), ((), ())), preferred_element_type=F32)


def nt(a, b):
    return lax.dot_general(a, b, (((1,), (1,)), ((), ())), preferred_element_type=F32)


def tn(a, b):
    return lax.dot_general(a, b, (((0,), (0,)), ((), ())), preferred_element_type=F32)


def norm_rows(rows):
    rows = rows.astype(F32)
    centre = rows - jnp.mean(rows, -1, keepdims=True)
    spread = jnp.mean(centre * centre, -1, keepdims=True)
    return centre * lax.rsqrt(spread + 1e-05)


def split_head(packed, head):
    first = head * 3 * HEAD
    return [packed[:, first + i * HEAD : first + (i + 1) * HEAD] for i in range(3)]


def exponentials(scores):
    weights = jnp.exp(scores - jnp.max(scores, -1, keepdims=True))
    return weights, 1.0 / jnp.sum(weights, -1, keepdims=True)


def pick_rows(rows, shares, columns, core, extra):
    each = rows // shares
    block = each + each * columns // rows
    place = lax.broadcasted_iota(jnp.int32, (shares // 2 * block, 1), 0)
    chip, row = place // block, place % block
    base = (chip * 2 + core) * each
    if extra:
        wanted = jnp.where(row >= each, base + (row - each) * (rows // columns), -1)
    else:
        wanted = jnp.where(row < each, base + row, -1)
    source = lax.broadcasted_iota(jnp.int32, (shares // 2 * block, rows), 1)
    return jnp.where(source == wanted, 1.0, 0.0).astype(BF16)


def picks_kernel(shares, columns, place_ref, normed_ref, after_ref, rows_ref, pick_ref):
    features = pick_ref.shape[2]
    for half in range(2):
        core = place_ref[0] if half == 0 else 1 - place_ref[0]
        pick_ref[half] = pick_rows(features, shares, columns, core, False)
        rows_ref[half] = nt(pick_ref[half], normed_ref[...]).astype(BF16)


def student_kernel(count_ref, place_ref, events_ref, qkv_ref, out_ref, proj_ref, *refs):
    ways = len(refs) - 6
    own_ref, peer_refs = refs[0], refs[1:ways]
    normed_ref, packed_ref, mixed_ref, weights_ref, kept_ref, part_ref = refs[ways:]
    kept_ref[...] = out_ref[...]
    columns = proj_ref.shape[1]
    length, features = events_ref.shape
    heads = out_ref.shape[0] // HEAD
    normed = norm_rows(events_ref[...]).astype(BF16)
    normed_ref[...] = normed
    packed = nt(normed, qkv_ref[...]).astype(BF16)
    packed_ref[...] = packed
    usable = lax.broadcasted_iota(jnp.int32, (length, length), 1) < count_ref[0]
    mixed = []
    for head in range(heads):
        query, keys, values = split_head(packed, head)
        scores = jnp.where(usable, nt(query, keys) * HEAD ** (-0.5), -1e30)
        weights, share = exponentials(scores)
        weights = (weights * share).astype(BF16)
        weights_ref[head] = weights
        mixed.append(nn(weights, values))
    mixed = jnp.concatenate(mixed, axis=1).astype(BF16)
    mixed_ref[...] = mixed
    part_ref[...] = nn(mixed, out_ref[...])
    rows = own_ref.shape[0]
    half = features // 2
    blocks = features // columns
    proj_half = proj_ref[pl.ds(pl.multiple_of(place_ref[0] * half, half), half), :]
    for k in range(ways):
        first = pl.multiple_of(place_ref[1 + k] * rows, rows)
        chosen = part_ref[pl.ds(first, rows), :].astype(BF16)
        if k not in (1, ways - 1):
            (own_ref if k == 0 else peer_refs[k - 1])[...] = chosen
            continue
        for b in range(blocks):
            peer_refs[k - 1][b * rows : (b + 1) * rows] = chosen[:, b * columns : (b + 1) * columns]
        peer_refs[k - 1][blocks * rows :] = proj_half


def rows_kernel(ways, *refs):
    sources, (feat_ref, proj_ref), held = refs[: ways + 2], refs[ways + 2 : ways + 4], refs[-ways - 3 : -1]
    for copy in fetch(sources, held, refs[-1]):
        copy.wait()
    events_ref, own_ref, before_ref, opposite_ref, behind_ref, far_ref = held
    rows, features = own_ref.shape
    columns = proj_ref.shape[2]
    blocks = features // columns
    for b in range(blocks):
        lanes = slice(b * columns, (b + 1) * columns)
        branch = own_ref[:, lanes].astype(F32) + opposite_ref[:, lanes].astype(F32)
        for peer in (before_ref, behind_ref):
            branch = branch + peer[b * rows : (b + 1) * rows].astype(F32)
        feat_ref[:, lanes] = (events_ref[:, lanes].astype(F32) + branch).astype(BF16)
    proj_ref[0] = before_ref[blocks * rows :]
    proj_ref[1] = far_ref[...]
    proj_ref[2] = behind_ref[blocks * rows :]


def teacher_norm_kernel(clip_ref, gain_ref, after_ref, normed_ref):
    normed_ref[...] = (norm_rows(clip_ref[...]) * gain_ref[...]).astype(BF16)


def teacher_kernel(
    place_ref, align_ref, normed_ref, own_ref, other_ref, feat_ref, part_ref, full_ref, mixed_ref
):
    blocks, rows, width = own_ref.shape
    for i, piece in enumerate((own_ref, other_ref)):
        core = place_ref[0] if i == 0 else 1 - place_ref[0]
        for b in range(blocks):
            full_ref[pl.ds(pl.multiple_of((2 * b + core) * rows, rows), rows), :] = piece[b]
    heads = width // (4 * HEAD)
    packed = nn(normed_ref[...], full_ref[:, : heads * 3 * HEAD]).astype(BF16)
    mixed = []
    for head in range(heads):
        query, keys, values = split_head(packed, head)
        weights, share = exponentials(nt(query, keys) * HEAD ** (-0.5))
        mixed.append(nn(weights.astype(BF16), values) * share)
    mixed_ref[...] = jnp.concatenate(mixed, axis=1)
    ways, shared = part_ref.shape[:2]
    outputs = full_ref.shape[0]
    per_block = BLOCK // shared
    for i in range(align_ref.shape[0]):
        first = pl.multiple_of(align_ref[i] * BLOCK, BLOCK)
        chosen = mixed_ref[pl.ds(first, BLOCK), :].astype(BF16)
        part = nt(chosen, full_ref[:, heads * 3 * HEAD :]).astype(BF16)
        for k in range(per_block):
            part_ref[i * per_block + k, :, :outputs] = part[k * shared : (k + 1) * shared]
    for i in range(ways):
        part_ref[i, :, outputs:] = feat_ref[...]


def assemble_kernel(ways, place_ref, own_ref, mine_ref, other_ref, proj_ref, whole_ref):
    features, columns = own_ref.shape
    half = features // 2
    first = pl.multiple_of(place_ref[0] * half, half)
    second = pl.multiple_of((1 - place_ref[0]) * half, half)
    proj_ref[place_ref[1]] = own_ref[...].T
    for k in range(1, ways):
        whole_ref[pl.ds(first, half), :] = mine_ref[k - 1]
        whole_ref[pl.ds(second, half), :] = other_ref[k - 1]
        proj_ref[place_ref[1 + k]] = whole_ref[...].T


def predict_kernel(feat_ref, proj_ref, pred_ref):
    ways, columns, features = proj_ref.shape
    for k in range(ways):
        pred_ref[:, k * columns : (k + 1) * columns] = nt(feat_ref[...], proj_ref[k])


def extra_kernel(shares, columns, place_ref, parts_ref, after_ref, extra_ref):
    features = extra_ref.shape[1] * columns
    rows = parts_ref.shape[0] * parts_ref.shape[1]
    feat = parts_ref[...].reshape(rows, parts_ref.shape[2])[:, -features:]
    shifted = [feat]
    for b in range(1, features // columns):
        shifted.append(jnp.concatenate([feat[:, b:], feat[:, :b]], 1))
    for half in range(2):
        core = place_ref[0] if half == 0 else 1 - place_ref[0]
        pick = pick_rows(features, shares, columns, core, True)
        for b in range(features // columns):
            extra_ref[half, b] = nt(pick, shifted[b]).astype(BF16)


def diff_kernel(
    clips, count_ref, place_ref, parts_ref, tokens_ref, pred_ref, proj_ref, out_ref
):
    rows, width = tokens_ref.shape
    ways, columns, features = proj_ref.shape
    branch = parts_ref[0, :, :width].astype(F32)
    for i in range(1, ways):
        branch = branch + parts_ref[i, :, :width].astype(F32)
    target = (tokens_ref[...].astype(F32) + branch).astype(BF16).astype(F32)
    count = count_ref[0]
    live = lax.broadcasted_iota(jnp.int32, (rows, 1), 0) + place_ref[1] * rows < count
    scale = jnp.full((1, 1), count, jnp.int32).astype(F32) * width
    factor = 2.0 / (scale * clips)
    diff = jnp.where(live, pred_ref[...] - target, 0.0)
    squares = jnp.sum(diff * diff, -1, keepdims=True) / scale
    dpred = (diff * factor).astype(BF16)
    dfeat = jnp.zeros((rows, features), F32)
    for k in range(ways):
        dfeat = dfeat + nn(dpred[:, k * columns : (k + 1) * columns], proj_ref[k])
    dfeat = dfeat.astype(BF16)
    high = squares.astype(BF16)
    rest = squares - high.astype(F32)
    middle = rest.astype(BF16)
    low = (rest - middle.astype(F32)).astype(BF16)
    lane = lax.broadcasted_iota(jnp.int32, (rows, BLOCK), 1)
    tail = jnp.where(lane == 0, high.astype(F32), jnp.where(lane == 1, middle.astype(F32), 0.0))
    tail = jnp.where(lane == 2, low.astype(F32), tail).astype(BF16)
    for i in range(ways):
        out_ref[i, :, :features] = dfeat
        out_ref[i, :, features : features + columns] = dpred[:, i * columns : (i + 1) * columns]
        out_ref[i, :, features + columns :] = tail


def backward_kernel(held, back_ref, feat_ref, *refs):
    sources, (keep_ref, send_ref, loss_ref) = refs[:held], refs[held : held + 3]
    copies = fetch(sources, refs[2 * held + 3 : -1], refs[-1])
    out_ref, packed_ref, weights_ref, mixed_ref, normed_ref, pick_ref = refs[2 * held + 3 : -1]
    features = out_ref.shape[1]
    heads = out_ref.shape[0] // HEAD
    dfeat = back_ref[:, :features]
    columns = back_ref.shape[1] - features - BLOCK
    dpred = back_ref[:, features : features + columns]
    tail = back_ref[:, features + columns :].astype(F32)
    loss_ref[...] = jnp.sum(jnp.sum(tail, 0, keepdims=True), 1, keepdims=True)
    copies[0].wait()
    dmixed = nt(dfeat, out_ref[...]).astype(BF16)
    for copy in copies[1:3]:
        copy.wait()
    packed = packed_ref[...]
    pieces = []
    for head in range(heads):
        query, keys, values = split_head(packed, head)
        rounded = weights_ref[head]
        weights = rounded.astype(F32)
        cot = dmixed[:, head * HEAD : (head + 1) * HEAD]
        dvalues = tn(rounded, cot)
        dweights = nt(cot, values)
        inner = jnp.sum(dweights * weights, -1, keepdims=True)
        dscores = (weights * (dweights - inner) * HEAD ** (-0.5)).astype(BF16)
        pieces += [piece.astype(BF16) for piece in (nn(dscores, keys), tn(dscores, query), dvalues)]
    dpacked = jnp.concatenate(pieces, axis=1)
    used = dpacked.shape[1]
    length = dpacked.shape[0]
    right = jnp.concatenate([dpacked, jnp.zeros((length, features - used), BF16)], 1)
    for copy in copies[3:]:
        copy.wait()
    tailed = features - columns
    mixed = jnp.concatenate([jnp.zeros((length, used - tailed), BF16), mixed_ref[...]], 1)
    for half, into in enumerate((keep_ref, send_ref)):
        dfeat_rows = nt(pick_ref[half], dfeat).astype(BF16)
        normed_rows = normed_ref[half]
        for b in range(features // columns):
            block = slice(b * columns, (b + 1) * columns)
            total = nn(normed_rows, right[:, block]) + nn(feat_ref[half, b], dpred)
            if b == features // columns - 1:
                total = total + nn(dfeat_rows, mixed)
            into[:, block] = total.astype(BF16)


SWAP = [(0, 1), (1, 0)]


def from_peers(rows, axis, places=None):
    ways = lax.axis_size(axis)
    return [
        lax.ppermute(rows(k), axis, [(i, (i + k) % ways) for i in range(ways)])
        for k in (range(1, ways) if places is None else places)
    ]


def add(a, b):
    return a.astype(F32) + b.astype(F32)


def result_kernel(parts_ref, q_ref, o_ref, p_ref):
    each, used = q_ref.shape
    columns = p_ref.shape[1]
    total = jnp.sum(parts_ref[...].astype(F32), 0)
    q_ref[...] = total[:each, :used]
    o_ref[...] = total[:each, used:]
    for i in range(total.shape[0] - each):
        for b in range(total.shape[1] // columns):
            row = i * (total.shape[1] // columns) + b
            p_ref[row : row + 1] = total[each + i : each + i + 1, b * columns : (b + 1) * columns]


def on_device(
    teacher_clips, teacher_gain, teacher_qkv, teacher_out_t, event_tokens, valid_counts, alignment,
    student_qkv, student_out, projector,
):
    clip, events, align = teacher_clips[0], event_tokens[0], alignment[0]
    length, width = clip.shape
    features = events.shape[1]
    columns = projector.shape[1]
    ways = lax.axis_size("x")
    rows = length // ways
    own_c, own_x = lax.axis_index("c"), lax.axis_index("x")
    shares = 1
    for axis in CLIP:
        shares = shares * lax.axis_size(axis)

    senders = lax.axis_size("y") * lax.axis_size("z")
    shard = jnp.concatenate([teacher_qkv, teacher_out_t], 1)
    shard = jnp.broadcast_to(shard[None], (senders, *shard.shape))
    own_core = lax.all_to_all(shard, ("y", "z"), 0, 0)
    heads = student_out.shape[0] // HEAD
    each = features // shares
    picked = shares // 2 * (each + each * columns // features)
    places = jnp.stack([own_c] + [(own_x + k) % ways for k in range(ways)]).astype(jnp.int32)
    message_rows = rows * features // columns + features // 2
    half = features // 2
    proj_half = lax.dynamic_slice_in_dim(projector, own_c * half, half, 0)
    far = from_peers(lambda k: proj_half, "x", range(2, ways - 1))
    outs = pl.pallas_call(
        student_kernel,
        out_shape=(
            pltpu.HBM((rows, features), BF16),
            *[
                shape((message_rows, columns) if k in (1, ways - 1) else (rows, features), BF16)
                for k in range(1, ways)
            ],
            pltpu.HBM((length, features), BF16),
            pltpu.HBM((length, 3 * HEAD * heads), BF16),
            pltpu.HBM((length, HEAD * heads), BF16),
            pltpu.HBM((heads, length, length), BF16),
            *in_place([student_out]),
        ),
        in_specs=[SMEM] * 2 + [VMEM] * 4,
        out_specs=(pl.BlockSpec(),) + (VMEM,) * (ways - 1) + (pl.BlockSpec(),) * 5,
        scratch_shapes=[pltpu.VMEM((length, features), F32)],
        compiler_params=PARAMS,
        cost_estimate=cost(4),
        name="student_forward",
    )(valid_counts, places, events, student_qkv.T, student_out, projector)
    own_part, peer_parts = outs[0], outs[1:ways]
    normed, packed, mixed, weights, kept_out = outs[ways:]
    normed_rows, pick = pl.pallas_call(
        lambda *refs: picks_kernel(shares, columns, *refs),
        out_shape=(
            pltpu.HBM((2, picked, length), BF16), pltpu.HBM((2, picked, features), BF16),
        ),
        in_specs=[SMEM, VMEM, ANY],
        out_specs=(pl.BlockSpec(),) * 2,
        compiler_params=PARAMS,
        cost_estimate=cost(2),
        name="student_picks",
    )(places, normed, far[0])

    received = from_peers(lambda k: peer_parts[k - 1], "x") + far
    own_events = lax.dynamic_slice_in_dim(events, own_x * rows, rows, 0)
    feat_rows, proj_halves = pl.pallas_call(
        lambda *refs: rows_kernel(ways, *refs),
        out_shape=(
            shape((rows, features), BF16), shape((ways - 1, features // 2, columns), BF16),
            *in_place(received),
        ),
        in_specs=[ANY] * 2 + [HBM] * ways,
        out_specs=(VMEM,) * 2 + (HBM,) * ways,
        input_output_aliases={2 + k: 2 + k for k in range(ways)},
        scratch_shapes=buffers((own_events, own_part, *received)),
        compiler_params=PARAMS,
        cost_estimate=cost(1),
        name="student_rows",
    )(own_events, own_part, *received)[:2]
    own_core, feat_rows, proj_halves, normed_rows = lax.optimization_barrier(
        (own_core, feat_rows, proj_halves, normed_rows)
    )
    other_core = lax.ppermute(own_core, "c", SWAP)
    proj_others = lax.ppermute(proj_halves, "c", SWAP)
    teacher_normed = pl.pallas_call(
        teacher_norm_kernel,
        out_shape=shape((length, width), BF16),
        in_specs=[VMEM] * 2 + [ANY],
        out_specs=VMEM,
        compiler_params=PARAMS,
        cost_estimate=cost(1),
        name="teacher_norm",
    )(clip, teacher_gain.reshape(1, width), feat_rows)

    teacher_part = pl.pallas_call(
        teacher_kernel,
        out_shape=shape((ways, rows, width + features), BF16),
        in_specs=[SMEM] * 2 + [VMEM] * 4,
        out_specs=VMEM,
        scratch_shapes=[
            pltpu.VMEM((senders * 2 * shard.shape[1], shard.shape[2]), BF16),
            pltpu.VMEM((length, teacher_out_t.shape[1]), F32),
        ],
        compiler_params=PARAMS,
        cost_estimate=cost(5),
        name="teacher",
    )(places, align, teacher_normed, own_core, other_core, feat_rows)

    teacher_parts = lax.all_to_all(teacher_part, "x", 0, 0)
    per_block = BLOCK // rows
    source = align[own_x // per_block] * BLOCK + own_x % per_block * rows
    own_tokens = lax.dynamic_slice_in_dim(clip, source, rows, 0)
    sources = jnp.stack([own_c] + [(own_x - k + ways) % ways for k in range(ways)]).astype(jnp.int32)
    whole_proj = pl.pallas_call(
        lambda *refs: assemble_kernel(ways, *refs),
        out_shape=pltpu.HBM((ways, columns, features), BF16),
        in_specs=[SMEM] + [VMEM] * 3,
        out_specs=pl.BlockSpec(),
        scratch_shapes=[pltpu.VMEM((features, columns), BF16)],
        compiler_params=PARAMS,
        cost_estimate=cost(1),
        name="projector",
    )(sources, projector, proj_halves, proj_others)
    pred = pl.pallas_call(
        predict_kernel,
        out_shape=shape((rows, width), F32),
        in_specs=[VMEM] * 2,
        out_specs=VMEM,
        compiler_params=PARAMS,
        cost_estimate=cost(2),
        name="student_predict",
    )(feat_rows, whole_proj)
    message = pl.pallas_call(
        lambda *refs: diff_kernel(shares, *refs),
        out_shape=shape((ways, rows, features + columns + BLOCK), BF16),
        in_specs=[SMEM] * 2 + [VMEM] * 4,
        out_specs=VMEM,
        compiler_params=PARAMS,
        cost_estimate=cost(2),
        name="difference",
    )(valid_counts, sources, teacher_parts, own_tokens, pred, whole_proj)
    feat_extra = pl.pallas_call(
        lambda *refs: extra_kernel(shares, columns, *refs),
        out_shape=shape((2, features // columns, picked, length), BF16),
        in_specs=[SMEM, VMEM, ANY],
        out_specs=VMEM,
        compiler_params=PARAMS,
        cost_estimate=cost(3),
        name="student_extra",
    )(sources, teacher_parts, message)
    back = lax.all_to_all(message, "x", 0, 0).reshape(length, features + columns + BLOCK)

    held = (kept_out, packed, weights, mixed, normed_rows, pick)
    keep, send, loss = pl.pallas_call(
        lambda *refs: backward_kernel(len(held), *refs),
        out_shape=(
            shape((picked, features), BF16), shape((picked, features), BF16), shape((1, 1), F32),
            *in_place(held),
        ),
        in_specs=[VMEM] * 2 + [HBM] * len(held),
        out_specs=(VMEM,) * 3 + (HBM,) * len(held),
        scratch_shapes=buffers(held),
        input_output_aliases={2 + i: 3 + i for i in range(len(held))},
        compiler_params=PARAMS,
        cost_estimate=cost(4),
        name="student_backward",
    )(back, feat_extra, *held)[:3]

    total = add(keep, lax.ppermute(send, "c", SWAP)).astype(BF16)
    chips = shares // 2
    spread = lax.all_to_all(
        total.reshape(chips, total.shape[0] // chips, features), CLIP[:3], 0, 0
    )
    used = 3 * HEAD * heads
    grad_q, grad_o, grad_p = pl.pallas_call(
        result_kernel,
        out_shape=(
            shape((each, used), F32), shape((each, HEAD * heads), F32), shape((each, columns), F32),
        ),
        in_specs=[VMEM],
        out_specs=(VMEM,) * 3,
        compiler_params=PARAMS,
        cost_estimate=cost(1),
        name="gradient_rows",
    )(spread)
    return loss.reshape(1), grad_q, grad_o.T, grad_p


def solution(mesh):
    group, dp, tensor = mesh.devices.shape
    fine = Mesh(mesh.devices.reshape(group, 4, dp // 8, 2, tensor), (*CLIP, "x"))
    dp = CLIP[1:]
    in_specs = (
        P(CLIP, None, None), P(), P(dp, "x"), P(dp, "x"), P(CLIP, None, None), P(CLIP), P(CLIP, None),
        P(None, "x"), P("x", None), P(None, "x"),
    )
    out_specs = (P(CLIP), P(CLIP, "x"), P("x", CLIP), P(CLIP, "x"))
    return jax.shard_map(
        on_device, mesh=fine, in_specs=in_specs, out_specs=out_specs, check_vma=False
    )
```

```python
import jax
import jax.numpy as jnp
from jax import lax
from jax.experimental import pallas as pl
from jax.experimental.pallas import tpu as pltpu
from jax.sharding import Mesh, PartitionSpec as P

HEAD = 64
BLOCK = 128
F32 = jnp.float32
BF16 = jnp.bfloat16
CLIP = ("g", "y", "z", "c")
ANY = pl.BlockSpec(memory_space=pl.ANY)
HBM = pl.BlockSpec(memory_space=pltpu.HBM)
VMEM = pl.BlockSpec(memory_space=pltpu.VMEM)
SMEM = pl.BlockSpec(memory_space=pltpu.SMEM)
PARAMS = pltpu.CompilerParams(vmem_limit_bytes=20 * 1024 * 1024)


def cost(microseconds):
    return pl.CostEstimate(flops=microseconds * 10**9, bytes_accessed=10**6, transcendentals=0)


def fetch(sources, buffers, sems):
    copies = [
        pltpu.make_async_copy(source, buffer, sems.at[i])
        for i, (source, buffer) in enumerate(zip(sources, buffers))
    ]
    for copy in copies:
        copy.start()
    return copies


def buffers(arrays):
    return [pltpu.VMEM(array.shape, array.dtype) for array in arrays] + [
        pltpu.SemaphoreType.DMA((len(arrays),))
    ]


def in_place(arrays):
    return [pltpu.HBM(array.shape, array.dtype) for array in arrays]


def shape(dims, dtype):
    return jax.ShapeDtypeStruct(dims, dtype)


def nn(a, b):
    return lax.dot_general(a, b, (((1,), (0,)), ((), ())), preferred_element_type=F32)


def nt(a, b):
    return lax.dot_general(a, b, (((1,), (1,)), ((), ())), preferred_element_type=F32)


def tn(a, b):
    return lax.dot_general(a, b, (((0,), (0,)), ((), ())), preferred_element_type=F32)


def norm_rows(rows):
    rows = rows.astype(F32)
    centre = rows - jnp.mean(rows, -1, keepdims=True)
    spread = jnp.mean(centre * centre, -1, keepdims=True)
    return centre * lax.rsqrt(spread + 1e-05)


def split_head(packed, head):
    first = head * 3 * HEAD
    return [packed[:, first + i * HEAD : first + (i + 1) * HEAD] for i in range(3)]


def exponentials(scores):
    weights = jnp.exp(scores - jnp.max(scores, -1, keepdims=True))
    return weights, 1.0 / jnp.sum(weights, -1, keepdims=True)


def pick_rows(rows, shares, columns, core, extra):
    each = rows // shares
    block = each + each * columns // rows
    place = lax.broadcasted_iota(jnp.int32, (shares // 2 * block, 1), 0)
    chip, row = place // block, place % block
    base = (chip * 2 + core) * each
    if extra:
        wanted = jnp.where(row >= each, base + (row - each) * (rows // columns), -1)
    else:
        wanted = jnp.where(row < each, base + row, -1)
    source = lax.broadcasted_iota(jnp.int32, (shares // 2 * block, rows), 1)
    return jnp.where(source == wanted, 1.0, 0.0).astype(BF16)


def picks_kernel(shares, columns, place_ref, normed_ref, after_ref, rows_ref, pick_ref):
    features = pick_ref.shape[2]
    for half in range(2):
        core = place_ref[0] if half == 0 else 1 - place_ref[0]
        pick_ref[half] = pick_rows(features, shares, columns, core, False)
        rows_ref[half] = nt(pick_ref[half], normed_ref[...]).astype(BF16)


def student_kernel(count_ref, place_ref, events_ref, qkv_ref, out_ref, proj_ref, *refs):
    ways = len(refs) - 6
    own_ref, peer_refs = refs[0], refs[1:ways]
    normed_ref, packed_ref, mixed_ref, weights_ref, kept_ref, part_ref = refs[ways:]
    kept_ref[...] = out_ref[...]
    columns = proj_ref.shape[1]
    length, features = events_ref.shape
    heads = out_ref.shape[0] // HEAD
    normed = norm_rows(events_ref[...]).astype(BF16)
    normed_ref[...] = normed
    packed = nt(normed, qkv_ref[...]).astype(BF16)
    packed_ref[...] = packed
    usable = lax.broadcasted_iota(jnp.int32, (length, length), 1) < count_ref[0]
    mixed = []
    for head in range(heads):
        query, keys, values = split_head(packed, head)
        scores = jnp.where(usable, nt(query, keys) * HEAD ** (-0.5), -1e30)
        weights, share = exponentials(scores)
        weights = (weights * share).astype(BF16)
        weights_ref[head] = weights
        mixed.append(nn(weights, values))
    mixed = jnp.concatenate(mixed, axis=1).astype(BF16)
    mixed_ref[...] = mixed
    part_ref[...] = nn(mixed, out_ref[...])
    rows = own_ref.shape[0]
    half = features // 2
    blocks = features // columns
    proj_half = proj_ref[pl.ds(pl.multiple_of(place_ref[0] * half, half), half), :]
    for k in range(ways):
        first = pl.multiple_of(place_ref[1 + k] * rows, rows)
        chosen = part_ref[pl.ds(first, rows), :].astype(BF16)
        if k not in (1, ways - 1):
            (own_ref if k == 0 else peer_refs[k - 1])[...] = chosen
            continue
        for b in range(blocks):
            peer_refs[k - 1][b * rows : (b + 1) * rows] = chosen[:, b * columns : (b + 1) * columns]
        peer_refs[k - 1][blocks * rows :] = proj_half


def rows_kernel(ways, *refs):
    sources, (feat_ref, proj_ref), held = refs[: ways + 2], refs[ways + 2 : ways + 4], refs[-ways - 3 : -1]
    for copy in fetch(sources, held, refs[-1]):
        copy.wait()
    events_ref, own_ref, before_ref, opposite_ref, behind_ref, far_ref = held
    rows, features = own_ref.shape
    columns = proj_ref.shape[2]
    blocks = features // columns
    for b in range(blocks):
        lanes = slice(b * columns, (b + 1) * columns)
        branch = own_ref[:, lanes].astype(F32) + opposite_ref[:, lanes].astype(F32)
        for peer in (before_ref, behind_ref):
            branch = branch + peer[b * rows : (b + 1) * rows].astype(F32)
        feat_ref[:, lanes] = (events_ref[:, lanes].astype(F32) + branch).astype(BF16)
    proj_ref[0] = before_ref[blocks * rows :]
    proj_ref[1] = far_ref[...]
    proj_ref[2] = behind_ref[blocks * rows :]


def teacher_norm_kernel(clip_ref, gain_ref, after_ref, normed_ref):
    normed_ref[...] = (norm_rows(clip_ref[...]) * gain_ref[...]).astype(BF16)


def teacher_kernel(
    place_ref, align_ref, normed_ref, own_ref, other_ref, feat_ref, part_ref, full_ref, mixed_ref
):
    blocks, rows, width = own_ref.shape
    for i, piece in enumerate((own_ref, other_ref)):
        core = place_ref[0] if i == 0 else 1 - place_ref[0]
        for b in range(blocks):
            full_ref[pl.ds(pl.multiple_of((2 * b + core) * rows, rows), rows), :] = piece[b]
    heads = width // (4 * HEAD)
    packed = nn(normed_ref[...], full_ref[:, : heads * 3 * HEAD]).astype(BF16)
    mixed = []
    for head in range(heads):
        query, keys, values = split_head(packed, head)
        weights, share = exponentials(nt(query, keys) * HEAD ** (-0.5))
        mixed.append(nn(weights.astype(BF16), values) * share)
    mixed_ref[...] = jnp.concatenate(mixed, axis=1)
    ways, shared = part_ref.shape[:2]
    outputs = full_ref.shape[0]
    per_block = BLOCK // shared
    for i in range(align_ref.shape[0]):
        first = pl.multiple_of(align_ref[i] * BLOCK, BLOCK)
        chosen = mixed_ref[pl.ds(first, BLOCK), :].astype(BF16)
        part = nt(chosen, full_ref[:, heads * 3 * HEAD :]).astype(BF16)
        for k in range(per_block):
            part_ref[i * per_block + k, :, :outputs] = part[k * shared : (k + 1) * shared]
    for i in range(ways):
        part_ref[i, :, outputs:] = feat_ref[...]


def assemble_kernel(ways, place_ref, own_ref, mine_ref, other_ref, proj_ref, whole_ref):
    features, columns = own_ref.shape
    half = features // 2
    first = pl.multiple_of(place_ref[0] * half, half)
    second = pl.multiple_of((1 - place_ref[0]) * half, half)
    proj_ref[place_ref[1]] = own_ref[...].T
    for k in range(1, ways):
        whole_ref[pl.ds(first, half), :] = mine_ref[k - 1]
        whole_ref[pl.ds(second, half), :] = other_ref[k - 1]
        proj_ref[place_ref[1 + k]] = whole_ref[...].T


def predict_kernel(feat_ref, proj_ref, pred_ref):
    ways, columns, features = proj_ref.shape
    for k in range(ways):
        pred_ref[:, k * columns : (k + 1) * columns] = nt(feat_ref[...], proj_ref[k])


def extra_kernel(shares, columns, place_ref, parts_ref, after_ref, extra_ref):
    features = extra_ref.shape[1] * columns
    rows = parts_ref.shape[0] * parts_ref.shape[1]
    feat = parts_ref[...].reshape(rows, parts_ref.shape[2])[:, -features:]
    shifted = [feat]
    for b in range(1, features // columns):
        shifted.append(jnp.concatenate([feat[:, b:], feat[:, :b]], 1))
    for half in range(2):
        core = place_ref[0] if half == 0 else 1 - place_ref[0]
        pick = pick_rows(features, shares, columns, core, True)
        for b in range(features // columns):
            extra_ref[half, b] = nt(pick, shifted[b]).astype(BF16)


def diff_kernel(
    clips, count_ref, place_ref, parts_ref, tokens_ref, pred_ref, proj_ref, out_ref
):
    rows, width = tokens_ref.shape
    ways, columns, features = proj_ref.shape
    branch = parts_ref[0, :, :width].astype(F32)
    for i in range(1, ways):
        branch = branch + parts_ref[i, :, :width].astype(F32)
    target = (tokens_ref[...].astype(F32) + branch).astype(BF16).astype(F32)
    count = count_ref[0]
    live = lax.broadcasted_iota(jnp.int32, (rows, 1), 0) + place_ref[1] * rows < count
    scale = jnp.full((1, 1), count, jnp.int32).astype(F32) * width
    factor = 2.0 / (scale * clips)
    diff = jnp.where(live, pred_ref[...] - target, 0.0)
    squares = jnp.sum(diff * diff, -1, keepdims=True) / scale
    dpred = (diff * factor).astype(BF16)
    dfeat = jnp.zeros((rows, features), F32)
    for k in range(ways):
        dfeat = dfeat + nn(dpred[:, k * columns : (k + 1) * columns], proj_ref[k])
    dfeat = dfeat.astype(BF16)
    high = squares.astype(BF16)
    rest = squares - high.astype(F32)
    middle = rest.astype(BF16)
    low = (rest - middle.astype(F32)).astype(BF16)
    lane = lax.broadcasted_iota(jnp.int32, (rows, BLOCK), 1)
    tail = jnp.where(lane == 0, high.astype(F32), jnp.where(lane == 1, middle.astype(F32), 0.0))
    tail = jnp.where(lane == 2, low.astype(F32), tail).astype(BF16)
    for i in range(ways):
        out_ref[i, :, :features] = dfeat
        out_ref[i, :, features : features + columns] = dpred[:, i * columns : (i + 1) * columns]
        out_ref[i, :, features + columns :] = tail


def backward_kernel(held, back_ref, feat_ref, weights_ref, *refs):
    sources, (keep_ref, send_ref, loss_ref) = refs[:held], refs[held : held + 3]
    copies = fetch(sources, refs[2 * held + 3 : -1], refs[-1])
    out_ref, packed_ref, mixed_ref, normed_ref, pick_ref = refs[2 * held + 3 : -1]
    features = out_ref.shape[1]
    heads = out_ref.shape[0] // HEAD
    dfeat = back_ref[:, :features]
    columns = back_ref.shape[1] - features - BLOCK
    dpred = back_ref[:, features : features + columns]
    tail = back_ref[:, features + columns :].astype(F32)
    loss_ref[...] = jnp.sum(jnp.sum(tail, 0, keepdims=True), 1, keepdims=True)
    copies[0].wait()
    dmixed = nt(dfeat, out_ref[...]).astype(BF16)
    copies[1].wait()
    packed = packed_ref[...]
    pieces = []
    for head in range(heads):
        query, keys, values = split_head(packed, head)
        rounded = weights_ref[head]
        weights = rounded.astype(F32)
        cot = dmixed[:, head * HEAD : (head + 1) * HEAD]
        dvalues = tn(rounded, cot)
        dweights = nt(cot, values)
        inner = jnp.sum(dweights * weights, -1, keepdims=True)
        dscores = (weights * (dweights - inner) * HEAD ** (-0.5)).astype(BF16)
        pieces += [piece.astype(BF16) for piece in (nn(dscores, keys), tn(dscores, query), dvalues)]
    dpacked = jnp.concatenate(pieces, axis=1)
    used = dpacked.shape[1]
    length = dpacked.shape[0]
    right = jnp.concatenate([dpacked, jnp.zeros((length, features - used), BF16)], 1)
    for copy in copies[2:]:
        copy.wait()
    tailed = features - columns
    mixed = jnp.concatenate([jnp.zeros((length, used - tailed), BF16), mixed_ref[...]], 1)
    for half, into in enumerate((keep_ref, send_ref)):
        dfeat_rows = nt(pick_ref[half], dfeat).astype(BF16)
        normed_rows = normed_ref[half]
        for b in range(features // columns):
            block = slice(b * columns, (b + 1) * columns)
            total = nn(normed_rows, right[:, block]) + nn(feat_ref[half, b], dpred)
            if b == features // columns - 1:
                total = total + nn(dfeat_rows, mixed)
            into[:, block] = total.astype(BF16)


SWAP = [(0, 1), (1, 0)]


def from_peers(rows, axis, places=None):
    ways = lax.axis_size(axis)
    return [
        lax.ppermute(rows(k), axis, [(i, (i + k) % ways) for i in range(ways)])
        for k in (range(1, ways) if places is None else places)
    ]


def add(a, b):
    return a.astype(F32) + b.astype(F32)


def result_kernel(parts_ref, q_ref, o_ref, p_ref):
    each, used = q_ref.shape
    columns = p_ref.shape[1]
    total = jnp.sum(parts_ref[...].astype(F32), 0)
    q_ref[...] = total[:each, :used]
    o_ref[...] = total[:each, used:]
    for i in range(total.shape[0] - each):
        for b in range(total.shape[1] // columns):
            row = i * (total.shape[1] // columns) + b
            p_ref[row : row + 1] = total[each + i : each + i + 1, b * columns : (b + 1) * columns]


def on_device(
    teacher_clips, teacher_gain, teacher_qkv, teacher_out_t, event_tokens, valid_counts, alignment,
    student_qkv, student_out, projector,
):
    clip, events, align = teacher_clips[0], event_tokens[0], alignment[0]
    length, width = clip.shape
    features = events.shape[1]
    columns = projector.shape[1]
    ways = lax.axis_size("x")
    rows = length // ways
    own_c, own_x = lax.axis_index("c"), lax.axis_index("x")
    shares = 1
    for axis in CLIP:
        shares = shares * lax.axis_size(axis)

    senders = lax.axis_size("y") * lax.axis_size("z")
    shard = jnp.concatenate([teacher_qkv, teacher_out_t], 1)
    shard = jnp.broadcast_to(shard[None], (senders, *shard.shape))
    own_core = lax.all_to_all(shard, ("y", "z"), 0, 0)
    heads = student_out.shape[0] // HEAD
    each = features // shares
    picked = shares // 2 * (each + each * columns // features)
    places = jnp.stack([own_c] + [(own_x + k) % ways for k in range(ways)]).astype(jnp.int32)
    message_rows = rows * features // columns + features // 2
    half = features // 2
    proj_half = lax.dynamic_slice_in_dim(projector, own_c * half, half, 0)
    far = from_peers(lambda k: proj_half, "x", range(2, ways - 1))
    outs = pl.pallas_call(
        student_kernel,
        out_shape=(
            pltpu.HBM((rows, features), BF16),
            *[
                shape((message_rows, columns) if k in (1, ways - 1) else (rows, features), BF16)
                for k in range(1, ways)
            ],
            pltpu.HBM((length, features), BF16),
            pltpu.HBM((length, 3 * HEAD * heads), BF16),
            pltpu.HBM((length, HEAD * heads), BF16),
            pltpu.HBM((heads, length, length), BF16),
            *in_place([student_out]),
        ),
        in_specs=[SMEM] * 2 + [VMEM] * 4,
        out_specs=(pl.BlockSpec(),) + (VMEM,) * (ways - 1) + (pl.BlockSpec(),) * 5,
        scratch_shapes=[pltpu.VMEM((length, features), F32)],
        compiler_params=PARAMS,
        cost_estimate=cost(4),
        name="student_forward",
    )(valid_counts, places, events, student_qkv.T, student_out, projector)
    own_part, peer_parts = outs[0], outs[1:ways]
    normed, packed, mixed, weights, kept_out = outs[ways:]
    normed_rows, pick = pl.pallas_call(
        lambda *refs: picks_kernel(shares, columns, *refs),
        out_shape=(
            pltpu.HBM((2, picked, length), BF16), pltpu.HBM((2, picked, features), BF16),
        ),
        in_specs=[SMEM, VMEM, ANY],
        out_specs=(pl.BlockSpec(),) * 2,
        compiler_params=PARAMS,
        cost_estimate=cost(2),
        name="student_picks",
    )(places, normed, far[0])

    received = from_peers(lambda k: peer_parts[k - 1], "x") + far
    own_events = lax.dynamic_slice_in_dim(events, own_x * rows, rows, 0)
    feat_rows, proj_halves = pl.pallas_call(
        lambda *refs: rows_kernel(ways, *refs),
        out_shape=(
            shape((rows, features), BF16), shape((ways - 1, features // 2, columns), BF16),
            *in_place(received),
        ),
        in_specs=[ANY] * 2 + [HBM] * ways,
        out_specs=(VMEM,) * 2 + (HBM,) * ways,
        input_output_aliases={2 + k: 2 + k for k in range(ways)},
        scratch_shapes=buffers((own_events, own_part, *received)),
        compiler_params=PARAMS,
        cost_estimate=cost(1),
        name="student_rows",
    )(own_events, own_part, *received)[:2]
    own_core, feat_rows, proj_halves, normed_rows = lax.optimization_barrier(
        (own_core, feat_rows, proj_halves, normed_rows)
    )
    other_core = lax.ppermute(own_core, "c", SWAP)
    proj_others = lax.ppermute(proj_halves, "c", SWAP)
    teacher_normed = pl.pallas_call(
        teacher_norm_kernel,
        out_shape=shape((length, width), BF16),
        in_specs=[VMEM] * 2 + [ANY],
        out_specs=VMEM,
        compiler_params=PARAMS,
        cost_estimate=cost(1),
        name="teacher_norm",
    )(clip, teacher_gain.reshape(1, width), feat_rows)

    teacher_part = pl.pallas_call(
        teacher_kernel,
        out_shape=shape((ways, rows, width + features), BF16),
        in_specs=[SMEM] * 2 + [VMEM] * 4,
        out_specs=VMEM,
        scratch_shapes=[
            pltpu.VMEM((senders * 2 * shard.shape[1], shard.shape[2]), BF16),
            pltpu.VMEM((length, teacher_out_t.shape[1]), F32),
        ],
        compiler_params=PARAMS,
        cost_estimate=cost(5),
        name="teacher",
    )(places, align, teacher_normed, own_core, other_core, feat_rows)

    teacher_parts = lax.all_to_all(teacher_part, "x", 0, 0)
    per_block = BLOCK // rows
    source = align[own_x // per_block] * BLOCK + own_x % per_block * rows
    own_tokens = lax.dynamic_slice_in_dim(clip, source, rows, 0)
    sources = jnp.stack([own_c] + [(own_x - k + ways) % ways for k in range(ways)]).astype(jnp.int32)
    whole_proj = pl.pallas_call(
        lambda *refs: assemble_kernel(ways, *refs),
        out_shape=pltpu.HBM((ways, columns, features), BF16),
        in_specs=[SMEM] + [VMEM] * 3,
        out_specs=pl.BlockSpec(),
        scratch_shapes=[pltpu.VMEM((features, columns), BF16)],
        compiler_params=PARAMS,
        cost_estimate=cost(1),
        name="projector",
    )(sources, projector, proj_halves, proj_others)
    pred = pl.pallas_call(
        predict_kernel,
        out_shape=shape((rows, width), F32),
        in_specs=[VMEM] * 2,
        out_specs=VMEM,
        compiler_params=PARAMS,
        cost_estimate=cost(2),
        name="student_predict",
    )(feat_rows, whole_proj)
    message = pl.pallas_call(
        lambda *refs: diff_kernel(shares, *refs),
        out_shape=shape((ways, rows, features + columns + BLOCK), BF16),
        in_specs=[SMEM] * 2 + [VMEM] * 4,
        out_specs=VMEM,
        compiler_params=PARAMS,
        cost_estimate=cost(2),
        name="difference",
    )(valid_counts, sources, teacher_parts, own_tokens, pred, whole_proj)
    feat_extra = pl.pallas_call(
        lambda *refs: extra_kernel(shares, columns, *refs),
        out_shape=shape((2, features // columns, picked, length), BF16),
        in_specs=[SMEM, VMEM, ANY],
        out_specs=VMEM,
        compiler_params=PARAMS,
        cost_estimate=cost(3),
        name="student_extra",
    )(sources, teacher_parts, message)
    back = lax.all_to_all(message, "x", 0, 0).reshape(length, features + columns + BLOCK)

    held = (kept_out, packed, mixed, normed_rows, pick)
    keep, send, loss = pl.pallas_call(
        lambda *refs: backward_kernel(len(held), *refs),
        out_shape=(
            shape((picked, features), BF16), shape((picked, features), BF16), shape((1, 1), F32),
            *in_place(held),
        ),
        in_specs=[VMEM] * 3 + [HBM] * len(held),
        out_specs=(VMEM,) * 3 + (HBM,) * len(held),
        scratch_shapes=buffers(held),
        input_output_aliases={3 + i: 3 + i for i in range(len(held))},
        compiler_params=PARAMS,
        cost_estimate=cost(4),
        name="student_backward",
    )(back, feat_extra, weights, *held)[:3]

    total = add(keep, lax.ppermute(send, "c", SWAP)).astype(BF16)
    chips = shares // 2
    spread = lax.all_to_all(
        total.reshape(chips, total.shape[0] // chips, features), CLIP[:3], 0, 0
    )
    used = 3 * HEAD * heads
    grad_q, grad_o, grad_p = pl.pallas_call(
        result_kernel,
        out_shape=(
            shape((each, used), F32), shape((each, HEAD * heads), F32), shape((each, columns), F32),
        ),
        in_specs=[VMEM],
        out_specs=(VMEM,) * 3,
        compiler_params=PARAMS,
        cost_estimate=cost(1),
        name="gradient_rows",
    )(spread)
    return loss.reshape(1), grad_q, grad_o.T, grad_p


def solution(mesh):
    group, dp, tensor = mesh.devices.shape
    fine = Mesh(mesh.devices.reshape(group, 4, dp // 8, 2, tensor), (*CLIP, "x"))
    dp = CLIP[1:]
    in_specs = (
        P(CLIP, None, None), P(), P(dp, "x"), P(dp, "x"), P(CLIP, None, None), P(CLIP), P(CLIP, None),
        P(None, "x"), P("x", None), P(None, "x"),
    )
    out_specs = (P(CLIP), P(CLIP, "x"), P("x", CLIP), P(CLIP, "x"))
    return jax.shard_map(
        on_device, mesh=fine, in_specs=in_specs, out_specs=out_specs, check_vma=False
    )
```
